512 devices in a mesh: pipe: 2 (over y_lo), ctx: 64 (over z, x, core), tp: 4 (over y_hi).
Axes of the slice: x: 4, y: 8 (y_hi: 4, y_lo: 2; y = y_hi * 2 + y_lo), z: 8, core: 2. Of those that a mesh axis runs over, the one named last changes fastest.
Arguments:
- queries: bfloat16 [2, 8192, 2048], P('pipe', 'ctx', 'tp'), may hold values from -96 to 96
- keys: bfloat16 [2, 8192, 128], P('pipe', 'ctx'), may hold values from -4 to 4
- values: bfloat16 [2, 8192, 128], P('pipe', 'ctx'), may hold values from -6 to 6
- grad_out: bfloat16 [2, 8192, 2048], P('pipe', 'ctx', 'tp'), may hold values from -6 to 6
- span_order: int32 [2, 64, 2], P('pipe'), may hold values from 0 to 127, as said below
Outputs:
- grad_queries: bfloat16 [2, 8192, 2048], P('pipe', 'ctx', 'tp')
- grad_keys: bfloat16 [2, 8192, 128], P('pipe', 'ctx')
- grad_values: bfloat16 [2, 8192, 128], P('pipe', 'ctx')
The draws below stay inside these ranges and needn't reach their ends.
Inputs may be any that keep to these rules, and one draw needn't show every extreme that they name: For each micro-batch m and index r, span_order[m, r, 0] is below 64 and span_order[m, r, 1] = 127 - span_order[m, r, 0]; every block number 0 to 127 appears exactly once in a micro-batch.
All inputs are finite; a program needn't handle non-finite values.
Results may differ from the reference program's by a relative error of at most 0.024.
Values may be sent and summed in bfloat16 or wider, within the bound.
A program may use at most 64 MiB of HBM per device.

```python
import jax
import jax.numpy as jnp
from jax import lax

HD = 128
QH = 16
TOK_DEV = 128
MB = 2
SEQ = 8192
N_CTX = 64


def shared_keys(key):
    return jnp.clip(jax.random.normal(key, (MB, SEQ, HD), jnp.float32), -4.0, 4.0)


def draw_keys(key, part):
    base = shared_keys(key)
    result = base
    return result.astype(jnp.bfloat16)


def draw_queries(key, part):
    key = jax.random.fold_in(key, 5)
    drawn = jnp.clip(jax.random.normal(key, (MB, SEQ, QH, HD), jnp.float32), -4.0, 4.0)
    result = drawn
    return result.reshape(MB, SEQ, QH * HD).astype(jnp.bfloat16)


def draw_span_order(key, part):
    key = jax.random.fold_in(key, 11)
    subkeys = jax.random.split(key, MB)
    firsts = jax.vmap(lambda sub: jax.random.permutation(sub, N_CTX))(subkeys).astype(jnp.int32)
    return jnp.stack([firsts, 2 * N_CTX - 1 - firsts], axis=-1).astype(jnp.int32)


def steps_of(own_key, dims, shards, low, top_value):
    level, own = 1.0, jax.random.fold_in(own_key, 6)
    for position, parts in shards:
        draws = jnp.exp(jax.random.uniform(jax.random.fold_in(own, position), (parts,), jnp.float32, low / len(shards), top_value / len(shards)))
        level = level * jnp.repeat(draws, dims[position] // parts).reshape([-1 if axis == position else 1 for axis in range(len(dims))])
    return level


def centred(own_key, dims, scale, limit, shards=(), kind=jnp.bfloat16):
    level = steps_of(own_key, dims, shards, -0.22, 0.18) if shards else 1.0
    values = jax.random.normal(own_key, dims, jnp.float32) * scale * level
    return jnp.minimum(jnp.maximum(values, -limit), limit).astype(kind)


def setup_inputs(seed: int = 0) -> dict:
    streams_of = jax.random.split(jax.random.key(seed), 6)
    return {
        "queries": draw_queries(jax.random.fold_in(streams_of[5], 71), 0),
        "keys": draw_keys(jax.random.fold_in(streams_of[5], 71), 0),
        "values": centred(streams_of[2], (MB, SEQ, HD), 1.0, 6.0, ((0, 2), (1, 64))),
        "grad_out": centred(streams_of[3], (MB, SEQ, QH * HD), 1.0, 6.0, ((0, 2), (1, 64), (2, 4))),
        "span_order": draw_span_order(jax.random.fold_in(streams_of[5], 71), 0),
    }


def head_grads(query_head, grad_head, key_rows, value_rows, positions, inv_root):
    scores = jnp.dot(query_head, key_rows.T, preferred_element_type=jnp.float32) * inv_root
    visible = positions[None, :] <= positions[:, None]
    scores = jnp.where(visible, scores, -jnp.inf)
    row_max = jnp.max(scores, axis=1)
    lse = row_max + jnp.log(jnp.sum(jnp.exp(scores - row_max[:, None]), axis=1))
    probs = jnp.exp(scores - lse[:, None])
    probs_low = probs.astype(jnp.bfloat16)
    attn_out = jnp.dot(probs_low, value_rows, preferred_element_type=jnp.float32).astype(jnp.bfloat16)
    delta = jnp.sum(grad_head.astype(jnp.float32) * attn_out.astype(jnp.float32), axis=1)
    grad_probs = jnp.dot(grad_head, value_rows.T, preferred_element_type=jnp.float32)
    grad_scores = (probs * (grad_probs - delta[:, None])).astype(jnp.bfloat16)
    grad_query = (jnp.dot(grad_scores, key_rows, preferred_element_type=jnp.float32) * inv_root).astype(jnp.bfloat16)
    grad_key = jnp.dot(grad_scores.T, query_head, preferred_element_type=jnp.float32) * inv_root
    grad_value = jnp.dot(probs_low.T, grad_head, preferred_element_type=jnp.float32)
    return grad_query, grad_key, grad_value


def micro_batch(query_all, grad_all, key_rows, value_rows, order_rows):
    half_len = TOK_DEV // 2
    positions = (order_rows[:, :, None] * half_len + jnp.arange(half_len, dtype=jnp.int32)[None, None, :]).reshape(SEQ).astype(jnp.int32)
    inv_root = HD ** -0.5
    query_heads = query_all.reshape(SEQ, QH, HD).transpose(1, 0, 2)
    grad_heads = grad_all.reshape(SEQ, QH, HD).transpose(1, 0, 2)

    def per_head(pair):
        return head_grads(pair[0], pair[1], key_rows, value_rows, positions, inv_root)

    grad_query, grad_key, grad_value = lax.map(per_head, (query_heads, grad_heads))
    grad_query = grad_query.transpose(1, 0, 2).reshape(SEQ, QH * HD)
    return grad_query, jnp.sum(grad_key, axis=0).astype(jnp.bfloat16), jnp.sum(grad_value, axis=0).astype(jnp.bfloat16)


def reference(queries, keys, values, grad_out, span_order):
    results = [micro_batch(queries[m], grad_out[m], keys[m], values[m], span_order[m]) for m in range(MB)]
    received = [results[(m + 1) % MB] for m in range(MB)]
    grad_queries = jnp.stack([item[0] for item in received])
    grad_keys = jnp.stack([item[1] for item in received])
    grad_values = jnp.stack([item[2] for item in received])
    return grad_queries, grad_keys, grad_values
```

```python
import functools

import jax
import jax.numpy as jnp
from jax import lax
from jax.experimental import pallas as pl
from jax.experimental.pallas import tpu as pltpu
from jax.sharding import PartitionSpec as P

MESH = pl.DeviceIdType.MESH
F32 = jnp.float32
BF16 = jnp.bfloat16

NZ = 8
NX = 4
NT = 4
HEADS = 4
HALF = 64
HD = 128
ROW = 2 * NX
ROWS = HEADS * HALF
KEYS = ROW * HALF
INV_ROOT = HD ** (-0.5)
LOG2E = 1.4426950408889634
NEG = -1e30
POS = 1e30


def dot_nt(a, b):
    return lax.dot_general(a, b, (((1,), (1,)), ((), ())), preferred_element_type=F32)


def dot_nn(a, b):
    return jnp.dot(a, b, preferred_element_type=F32)


def dot_tn(a, b):
    return lax.dot_general(a, b, (((0,), (0,)), ((), ())), preferred_element_type=F32)


def col_sum(v):
    return jnp.sum(v, axis=0, keepdims=True)


def col_max(v):
    return jnp.max(v, axis=0, keepdims=True)


def kernel(
    q_ref, k_ref, v_ref, g_ref, span_ref,
    dq_out, dk_out, dv_out,
    kbuf, vbuf, s1, s2, dp1, dp2, kselbuf, qq, oo, dql, dq2, dqst,
    pk, pv, sib, rr, cr, xr, zr, ysum, yr,
    p1send, p1k, p1v, fsend, frecv, csend, crecv, d2d_send, d2d_recv,
    sib_send, sib_recv, rsend, rrecv, bsend, brecv, xsend, xrecv, zsend, zrecv,
    ysend, yrecv, dqsem,
):
    pipe = lax.axis_index("pipe")
    me = lax.axis_index("ctx")
    t = lax.axis_index("tp")
    z = me // (2 * NX)
    x = (me // 2) % NX
    c = me % 2
    y = t * 2 + pipe

    def at(zz, xx, cc):
        return (pipe, (zz * NX + xx) * 2 + cc, t)

    def zoff(d):
        return lax.rem(z + d + NZ, NZ)

    def xoff(d):
        return lax.rem(x + d + NX, NX)

    def other(tt, cc):
        return (1 - pipe, (z * NX + x) * 2 + cc, tt)

    sibling = at(z, x, 1 - c)

    def remote(src, dst, ssem, rsem, dev):
        return pltpu.make_async_remote_copy(
            src_ref=src, dst_ref=dst, send_sem=ssem, recv_sem=rsem,
            device_id=dev, device_id_type=MESH,
        )

    barrier = pltpu.get_barrier_semaphore()
    count = 0

    def greet(dev):
        pl.semaphore_signal(barrier, inc=1, device_id=dev, device_id_type=MESH)

    greet(sibling)
    count += 1
    for cc in range(2):
        for d in range(1, NX):
            greet(at(z, xoff(d), cc))
            count += 1
        for d in range(1, NZ):
            greet(at(zoff(d), x, cc))
            count += 1
        for tt in range(NT):
            greet(other(tt, cc))
            count += 1
    pl.semaphore_wait(barrier, count)

    def first_k(d):
        return remote(k_ref.at[0], kbuf.at[me], p1send.at[d], p1k.at[2 * d + c], at(z, xoff(d), 0))

    def first_v(d):
        return remote(v_ref.at[0], vbuf.at[z, x, c], p1send.at[NX + d], p1v.at[2 * d + c],
                      at(zoff(d), x, 1))

    for d in range(1, NX):
        first_k(d).start()

    @pl.when(c == 1)
    def _():
        first_k(0).start()
        vbuf[z, x, 1] = v_ref[0]

    @pl.when(c == 0)
    def _():
        first_v(0).start()
        kbuf[me] = k_ref[0]

    for d in (1, 7, 2, 6, 3, 5, 4):
        first_v(d).start()

    def k_part(row, h):
        return pl.ds(row * ROW + h * (ROW // 2), ROW // 2)

    def fwd_k(way, k, h):
        step = 1 if way == 0 else -1
        part = k_part(zoff(-step * (k - 1)), h)
        i = (way * 4 + k - 1) * 2 + h
        return remote(kbuf.at[part], kbuf.at[part], fsend.at[i], frecv.at[i], at(zoff(step), x, 0))

    def got_k(way, k, h):
        step = 1 if way == 0 else -1
        return k_part(zoff(-step * k), h)

    def d2d_k(part, i):
        return remote(kbuf.at[part], kbuf.at[part], d2d_send.at[i], d2d_recv.at[i], sibling)

    def fwd_v(way, k, h):
        step = 1 if way == 0 else -1
        ref = vbuf.at[pl.ds(2 * h, 2), xoff(-step * (k - 1))]
        i = (way * 2 + k - 1) * 4 + h
        return remote(ref, ref, csend.at[i], crecv.at[i], at(z, xoff(step), 1))

    def d2d_v(col, h, i):
        ref = vbuf.at[pl.ds(2 * h, 2), col]
        return remote(ref, ref, d2d_send.at[i], d2d_recv.at[i], sibling)

    k_steps = [(w, k, h) for k in range(1, 5) for h in range(2) for w in range(2)
               if k < 4 or h == w]
    v_first = [(w, 1, (h + 2 * w) % 4) for h in range(4) for w in range(2)]
    v_steps = v_first + [(w, 2, h + 2 * w) for h in range(2) for w in range(2)]

    @pl.when(c == 0)
    def _():
        sent = []
        for d in range(NX):
            for cc in range(2):
                if (d, cc) != (0, 0):
                    pltpu.make_async_copy(kbuf.at[0], kbuf.at[0], p1k.at[2 * d + cc]).wait()
        for h in range(2):
            for w in range(2):
                cp = fwd_k(w, 1, h)
                cp.start()
                sent.append(cp)
        for h in range(2):
            cp = d2d_k(k_part(z, h), h)
            cp.start()
            sent.append(cp)
        for n, (w, k, h) in enumerate(k_steps):
            fwd_k(w, k, h).wait_recv()
            if k < 3 or (k == 3 and h == w):
                cp = fwd_k(w, k + 1, h)
                cp.start()
                sent.append(cp)
            cp = d2d_k(got_k(w, k, h), n + 2)
            cp.start()
            sent.append(cp)
        for cp in sent:
            cp.wait_send()
        for i in range(16):
            d2d_v(0, 0, i).wait_recv()
        first_v(0).wait_send()

    @pl.when(c == 1)
    def _():
        sent = []
        for d in range(NZ):
            for cc in range(2):
                if (d, cc) != (0, 1):
                    pltpu.make_async_copy(kbuf.at[0], kbuf.at[0], p1v.at[2 * d + cc]).wait()
        for (w, k, h) in v_first:
            cp = fwd_v(w, 1, h)
            cp.start()
            sent.append(cp)
        for h in range(4):
            cp = d2d_v(x, h, h)
            cp.start()
            sent.append(cp)
        for n, (w, k, h) in enumerate(v_steps):
            fwd_v(w, k, h).wait_recv()
            if k == 1 and h // 2 == w:
                cp = fwd_v(w, 2, h)
                cp.start()
                sent.append(cp)
            step = 1 if w == 0 else -1
            cp = d2d_v(xoff(-step * k), h, n + 4)
            cp.start()
            sent.append(cp)
        for cp in sent:
            cp.wait_send()
        for i in range(16):
            d2d_k(k_part(0, 0), i).wait_recv()
        first_k(0).wait_send()

    for d in range(1, NX):
        first_k(d).wait_send()
    for d in range(1, NZ):
        first_v(d).wait_send()

    for h in range(HEADS):
        cols = slice(h * HD, (h + 1) * HD)
        rows = slice(h * HALF, (h + 1) * HALF)
        qq[rows, 0:HD] = q_ref[0, 0:HALF, cols]
        qq[rows, HD:2 * HD] = q_ref[0, HALF:2 * HALF, cols]
        oo[rows, 0:HD] = g_ref[0, 0:HALF, cols]
        oo[rows, HD:2 * HD] = g_ref[0, HALF:2 * HALF, cols]

    my_block = span_ref[0, me, 0]

    def early(b, i):
        return span_ref[0, b * ROW + i, 0] < my_block

    def pick(buf, b):
        e, both = [], []
        for i in range(ROW):
            if buf is kbuf:
                blk = buf[b * ROW + i]
            else:
                blk = buf[b, i // 2, i % 2]
            lo, hi = blk[:HALF], blk[HALF:]
            s = early(b, i)
            zero = jnp.zeros_like(lo)
            e.append(lo)
            both.append(jnp.concatenate([jnp.where(s, lo, zero), jnp.where(s, zero, hi)], axis=1))
        return jnp.concatenate(e, axis=0), jnp.concatenate(both, axis=0)

    scale = INV_ROOT * LOG2E

    def sweep_scores(b, carry):
        m_e, m_l = carry
        ke, ksel = pick(kbuf, b)
        kselbuf[b] = ksel
        s1[b] = dot_nt(ke, qq[:, HD:]) * scale
        s2[b] = dot_nt(ksel, qq[...]) * scale
        m_l = jnp.maximum(m_l, col_max(s1[b]))
        for i in range(ROW):
            top = col_max(s2[b, i * HALF:(i + 1) * HALF])
            s = early(b, i)
            mine = b * ROW + i == me
            low = jnp.full_like(top, NEG)
            top = jnp.where(mine, low, top)
            m_e = jnp.maximum(m_e, jnp.where(s, top, low))
            m_l = jnp.maximum(m_l, jnp.where(s, low, top))
        return m_e, m_l

    start = jnp.full((1, ROWS), NEG, F32)
    m_e, m_l = lax.fori_loop(0, NZ, sweep_scores, (start, start))

    key_no = lax.broadcasted_iota(jnp.int32, (HALF, ROWS), 0)
    tok_no = lax.broadcasted_iota(jnp.int32, (HALF, ROWS), 1) % HALF
    seen = key_no <= tok_no
    k_e, k_l = k_ref[0, :HALF], k_ref[0, HALF:]
    v_e, v_l = v_ref[0, :HALF], v_ref[0, HALF:]
    q_e, q_l = qq[:, :HD], qq[:, HD:]
    o_e, o_l = oo[:, :HD], oo[:, HD:]
    see = jnp.where(seen, dot_nt(k_e, q_e) * scale, NEG)
    sll = jnp.where(seen, dot_nt(k_l, q_l) * scale, NEG)
    m_e = jnp.maximum(m_e, col_max(see))
    m_l = jnp.maximum(m_l, col_max(sll))
    pee = jnp.exp2(see - m_e)
    pll = jnp.exp2(sll - m_l)
    dpee = dot_nt(v_e, o_e)
    dpll = dot_nt(v_l, o_l)

    def sweep_sums(b, carry):
        l_e, l_l, d_e, d_l = carry
        ve, vsel = pick(vbuf, b)
        dp1[b] = dot_nt(ve, oo[:, HD:])
        dp2[b] = dot_nt(vsel, oo[...])
        for i in range(ROW):
            part = slice(i * HALF, (i + 1) * HALF)
            p = jnp.exp2(s1[b, part] - m_l)
            s1[b, part] = p
            l_l = l_l + col_sum(p)
            d_l = d_l + col_sum(p * dp1[b, part])
            s = early(b, i)
            top = jnp.where(s, m_e, m_l)
            top = jnp.where(b * ROW + i == me, jnp.full_like(top, POS), top)
            p = jnp.exp2(s2[b, part] - top)
            s2[b, part] = p
            ps = col_sum(p)
            pd = col_sum(p * dp2[b, part])
            zero = jnp.zeros_like(ps)
            l_e = l_e + jnp.where(s, ps, zero)
            l_l = l_l + jnp.where(s, zero, ps)
            d_e = d_e + jnp.where(s, pd, zero)
            d_l = d_l + jnp.where(s, zero, pd)
        return l_e, l_l, d_e, d_l

    l_e, l_l, d_e, d_l = lax.fori_loop(
        0, NZ, sweep_sums,
        (col_sum(pee), col_sum(pll), col_sum(pee * dpee), col_sum(pll * dpll)),
    )
    r_e = 1.0 / l_e
    r_l = 1.0 / l_l
    d_e = d_e * r_e
    d_l = d_l * r_l

    pee = pee * r_e
    pll = pll * r_l
    dsee = (pee * (dpee - d_e)).astype(BF16)
    dsll = (pll * (dpll - d_l)).astype(BF16)
    own_k_e = dot_nn(dsee, q_e) * INV_ROOT
    own_k_l = dot_nn(dsll, q_l) * INV_ROOT
    own_v_e = dot_nn(pee.astype(BF16), o_e)
    own_v_l = dot_nn(pll.astype(BF16), o_l)
    dq2[0:HD] = dot_tn(k_e, dsee)
    dq2[HD:2 * HD] = dot_tn(k_l, dsll)
    dql[...] = jnp.zeros_like(dql)

    def sib_send_k(b):
        part = pl.ds(b * ROW, ROW)
        return remote(pk.at[part], sib.at[part], sib_send.at[b], sib_recv.at[b], sibling)

    def sib_send_v(b):
        part = pl.ds(b * ROW, ROW)
        return remote(pv.at[part], sib.at[part], sib_send.at[b], sib_recv.at[b], sibling)

    def sweep_grads(b, _):
        ke_list = [kbuf[b * ROW + i, :HALF] for i in range(ROW)]
        ke = jnp.concatenate(ke_list, axis=0)
        ksel = kselbuf[b]
        p1 = s1[b] * r_l
        ds1 = (p1 * (dp1[b] - d_l)).astype(BF16)
        p1 = p1.astype(BF16)
        p2s, ds2s = [], []
        for i in range(ROW):
            part = slice(i * HALF, (i + 1) * HALF)
            s = early(b, i)
            p = s2[b, part] * jnp.where(s, r_e, r_l)
            ds2s.append((p * (dp2[b, part] - jnp.where(s, d_e, d_l))).astype(BF16))
            p2s.append(p.astype(BF16))
        p2 = jnp.concatenate(p2s, axis=0)
        ds2 = jnp.concatenate(ds2s, axis=0)
        v1 = dot_nn(p1, oo[:, HD:])
        v2 = dot_nn(p2, oo[...])
        k1 = dot_nn(ds1, qq[:, HD:]) * INV_ROOT
        k2 = dot_nn(ds2, qq[...]) * INV_ROOT
        dql[...] += dot_tn(ke, ds1)
        dq2[...] += dot_tn(ksel, ds2)
        for i in range(ROW):
            part = slice(i * HALF, (i + 1) * HALF)
            s = early(b, i)
            zero = jnp.zeros((HALF, HD), F32)
            pv[b * ROW + i, :HALF] = (v1[part] + jnp.where(s, v2[part, :HD], zero)).astype(BF16)
            pv[b * ROW + i, HALF:] = jnp.where(s, zero, v2[part, HD:]).astype(BF16)
            pk[b * ROW + i, :HALF] = (k1[part] + jnp.where(s, k2[part, :HD], zero)).astype(BF16)
            pk[b * ROW + i, HALF:] = jnp.where(s, zero, k2[part, HD:]).astype(BF16)

        @pl.when(b == z)
        def _():
            pv[me, :HALF] = (pv[me, :HALF].astype(F32) + own_v_e).astype(BF16)
            pv[me, HALF:] = (pv[me, HALF:].astype(F32) + own_v_l).astype(BF16)
            pk[me, :HALF] = (pk[me, :HALF].astype(F32) + own_k_e).astype(BF16)
            pk[me, HALF:] = (pk[me, HALF:].astype(F32) + own_k_l).astype(BF16)

        @pl.when(c == 0)
        def _():
            sib_send_v(b).start()

        @pl.when(c == 1)
        def _():
            sib_send_k(b).start()

        return 0

    lax.fori_loop(0, NZ, sweep_grads, 0)

    for j, acc in enumerate((dq2[0:HD], dq2[HD:2 * HD] + dql[...])):
        g = (acc * INV_ROOT).T.astype(BF16)
        for h in range(HEADS):
            dqst[j * HALF:(j + 1) * HALF, h * HD:(h + 1) * HD] = g[h * HALF:(h + 1) * HALF]
    dq_copy = remote(dqst, dq_out.at[0], dqsem.at[0], dqsem.at[1], other(t, c))
    dq_copy.start()

    def add_into(dst, idx, *terms):
        total = dst[idx].astype(F32)
        for ref, i in terms:
            total = total + ref[i].astype(F32)
        dst[idx] = total.astype(BF16)

    @pl.when(c == 0)
    def _():
        for b in range(NZ):
            sib_send_k(b).wait_recv()
        sent = []

        def slot(way, k, h):
            return (way, k - 1, pl.ds(h * (ROW // 2), ROW // 2))

        def send(way, k, h):
            step = 1 if way == 0 else -1
            i = (way * 4 + k - 1) * 2 + h
            return remote(pk.at[k_part(zoff(step * k), h)], rr.at[slot(way, k, h)],
                          rsend.at[i], rrecv.at[i], at(zoff(step), x, 0))

        def hop(way, k, h, has):
            step = 1 if way == 0 else -1
            part = k_part(zoff(step * k), h)
            terms = [(sib, part)]
            if has:
                send(way, k + 1, h).wait_recv()
                terms.append((rr, slot(way, k + 1, h)))
            add_into(pk, part, *terms)
            cp = send(way, k, h)
            cp.start()
            sent.append(cp)

        hop(0, 4, 0, False)
        hop(1, 4, 1, False)
        hop(0, 3, 1, False)
        hop(1, 3, 0, False)
        hop(0, 3, 0, True)
        hop(1, 3, 1, True)
        for k in (2, 1):
            for h in (1, 0):
                hop(0, k, h, True)
                hop(1, k, 1 - h, True)
        for h in (1, 0):
            for w, hh in ((0, h), (1, 1 - h)):
                send(w, 1, hh).wait_recv()
        for h in range(2):
            add_into(pk, k_part(z, h), (sib, k_part(z, h)), (rr, slot(0, 1, h)), (rr, slot(1, 1, h)))

        def across(d):
            return remote(pk.at[pl.ds(z * ROW + 2 * xoff(d), 2)], xr.at[d], xsend.at[d],
                          xrecv.at[d], at(z, xoff(d), 0))

        for d in range(1, NX):
            across(d).start()
        for d in range(1, NX):
            across(d).wait_recv()
        mine = pl.ds(z * ROW + 2 * x, 2)
        total = pk[mine].astype(F32)
        for d in range(1, NX):
            total = total + xr[d].astype(F32)
        ysum[...] = total.astype(BF16)
        for d in range(1, NX):
            across(d).wait_send()
        for cp in sent:
            cp.wait_send()
        for b in range(NZ):
            sib_send_v(b).wait_send()

    @pl.when(c == 1)
    def _():
        for b in range(NZ):
            sib_send_v(b).wait_recv()
        sent = []

        def cell(zz, xx):
            return pl.ds((zz * NX + xx) * 2, 2)

        def send(way, k, h, j):
            step = 1 if way == 0 else -1
            zz = 2 * h + j
            i = (way * 2 + k - 1) * NZ + zz
            return remote(pv.at[cell(zz, xoff(step * k))], cr.at[way, k - 1, zz],
                          bsend.at[i], brecv.at[i], at(z, xoff(step), 1))

        def hop(way, k, h, has):
            step = 1 if way == 0 else -1
            for j in range(2):
                zz = 2 * h + j
                part = cell(zz, xoff(step * k))
                terms = [(sib, part)]
                if has:
                    send(way, k + 1, h, j).wait_recv()
                    terms.append((cr, (way, k, zz)))
                add_into(pv, part, *terms)
                cp = send(way, k, h, j)
                cp.start()
                sent.append(cp)

        for h in range(2):
            hop(0, 2, h, False)
            hop(1, 2, h + 2, False)
        for h in range(2):
            hop(0, 1, h + 2, False)
            hop(1, 1, h, False)
        for h in range(2):
            hop(0, 1, h, True)
            hop(1, 1, h + 2, True)

        def across(d):
            return remote(pv.at[cell(zoff(d), x)], zr.at[d], zsend.at[d], zrecv.at[d],
                          at(zoff(d), x, 1))

        for zz in range(NZ):
            for w in range(2):
                send(w, 1, zz // 2, zz % 2).wait_recv()
            add_into(pv, cell(zz, x), (sib, cell(zz, x)), (cr, (0, 0, zz)), (cr, (1, 0, zz)))
        for d in (4, 3, 5, 2, 6, 1, 7):
            across(d).start()
        for d in range(1, NZ):
            across(d).wait_recv()
        total = pv[cell(z, x)].astype(F32)
        for d in range(1, NZ):
            total = total + zr[d].astype(F32)
        ysum[...] = total.astype(BF16)
        for d in range(1, NZ):
            across(d).wait_send()
        for cp in sent:
            cp.wait_send()
        for b in range(NZ):
            sib_send_k(b).wait_send()

    def last(tt, cc):
        i = tt * 2 + cc
        return remote(ysum.at[cc], yr.at[c, t], ysend.at[i], yrecv.at[c, t], other(tt, cc))

    for tt in range(NT):
        for cc in range(2):
            last(tt, cc).start()
    for kind in range(2):
        for tt in range(NT):
            pltpu.make_async_copy(ysum.at[0], ysum.at[0], yrecv.at[kind, tt]).wait()
    for kind, out in ((0, dk_out), (1, dv_out)):
        total = yr[kind, 0].astype(F32)
        for tt in range(1, NT):
            total = total + yr[kind, tt].astype(F32)
        out[0] = total.astype(BF16)
    for tt in range(NT):
        for cc in range(2):
            last(tt, cc).wait_send()
    dq_copy.wait()


def per_device(queries, keys, values, grad_out, span_order):
    vmem = pl.BlockSpec(memory_space=pltpu.VMEM)
    dma = pltpu.SemaphoreType.DMA
    scratch = [
        pltpu.VMEM((NZ * ROW, 128, HD), BF16),
        pltpu.VMEM((NZ, NX, 2, 128, HD), BF16),
        pltpu.VMEM((NZ, KEYS, ROWS), F32),
        pltpu.VMEM((NZ, KEYS, ROWS), F32),
        pltpu.VMEM((NZ, KEYS, ROWS), F32),
        pltpu.VMEM((NZ, KEYS, ROWS), F32),
        pltpu.VMEM((NZ, KEYS, 2 * HD), BF16),
        pltpu.VMEM((ROWS, 2 * HD), BF16),
        pltpu.VMEM((ROWS, 2 * HD), BF16),
        pltpu.VMEM((HD, ROWS), F32),
        pltpu.VMEM((2 * HD, ROWS), F32),
        pltpu.VMEM((128, HEADS * HD), BF16),
        pltpu.VMEM((NZ * ROW, 128, HD), BF16),
        pltpu.VMEM((NZ * ROW, 128, HD), BF16),
        pltpu.VMEM((NZ * ROW, 128, HD), BF16),
        pltpu.VMEM((2, 4, ROW, 128, HD), BF16),
        pltpu.VMEM((2, 2, NZ, 2, 128, HD), BF16),
        pltpu.VMEM((NX, 2, 128, HD), BF16),
        pltpu.VMEM((NZ, 2, 128, HD), BF16),
        pltpu.VMEM((2, 128, HD), BF16),
        pltpu.VMEM((2, NT, 128, HD), BF16),
        dma((NX + NZ,)), dma((2 * NX,)), dma((2 * NZ,)),
        dma((16,)), dma((16,)), dma((16,)), dma((16,)),
        dma((16,)), dma((16,)),
        dma((NZ,)), dma((NZ,)),
        dma((16,)), dma((16,)), dma((32,)), dma((32,)),
        dma((NX,)), dma((NX,)), dma((NZ,)), dma((NZ,)),
        dma((8,)), dma((2, NT)), dma((2,)),
    ]
    return pl.pallas_call(
        kernel,
        out_shape=(
            jax.ShapeDtypeStruct(queries.shape, BF16),
            jax.ShapeDtypeStruct(keys.shape, BF16),
            jax.ShapeDtypeStruct(values.shape, BF16),
        ),
        in_specs=[vmem, vmem, vmem, vmem, pl.BlockSpec(memory_space=pltpu.SMEM)],
        out_specs=(pl.BlockSpec(memory_space=pl.ANY), vmem, vmem),
        scratch_shapes=scratch,
        compiler_params=pltpu.CompilerParams(
            collective_id=1, has_side_effects=True, vmem_limit_bytes=56 * 2**20
        ),
        name="attention_backward",
    )(queries, keys, values, grad_out, span_order)


def solution(mesh):
    return jax.shard_map(
        per_device,
        mesh=mesh,
        in_specs=(
            P("pipe", "ctx", "tp"),
            P("pipe", "ctx", None),
            P("pipe", "ctx", None),
            P("pipe", "ctx", "tp"),
            P("pipe", None, None),
        ),
        out_specs=(P("pipe", "ctx", "tp"), P("pipe", "ctx", None), P("pipe", "ctx", None)),
        check_vma=False,
    )
```

```python
import functools

import jax
import jax.numpy as jnp
from jax import lax
from jax.experimental import pallas as pl
from jax.experimental.pallas import tpu as pltpu
from jax.sharding import PartitionSpec as P

MESH = pl.DeviceIdType.MESH
F32 = jnp.float32
BF16 = jnp.bfloat16

NZ = 8
NX = 4
NT = 4
HEADS = 4
HALF = 64
HD = 128
ROW = 2 * NX
ROWS = HEADS * HALF
KEYS = ROW * HALF
INV_ROOT = HD ** (-0.5)
LOG2E = 1.4426950408889634
NEG = -1e30
POS = 1e30
ORDER = (0, 1, -1, 2, -2, 3, -3, 4)
ACROSS = (0, 1, 3, 2)
SETS = ((0, 1), (3, 2))


def dot_nt(a, b):
    return lax.dot_general(a, b, (((1,), (1,)), ((), ())), preferred_element_type=F32)


def dot_nn(a, b):
    return jnp.dot(a, b, preferred_element_type=F32)


def dot_tn(a, b):
    return lax.dot_general(a, b, (((0,), (0,)), ((), ())), preferred_element_type=F32)


def col_sum(v):
    return jnp.sum(v, axis=0, keepdims=True)


def col_max(v):
    return jnp.max(v, axis=0, keepdims=True)


def kernel(
    q_ref, k_ref, v_ref, g_ref, span_ref,
    dq_out, dk_out, dv_out,
    kbuf, vbuf, s1, s2, dp1, dp2, kselbuf, qq, oo, dql, dq2, dqst, state, tops, diag,
    pk, pv, sib, rr, cr1, cr2, zr, xr, ysum, yr,
    p1ks, p1kr, p1vs, p1vr, zks, zkr, zvs, zvr, x1s, x1r, x2s, x2r, d2ds, d2dr,
    sibs, sibr, rs, rrsem, c1s, c1r, c2s, c2r, zs, zrsem, xs, xrsem, ys, yrsem, dqsem,
):
    pipe = lax.axis_index("pipe")
    me = lax.axis_index("ctx")
    t = lax.axis_index("tp")
    z = me // (2 * NX)
    x = (me // 2) % NX
    c = me % 2

    def at(zz, xx, cc):
        return (pipe, (zz * NX + xx) * 2 + cc, t)

    def zoff(d):
        return lax.rem(z + d + NZ, NZ)

    def xoff(d):
        return lax.rem(x + d + NX, NX)

    def row_of(n):
        return zoff(((n + 1) // 2) * (2 * (n % 2) - 1))

    def other(tt, cc):
        return (1 - pipe, (z * NX + x) * 2 + cc, tt)

    sibling = at(z, x, 1 - c)

    def remote(src, dst, ssem, rsem, dev):
        return pltpu.make_async_remote_copy(
            src_ref=src, dst_ref=dst, send_sem=ssem, recv_sem=rsem,
            device_id=dev, device_id_type=MESH,
        )

    barrier = pltpu.get_barrier_semaphore()
    count = 0

    def greet(dev):
        pl.semaphore_signal(barrier, inc=1, device_id=dev, device_id_type=MESH)

    greet(sibling)
    count += 1
    for cc in range(2):
        for d in range(1, NX):
            greet(at(z, xoff(d), cc))
            count += 1
        for d in (1, -1, 2, -2):
            greet(at(zoff(d), x, cc))
            count += 1
        for tt in range(NT):
            greet(other(tt, cc))
            count += 1

    for h in range(HEADS):
        cols = slice(h * HD, (h + 1) * HD)
        rows = slice(h * HALF, (h + 1) * HALF)
        qq[rows, 0:HD] = q_ref[0, 0:HALF, cols]
        qq[rows, HD:2 * HD] = q_ref[0, HALF:2 * HALF, cols]
        oo[rows, 0:HD] = g_ref[0, 0:HALF, cols]
        oo[rows, HD:2 * HD] = g_ref[0, HALF:2 * HALF, cols]

    scale = INV_ROOT * LOG2E
    key_no = lax.broadcasted_iota(jnp.int32, (HALF, ROWS), 0)
    tok_no = lax.broadcasted_iota(jnp.int32, (HALF, ROWS), 1) % HALF
    seen = key_no <= tok_no
    for j in range(2):
        half = slice(j * HALF, (j + 1) * HALF)
        cols = slice(j * HD, (j + 1) * HD)
        s = jnp.where(seen, dot_nt(k_ref[0, half], qq[:, cols]) * scale, NEG)
        top = col_max(s)
        p = jnp.exp2(s - top)
        dp = dot_nt(v_ref[0, half], oo[:, cols])
        diag[2 * j] = p
        diag[2 * j + 1] = dp
        state[j:j + 1] = top
        state[2 + j:3 + j] = col_sum(p)
        state[4 + j:5 + j] = col_sum(p * dp)
        tops[NZ, j:j + 1] = top

    pl.semaphore_wait(barrier, count)

    def first_k(d):
        return remote(k_ref.at[0], kbuf.at[z, x, c], p1ks.at[d], p1kr.at[d, c], at(z, xoff(d), 0))

    def first_v(i):
        return remote(v_ref.at[0], vbuf.at[z, x, c], p1vs.at[i], p1vr.at[i, c],
                      at(zoff((0, 1, -1, 2, -2)[i]), x, 1))

    def k_send(way, k, j):
        step = 1 if way == 0 else -1
        ref = kbuf.at[zoff(-step * (k - 1)), xoff(j)]
        return remote(ref, ref, zks.at[way, k - 1, j], zkr.at[way, k - 1, j], at(zoff(step), x, 0))

    def v_far(way, k):
        step = 1 if way == 0 else -1
        if k == 3:
            ref = vbuf.at[zoff(-2 * step), x]
        else:
            ref = vbuf.at[zoff(-2 * step), x, way]
        return remote(ref, ref, zvs.at[way, k - 3], zvr.at[way, k - 3],
                      at(zoff(step * (k - 2)), x, 1))

    def v_x1(way, n):
        step = 1 if way == 0 else -1
        ref = vbuf.at[zoff(ORDER[n]), x]
        return remote(ref, ref, x1s.at[way, n], x1r.at[way, n], at(z, xoff(step), 1))

    def v_x2(way, n):
        step = 1 if way == 0 else -1
        ref = vbuf.at[zoff(ORDER[n]), xoff(-step), way]
        return remote(ref, ref, x2s.at[way, n], x2r.at[way, n], at(z, xoff(step), 1))

    def hand_over(buf, n):
        ref = buf.at[row_of(n)]
        return remote(ref, ref, d2ds.at[n], d2dr.at[n], sibling)

    def landed(sem):
        pltpu.make_async_copy(kbuf.at[0, 0, 0], kbuf.at[0, 0, 0], sem).wait()

    def gather_k(n):
        d = ORDER[n]
        k = abs(d)
        if k == 0:
            for j in ACROSS:
                src = (NX - j) % NX
                for cc in range(2):
                    if (src, cc) != (0, 0):
                        landed(p1kr.at[src, cc])
                for w in range(2):
                    k_send(w, 1, j).start()
        elif k < 4:
            w = 1 if d > 0 else 0
            for j in ACROSS:
                k_send(w, k, j).wait_recv()
                if k < 3 or j in SETS[w]:
                    k_send(w, k + 1, j).start()
        else:
            for w in range(2):
                for j in SETS[w]:
                    k_send(w, 4, j).wait_recv()
        hand_over(kbuf, n).start()

    def v_stage1(n):
        d = ORDER[n]
        if d == 0:
            landed(p1vr.at[0, 0])
        elif abs(d) <= 2:
            i = (0, 1, -1, 2, -2).index(-d)
            for cc in range(2):
                landed(p1vr.at[i, cc])
            if abs(d) == 2:
                w = 1 if d > 0 else 0
                v_far(w, 3).start()
                v_far(w, 4).start()
        elif abs(d) == 3:
            v_far(1 if d > 0 else 0, 3).wait_recv()
        else:
            v_far(0, 4).wait_recv()
            v_far(1, 4).wait_recv()
        for w in range(2):
            v_x1(w, n).start()

    def v_stage2(n):
        for w in range(2):
            v_x1(w, n).wait_recv()
            v_x2(w, n).start()

    def v_stage3(n):
        for w in range(2):
            v_x2(w, n).wait_recv()
        hand_over(vbuf, n).start()

    for d in (1, 3, 2):
        first_k(d).start()

    @pl.when(c == 1)
    def _():
        first_k(0).start()
        vbuf[z, x, 1] = v_ref[0]

    @pl.when(c == 0)
    def _():
        first_v(0).start()
        kbuf[z, x, 0] = k_ref[0]

    for i in (3, 4, 1, 2):
        first_v(i).start()

    my_block = span_ref[0, me, 0]

    def early(b, i):
        return span_ref[0, b * ROW + i, 0] < my_block

    def pick(buf, b):
        e, both = [], []
        for i in range(ROW):
            blk = buf[b, i // 2, i % 2]
            lo, hi = blk[:HALF], blk[HALF:]
            s = early(b, i)
            zero = jnp.zeros_like(lo)
            e.append(lo)
            both.append(jnp.concatenate([jnp.where(s, lo, zero), jnp.where(s, zero, hi)], axis=1))
        return jnp.concatenate(e, axis=0), jnp.concatenate(both, axis=0)

    def softmax_row(n):
        b = row_of(n)

        @pl.when(c == 0)
        def _():
            hand_over(vbuf, n).wait_recv()

        @pl.when(c == 1)
        def _():
            hand_over(kbuf, n).wait_recv()

        ke, ksel = pick(kbuf, b)
        kselbuf[b] = ksel
        s1[b] = dot_nt(ke, qq[:, HD:]) * scale
        s2[b] = dot_nt(ksel, qq[...]) * scale
        ve, vsel = pick(vbuf, b)
        dp1[b] = dot_nt(ve, oo[:, HD:])
        dp2[b] = dot_nt(vsel, oo[...])
        old_e, old_l = state[0:1], state[1:2]
        m_e, m_l = old_e, jnp.maximum(old_l, col_max(s1[b]))
        low = jnp.full((1, ROWS), NEG, F32)
        high = jnp.full((1, ROWS), POS, F32)
        for i in range(ROW):
            top = col_max(s2[b, i * HALF:(i + 1) * HALF])
            s = early(b, i)
            top = jnp.where(b * ROW + i == me, low, top)
            m_e = jnp.maximum(m_e, jnp.where(s, top, low))
            m_l = jnp.maximum(m_l, jnp.where(s, low, top))
        a_e = jnp.exp2(old_e - m_e)
        a_l = jnp.exp2(old_l - m_l)
        l_e, l_l = state[2:3] * a_e, state[3:4] * a_l
        d_e, d_l = state[4:5] * a_e, state[5:6] * a_l
        for i in range(ROW):
            part = slice(i * HALF, (i + 1) * HALF)
            p = jnp.exp2(s1[b, part] - m_l)
            s1[b, part] = p
            l_l = l_l + col_sum(p)
            d_l = d_l + col_sum(p * dp1[b, part])
            s = early(b, i)
            top = jnp.where(s, m_e, m_l)
            top = jnp.where(b * ROW + i == me, high, top)
            p = jnp.exp2(s2[b, part] - top)
            s2[b, part] = p
            ps = col_sum(p)
            pd = col_sum(p * dp2[b, part])
            zero = jnp.zeros_like(ps)
            l_e = l_e + jnp.where(s, ps, zero)
            l_l = l_l + jnp.where(s, zero, ps)
            d_e = d_e + jnp.where(s, pd, zero)
            d_l = d_l + jnp.where(s, zero, pd)
        for i, v in enumerate((m_e, m_l, l_e, l_l, d_e, d_l)):
            state[i:i + 1] = v
        tops[b, 0:1] = m_e
        tops[b, 1:2] = m_l

    LAG = 3
    core0 = {i: (lambda i=i: gather_k(i)) for i in range(NZ)}
    core1_plan = {
        0: ((v_stage1, 0), (v_stage1, 1), (v_stage1, 2)),
        1: ((v_stage1, 3), (v_stage1, 4), (v_stage2, 0)),
        2: ((v_stage2, 1), (v_stage2, 2), (v_stage3, 0)),
        3: ((v_stage1, 5), (v_stage1, 6), (v_stage1, 7), (v_stage3, 1), (v_stage3, 2)),
        4: ((v_stage2, 3), (v_stage2, 4)),
        5: ((v_stage3, 3), (v_stage3, 4), (v_stage2, 5), (v_stage2, 6), (v_stage2, 7)),
        6: ((v_stage3, 5), (v_stage3, 6), (v_stage3, 7)),
    }

    def gather_step(i, _):
        for j in range(NZ):
            @pl.when((i == j) & (c == 0))
            def _():
                core0[j]()

            if j in core1_plan:
                @pl.when((i == j) & (c == 1))
                def _():
                    for stage, n in core1_plan[j]:
                        stage(n)

        @pl.when(i >= LAG)
        def _():
            softmax_row(i - LAG)

        return 0

    lax.fori_loop(0, NZ + LAG, gather_step, 0)

    m_e, m_l = state[0:1], state[1:2]
    r_e, r_l = 1.0 / state[2:3], 1.0 / state[3:4]
    d_e, d_l = state[4:5] * r_e, state[5:6] * r_l

    own_k, own_v = [], []
    for j, (m, r, d) in enumerate(((m_e, r_e, d_e), (m_l, r_l, d_l))):
        half = slice(j * HALF, (j + 1) * HALF)
        cols = slice(j * HD, (j + 1) * HD)
        p = diag[2 * j] * (jnp.exp2(tops[NZ, j:j + 1] - m) * r)
        ds = (p * (diag[2 * j + 1] - d)).astype(BF16)
        own_k.append(dot_nn(ds, qq[:, cols]) * INV_ROOT)
        own_v.append(dot_nn(p.astype(BF16), oo[:, cols]))
        dq2[cols] = dot_tn(k_ref[0, half], ds)
    for j in range(2):
        diag[j, :, :HD] = own_k[j]
        diag[j, :, HD:] = own_v[j]
    dql[...] = jnp.zeros_like(dql)
    state[2:3] = r_e
    state[3:4] = r_l
    state[4:5] = d_e
    state[5:6] = d_l

    def give(buf, m):
        b = row_of(NZ - 1 - m)
        return remote(buf.at[b], sib.at[b], sibs.at[m], sibr.at[m], sibling)

    def gradient_row(m):
        b = row_of(NZ - 1 - m)
        r_e, r_l, d_e, d_l = state[2:3], state[3:4], state[4:5], state[5:6]
        f_e = jnp.exp2(tops[b, 0:1] - state[0:1]) * r_e
        f_l = jnp.exp2(tops[b, 1:2] - state[1:2]) * r_l
        ke = jnp.concatenate([kbuf[b, i // 2, i % 2, :HALF] for i in range(ROW)], axis=0)
        ksel = kselbuf[b]
        p1 = s1[b] * f_l
        ds1 = (p1 * (dp1[b] - d_l)).astype(BF16)
        p1 = p1.astype(BF16)
        p2s, ds2s = [], []
        for i in range(ROW):
            part = slice(i * HALF, (i + 1) * HALF)
            s = early(b, i)
            p = s2[b, part] * jnp.where(s, f_e, f_l)
            ds2s.append((p * (dp2[b, part] - jnp.where(s, d_e, d_l))).astype(BF16))
            p2s.append(p.astype(BF16))
        p2 = jnp.concatenate(p2s, axis=0)
        ds2 = jnp.concatenate(ds2s, axis=0)
        v1 = dot_nn(p1, oo[:, HD:])
        v2 = dot_nn(p2, oo[...])
        k1 = dot_nn(ds1, qq[:, HD:]) * INV_ROOT
        k2 = dot_nn(ds2, qq[...]) * INV_ROOT
        dql[...] += dot_tn(ke, ds1)
        dq2[...] += dot_tn(ksel, ds2)
        for i in range(ROW):
            part = slice(i * HALF, (i + 1) * HALF)
            s = early(b, i)
            zero = jnp.zeros((HALF, HD), F32)
            cell = (b, i // 2, i % 2)
            lo, hi = slice(0, HALF), slice(HALF, 2 * HALF)
            pv[(*cell, lo)] = (v1[part] + jnp.where(s, v2[part, :HD], zero)).astype(BF16)
            pv[(*cell, hi)] = jnp.where(s, zero, v2[part, HD:]).astype(BF16)
            pk[(*cell, lo)] = (k1[part] + jnp.where(s, k2[part, :HD], zero)).astype(BF16)
            pk[(*cell, hi)] = jnp.where(s, zero, k2[part, HD:]).astype(BF16)

        @pl.when(m == NZ - 1)
        def _():
            for j in range(2):
                half = slice(j * HALF, (j + 1) * HALF)
                pk[z, x, c, half] = (pk[z, x, c, half].astype(F32) + diag[j, :, :HD]).astype(BF16)
                pv[z, x, c, half] = (pv[z, x, c, half].astype(F32) + diag[j, :, HD:]).astype(BF16)

        @pl.when(c == 0)
        def _():
            give(pv, m).start()

        @pl.when(c == 1)
        def _():
            give(pk, m).start()

    def add_into(dst, idx, *terms):
        total = dst[idx].astype(F32)
        for ref, i in terms:
            total = total + ref[i].astype(F32)
        dst[idx] = total.astype(BF16)

    def k_back(way, k, j):
        step = 1 if way == 0 else -1
        return remote(pk.at[zoff(step * k), xoff(j)], rr.at[way, k - 1, j],
                      rs.at[way, k - 1, j], rrsem.at[way, k - 1, j], at(zoff(step), x, 0))

    def k_across(j):
        return remote(pk.at[z, xoff(j)], xr.at[j], xs.at[j], xrsem.at[j], at(z, xoff(j), 0))

    def k_hop(m):
        give(pk, m).wait_recv()
        d = ORDER[NZ - 1 - m]
        k = abs(d)
        if k == 4:
            plan = [(w, j, False) for i in range(2) for w, j in ((0, SETS[0][i]), (1, SETS[1][i]))]
        else:
            w = 0 if d > 0 else 1
            plan = [(w, j, k < 3 or j in SETS[w]) for j in SETS[1 - w] + SETS[w]]
        for w, j, has in plan:
            cell = (zoff(d), xoff(j))
            terms = [(sib, cell)]
            if has:
                k_back(w, k + 1, j).wait_recv()
                terms.append((rr, (w, k, j)))
            add_into(pk, cell, *terms)
            k_back(w, k, j).start()

    def k_last():
        give(pk, NZ - 1).wait_recv()
        for j in (2, 1, 3, 0):
            for w in range(2):
                k_back(w, 1, j).wait_recv()
            cell = (z, xoff(j))
            add_into(pk, cell, (sib, cell), (rr, (0, 0, j)), (rr, (1, 0, j)))
            if j:
                k_across(j).start()
        total = pk[z, x].astype(F32)
        for j in range(1, NX):
            k_across(j).wait_recv()
            total = total + xr[j].astype(F32)
        ysum[...] = total.astype(BF16)

    def v_back2(way, m):
        step = 1 if way == 0 else -1
        return remote(pv.at[zoff(ORDER[NZ - 1 - m]), xoff(2), way], cr2.at[way, m],
                      c2s.at[way, m], c2r.at[way, m], at(z, xoff(step), 1))

    def v_back1(way, m):
        step = 1 if way == 0 else -1
        return remote(pv.at[zoff(ORDER[NZ - 1 - m]), xoff(step)], cr1.at[way, m],
                      c1s.at[way, m], c1r.at[way, m], at(z, xoff(step), 1))

    def v_z(way, k):
        step = 1 if way == 0 else -1
        if k == 4:
            src, dst, far = pv.at[zoff(4), x, way], zr.at[way, 3, way], 2
        else:
            src, dst, far = pv.at[zoff(step * k), x], zr.at[way, k - 1], (1, 2, 1)[k - 1]
        return remote(src, dst, zs.at[way, k - 1], zrsem.at[way, k - 1], at(zoff(step * far), x, 1))

    def v_hop2(m):
        give(pv, m).wait_recv()
        for w in range(2):
            cell = (zoff(ORDER[NZ - 1 - m]), xoff(2), w)
            add_into(pv, cell, (sib, cell))
            v_back2(w, m).start()

    def v_hop1(m):
        for w in range(2):
            row = zoff(ORDER[NZ - 1 - m])
            col = xoff(1 if w == 0 else -1)
            add_into(pv, (row, col, 1 - w), (sib, (row, col, 1 - w)))
            v_back2(w, m).wait_recv()
            add_into(pv, (row, col, w), (sib, (row, col, w)), (cr2, (w, m)))
            v_back1(w, m).start()

    def v_hop0(m):
        d = ORDER[NZ - 1 - m]
        k = abs(d)
        w = 0 if d > 0 else 1
        cell = (zoff(d), x)
        for ww in range(2):
            v_back1(ww, m).wait_recv()
        terms = [(sib, cell), (cr1, (0, m)), (cr1, (1, m))]
        if k == 2:
            v_z(w, 3).wait_recv()
            terms.append((zr, (w, 2)))
        add_into(pv, cell, *terms)
        if k == 2:
            v_z(w, 4).wait_recv()
            add_into(pv, (*cell, w), (zr, (w, 3, w)))
        if k == 4:
            v_z(0, 4).start()
            v_z(1, 4).start()
        elif k > 0:
            v_z(w, k).start()

    def v_last():
        total = pv[z, x].astype(F32)
        for k in (1, 2):
            for w in range(2):
                v_z(w, k).wait_recv()
                total = total + zr[w, k - 1].astype(F32)
        ysum[...] = total.astype(BF16)

    back0 = {2: ((k_hop, 0),), 5: ((k_hop, 1),), 6: ((k_hop, 2),)}
    back1 = {m: ((v_hop2, m - 2),) + (((v_hop1, m - 5),) if m >= 5 else ()) for m in range(2, NZ)}

    def scatter_step(m, _):
        gradient_row(m)
        for j in range(NZ):
            for core, plan in ((0, back0), (1, back1)):
                if j in plan:
                    @pl.when((m == j) & (c == core))
                    def _():
                        for stage, n in plan[j]:
                            stage(n)
        return 0

    lax.fori_loop(0, NZ, scatter_step, 0)

    @pl.when(c == 0)
    def _():
        k_hop(3)

    @pl.when(c == 1)
    def _():
        v_hop2(6)
        v_hop2(7)
        v_hop1(3)
        v_hop1(4)

    for j, acc in enumerate((dq2[0:HD], dq2[HD:2 * HD] + dql[...])):
        g = (acc * INV_ROOT).T.astype(BF16)
        for h in range(HEADS):
            dqst[j * HALF:(j + 1) * HALF, h * HD:(h + 1) * HD] = g[h * HALF:(h + 1) * HALF]
    dq_copy = remote(dqst, dq_out.at[0], dqsem.at[0], dqsem.at[1], other(t, c))
    dq_copy.start()

    @pl.when(c == 0)
    def _():
        for m in (4, 5, 6):
            k_hop(m)
        k_last()

    @pl.when(c == 1)
    def _():
        v_hop0(0)
        v_hop0(1)
        v_hop0(2)
        v_hop1(5)
        v_hop1(6)
        v_hop1(7)
        for m in range(3, NZ):
            v_hop0(m)
        v_last()

    def last(tt, cc):
        i = tt * 2 + cc
        return remote(ysum.at[cc], yr.at[c, t], ys.at[i], yrsem.at[c, t], other(tt, cc))

    for tt in range(NT):
        for cc in range(2):
            last(tt, cc).start()

    @pl.when(c == 0)
    def _():
        first_v(0).wait_send()
        for w in range(2):
            for k in range(1, 5):
                for j in range(NX):
                    if k < 4 or j in SETS[w]:
                        k_send(w, k, j).wait_send()
                        k_back(w, k, j).wait_send()
        for n in range(NZ):
            hand_over(kbuf, n).wait_send()
            give(pv, n).wait_send()
        for j in range(1, NX):
            k_across(j).wait_send()

    @pl.when(c == 1)
    def _():
        first_k(0).wait_send()
        for w in range(2):
            for n in range(NZ):
                v_x1(w, n).wait_send()
                v_x2(w, n).wait_send()
                v_back1(w, n).wait_send()
                v_back2(w, n).wait_send()
            for k in (3, 4):
                v_far(w, k).wait_send()
            for k in range(1, 5):
                v_z(w, k).wait_send()
        for n in range(NZ):
            hand_over(vbuf, n).wait_send()
            give(pk, n).wait_send()

    for d in range(1, NX):
        first_k(d).wait_send()
    for i in range(1, 5):
        first_v(i).wait_send()

    for kind, out in ((0, dk_out), (1, dv_out)):
        total = jnp.zeros((128, HD), F32)
        for tt in range(NT):
            landed(yrsem.at[kind, tt])
            total = total + yr[kind, tt].astype(F32)
        out[0] = total.astype(BF16)
    for tt in range(NT):
        for cc in range(2):
            last(tt, cc).wait_send()
    dq_copy.wait()


def per_device(queries, keys, values, grad_out, span_order):
    vmem = pl.BlockSpec(memory_space=pltpu.VMEM)
    dma = pltpu.SemaphoreType.DMA

    def plane():
        return pltpu.VMEM((NZ, NX, 2, 128, HD), BF16)

    scratch = [
        plane(),
        plane(),
        pltpu.VMEM((NZ, KEYS, ROWS), F32),
        pltpu.VMEM((NZ, KEYS, ROWS), F32),
        pltpu.VMEM((NZ, KEYS, ROWS), F32),
        pltpu.VMEM((NZ, KEYS, ROWS), F32),
        pltpu.VMEM((NZ, KEYS, 2 * HD), BF16),
        pltpu.VMEM((ROWS, 2 * HD), BF16),
        pltpu.VMEM((ROWS, 2 * HD), BF16),
        pltpu.VMEM((HD, ROWS), F32),
        pltpu.VMEM((2 * HD, ROWS), F32),
        pltpu.VMEM((128, HEADS * HD), BF16),
        pltpu.VMEM((8, ROWS), F32),
        pltpu.VMEM((NZ + 1, 8, ROWS), F32),
        pltpu.VMEM((4, HALF, ROWS), F32),
        plane(),
        plane(),
        plane(),
        pltpu.VMEM((2, 4, NX, 2, 128, HD), BF16),
        pltpu.VMEM((2, NZ, 2, 128, HD), BF16),
        pltpu.VMEM((2, NZ, 128, HD), BF16),
        pltpu.VMEM((2, 4, 2, 128, HD), BF16),
        pltpu.VMEM((NX, 2, 128, HD), BF16),
        pltpu.VMEM((2, 128, HD), BF16),
        pltpu.VMEM((2, NT, 128, HD), BF16),
        dma((NX,)), dma((NX, 2)), dma((5,)), dma((5, 2)),
        dma((2, 4, NX)), dma((2, 4, NX)), dma((2, 2)), dma((2, 2)),
        dma((2, NZ)), dma((2, NZ)), dma((2, NZ)), dma((2, NZ)),
        dma((NZ,)), dma((NZ,)),
        dma((NZ,)), dma((NZ,)),
        dma((2, 4, NX)), dma((2, 4, NX)),
        dma((2, NZ)), dma((2, NZ)), dma((2, NZ)), dma((2, NZ)),
        dma((2, 4)), dma((2, 4)), dma((NX,)), dma((NX,)),
        dma((8,)), dma((2, NT)), dma((2,)),
    ]
    return pl.pallas_call(
        kernel,
        out_shape=(
            jax.ShapeDtypeStruct(queries.shape, BF16),
            jax.ShapeDtypeStruct(keys.shape, BF16),
            jax.ShapeDtypeStruct(values.shape, BF16),
        ),
        in_specs=[vmem, vmem, vmem, vmem, pl.BlockSpec(memory_space=pltpu.SMEM)],
        out_specs=(pl.BlockSpec(memory_space=pl.ANY), vmem, vmem),
        scratch_shapes=scratch,
        compiler_params=pltpu.CompilerParams(
            collective_id=1, has_side_effects=True, vmem_limit_bytes=56 * 2**20
        ),
        name="attention_backward",
    )(queries, keys, values, grad_out, span_order)


def solution(mesh):
    return jax.shard_map(
        per_device,
        mesh=mesh,
        in_specs=(
            P("pipe", "ctx", "tp"),
            P("pipe", "ctx", None),
            P("pipe", "ctx", None),
            P("pipe", "ctx", "tp"),
            P("pipe", None, None),
        ),
        out_specs=(P("pipe", "ctx", "tp"), P("pipe", "ctx", None), P("pipe", "ctx", None)),
        check_vma=False,
    )
```

```python
import functools

import jax
import jax.numpy as jnp
from jax import lax
from jax.experimental import pallas as pl
from jax.experimental.pallas import tpu as pltpu
from jax.sharding import PartitionSpec as P

MESH = pl.DeviceIdType.MESH
F32 = jnp.float32
BF16 = jnp.bfloat16

NZ = 8
NX = 4
NT = 4
HEADS = 4
HALF = 64
HD = 128
ROWS = HEADS * HALF
SLOTS = 2 * ROWS
KEYS = NX * HALF
INV_ROOT = HD ** (-0.5)
LOG2E = 1.4426950408889634
NEG = -1e30
POS = 1e30
ORDER = (0, 1, -1, 2, -2, 3, -3, 4)
ACROSS = (0, 1, 3, 2)
SETS = ((0, 1), (3, 2))


def dot_nt(a, b):
    return lax.dot_general(a, b, (((1,), (1,)), ((), ())), preferred_element_type=F32)


def dot_nn(a, b):
    return jnp.dot(a, b, preferred_element_type=F32)


def dot_tn(a, b):
    return lax.dot_general(a, b, (((0,), (0,)), ((), ())), preferred_element_type=F32)


def col_sum(v):
    return jnp.sum(v, axis=0, keepdims=True)


def col_max(v):
    return jnp.max(v, axis=0, keepdims=True)


def kernel(
    q_ref, k_ref, v_ref, g_ref, span_ref,
    dq_out, dk_out, dv_out,
    kbuf, vbuf, s1, s2, dp1, dp2, kselbuf, qq, oo, pq, pg, dql, dq2, dqst, dqr,
    state, tops, diag, sums_out, sums_in,
    pk, pv, sib, rr, cx, zr, xr, ysum, yr,
    p1ks, p1kr, p1vs, p1vr, zks, zkr, x1s, x1r, d2ds, d2dr,
    pqs, pqr, sums_s, sums_r, sibs, sibr, rs, rrsem, c1s, c1r, zs, zrsem, xs, xrsem, ys, yrsem, dqs, dqsr,
):
    pipe = lax.axis_index("pipe")
    me = lax.axis_index("ctx")
    t = lax.axis_index("tp")
    z = me // (2 * NX)
    x = (me // 2) % NX
    c = me % 2
    half = t % 2
    mates = (t + 1 - 2 * half, lax.rem(t + 2 * half + NT - 1, NT))

    def at(zz, xx, cc):
        return (pipe, (zz * NX + xx) * 2 + cc, t)

    def zoff(d):
        return lax.rem(z + d + NZ, NZ)

    def xoff(d):
        return lax.rem(x + d + NX, NX)

    def row_of(n):
        return zoff(((n + 1) // 2) * (2 * (n % 2) - 1))

    def mate(j):
        return (pipe, me, mates[j])

    def other(tt, cc):
        return (1 - pipe, (z * NX + x) * 2 + cc, tt)

    sibling = at(z, x, 1 - c)

    def remote(src, dst, ssem, rsem, dev):
        return pltpu.make_async_remote_copy(
            src_ref=src, dst_ref=dst, send_sem=ssem, recv_sem=rsem,
            device_id=dev, device_id_type=MESH,
        )

    barrier = pltpu.get_barrier_semaphore()
    count = 0

    def greet(dev):
        pl.semaphore_signal(barrier, inc=1, device_id=dev, device_id_type=MESH)

    greet(sibling)
    count += 1
    for cc in range(2):
        for d in range(1, NX):
            greet(at(z, xoff(d), cc))
            count += 1
        for d in range(1, NZ):
            greet(at(zoff(d), x, cc))
            count += 1
        for tt in range(NT):
            greet(other(tt, cc))
            count += 1
    for j in range(2):
        greet(mate(j))
        count += 1

    def lay_rows(dst, base, src, lo, j):
        for h in range(HEADS):
            dst[base + h * HALF:base + (h + 1) * HALF, j * HD:(j + 1) * HD] = src[
                lo:lo + HALF, h * HD:(h + 1) * HD]

    for j in range(2):
        lay_rows(qq, 0, q_ref.at[0], j * HALF, j)
        lay_rows(oo, 0, g_ref.at[0], j * HALF, j)
    low = jnp.full((1, SLOTS), NEG, F32)
    state[...] = jnp.zeros_like(state)
    sums_out[...] = jnp.zeros_like(sums_out)
    for j in range(2):
        state[j:j + 1] = low
    dql[...] = jnp.zeros_like(dql)
    dq2[...] = jnp.zeros_like(dq2)
    scale = INV_ROOT * LOG2E

    pl.semaphore_wait(barrier, count)

    def swap_rows(j, kind):
        src = (q_ref, g_ref)[kind].at[0, pl.ds(j * HALF, HALF)]
        dst = (pq, pg)[kind].at[j]
        return remote(src, dst, pqs.at[j, kind], pqr.at[j, kind], mate(j))

    for kind in range(2):
        for j in range(2):
            swap_rows(j, kind).start()

    def first_k(d):
        return remote(k_ref.at[0], kbuf.at[z, x], p1ks.at[d], p1kr.at[d], at(z, xoff(d), 1))

    def first_v(d):
        return remote(v_ref.at[0], vbuf.at[z, x], p1vs.at[d], p1vr.at[d], at(zoff(d), x, 0))

    def k_send(way, k, j):
        step = 1 if way == 0 else -1
        back, far = (2, 2) if k == 4 else (k - 1, 1)
        ref = kbuf.at[zoff(-step * back), xoff(j)]
        return remote(ref, ref, zks.at[way, k - 1, j], zkr.at[way, k - 1, j],
                      at(zoff(step * far), x, 1))

    def v_x(d, n):
        ref = vbuf.at[zoff(ORDER[n]), x]
        return remote(ref, ref, x1s.at[d, n], x1r.at[d, n], at(z, xoff(d), 0))

    def hand_over(buf, n):
        ref = buf.at[row_of(n)]
        return remote(ref, ref, d2ds.at[n], d2dr.at[n], sibling)

    def landed(sem):
        pltpu.make_async_copy(kbuf.at[0, 0], kbuf.at[0, 0], sem).wait()

    def gather_k(n):
        d = ORDER[n]
        k = abs(d)
        if k == 0:
            for j in ACROSS:
                src = (NX - j) % NX
                if src:
                    landed(p1kr.at[src])
                else:
                    @pl.when(half == 0)
                    def _():
                        landed(p1kr.at[0])
                for w in range(2):
                    k_send(w, 1, j).start()
        elif k < 4:
            w = 1 if d > 0 else 0
            for j in ACROSS:
                k_send(w, k, j).wait_recv()
                if k == 1:
                    k_send(w, 2, j).start()
                if k == 2:
                    if j in SETS[w]:
                        k_send(w, 4, j).start()
                    k_send(w, 3, j).start()
        else:
            for w in range(2):
                for j in SETS[w]:
                    k_send(w, 4, j).wait_recv()
        hand_over(kbuf, n).start()

    def v_stage1(n):
        d = ORDER[n]
        if d:
            landed(p1vr.at[-d % NZ])
        else:
            @pl.when(half == 1)
            def _():
                landed(p1vr.at[0])
        for dx in (1, 3, 2):
            v_x(dx, n).start()

    def v_stage2(n):
        for dx in range(1, NX):
            v_x(dx, n).wait_recv()
        hand_over(vbuf, n).start()

    @pl.when(c == half)
    def _():
        for d in (1, 3, 2):
            first_k(d).start()

        @pl.when(c == 0)
        def _():
            first_k(0).start()
            vbuf[z, x] = v_ref[0]

        @pl.when(c == 1)
        def _():
            first_v(0).start()
            kbuf[z, x] = k_ref[0]

        for d in (1, 7, 2, 6, 3, 5, 4):
            first_v(d).start()

    def drain_gather():
        @pl.when(c == 1)
        def _():
            for w in range(2):
                for k in range(1, 5):
                    for j in range(NX):
                        if k < 4 or j in SETS[w]:
                            k_send(w, k, j).wait_send()
            for n in range(NZ):
                hand_over(kbuf, n).wait_send()

        @pl.when(c == 0)
        def _():
            for n in range(NZ):
                for dx in range(1, NX):
                    v_x(dx, n).wait_send()
                hand_over(vbuf, n).wait_send()

        @pl.when(c == half)
        def _():
            for d in range(1, NX):
                first_k(d).wait_send()
            for d in range(1, NZ):
                first_v(d).wait_send()

            @pl.when(c == 0)
            def _():
                first_k(0).wait_send()

            @pl.when(c == 1)
            def _():
                first_v(0).wait_send()

        for j in range(2):
            for kind in range(2):
                swap_rows(j, kind).wait_send()
            swap_sums(j).wait_send()

    my_block = span_ref[0, 0, me]

    def index(b, i):
        return (b * NX + i) * 2 + half

    def early(b, i):
        return span_ref[0, 0, index(b, i)] < my_block

    def pick(buf, b):
        e, both = [], []
        for i in range(NX):
            blk = buf[b, i]
            lo, hi = blk[:HALF], blk[HALF:]
            s = early(b, i)
            zero = jnp.zeros_like(lo)
            e.append(lo)
            both.append(jnp.concatenate([jnp.where(s, lo, zero), jnp.where(s, zero, hi)], axis=1))
        return jnp.concatenate(e, axis=0), jnp.concatenate(both, axis=0)

    def softmax_row(n):
        b = row_of(n)

        @pl.when(c == 1)
        def _():
            hand_over(vbuf, n).wait_recv()

        @pl.when(c == 0)
        def _():
            hand_over(kbuf, n).wait_recv()

        ke, ksel = pick(kbuf, b)
        kselbuf[b] = ksel
        s1[b] = dot_nt(ke, qq[:, HD:]) * scale
        s2[b] = dot_nt(ksel, qq[...]) * scale
        ve, vsel = pick(vbuf, b)
        dp1[b] = dot_nt(ve, oo[:, HD:])
        dp2[b] = dot_nt(vsel, oo[...])
        old_e, old_l = state[0:1], state[1:2]
        m_e, m_l = old_e, jnp.maximum(old_l, col_max(s1[b]))
        low = jnp.full((1, SLOTS), NEG, F32)
        high = jnp.full((1, SLOTS), POS, F32)
        for i in range(NX):
            top = col_max(s2[b, i * HALF:(i + 1) * HALF])
            s = early(b, i)
            top = jnp.where(index(b, i) == me, low, top)
            m_e = jnp.maximum(m_e, jnp.where(s, top, low))
            m_l = jnp.maximum(m_l, jnp.where(s, low, top))
        a_e = jnp.exp2(old_e - m_e)
        a_l = jnp.exp2(old_l - m_l)
        l_e, l_l = state[2:3] * a_e, state[3:4] * a_l
        d_e, d_l = state[4:5] * a_e, state[5:6] * a_l
        for i in range(NX):
            part = slice(i * HALF, (i + 1) * HALF)
            p = jnp.exp2(s1[b, part] - m_l)
            s1[b, part] = p
            l_l = l_l + col_sum(p)
            d_l = d_l + col_sum(p * dp1[b, part])
            s = early(b, i)
            top = jnp.where(s, m_e, m_l)
            top = jnp.where(index(b, i) == me, high, top)
            p = jnp.exp2(s2[b, part] - top)
            s2[b, part] = p
            ps = col_sum(p)
            pd = col_sum(p * dp2[b, part])
            zero = jnp.zeros_like(ps)
            l_e = l_e + jnp.where(s, ps, zero)
            l_l = l_l + jnp.where(s, zero, ps)
            d_e = d_e + jnp.where(s, pd, zero)
            d_l = d_l + jnp.where(s, zero, pd)
        for i, v in enumerate((m_e, m_l, l_e, l_l, d_e, d_l)):
            state[i:i + 1] = v
        tops[b, 0:1] = m_e
        tops[b, 1:2] = m_l

    def diagonal():
        key_no = lax.broadcasted_iota(jnp.int32, (HALF, SLOTS), 0)
        tok_no = lax.broadcasted_iota(jnp.int32, (HALF, SLOTS), 1) % HALF
        seen = key_no <= tok_no
        for j in range(2):
            part = slice(j * HALF, (j + 1) * HALF)
            cols = slice(j * HD, (j + 1) * HD)
            s = jnp.where(seen, dot_nt(k_ref[0, part], qq[:, cols]) * scale, NEG)
            top = col_max(s)
            p = jnp.exp2(s - top)
            dp = dot_nt(v_ref[0, part], oo[:, cols])
            diag[2 * j] = p
            diag[2 * j + 1] = dp
            state[j:j + 1] = top
            state[2 + j:3 + j] = col_sum(p)
            state[4 + j:5 + j] = col_sum(p * dp)
            tops[NZ, j:j + 1] = top

    def swap_sums(j):
        return remote(sums_out.at[j], sums_in.at[j], sums_s.at[j], sums_r.at[j], mate(j))

    LAG = 5
    plans = (
        {
            0: [(v_stage1, n) for n in range(5)],
            1: [(v_stage1, 5), (v_stage1, 6), (v_stage1, 7), (v_stage2, 0), (v_stage2, 1)],
            2: [(v_stage2, 2), (v_stage2, 3)],
            3: [(v_stage2, 4)],
            4: [(v_stage2, 5)],
            5: [(v_stage2, 6)],
            6: [(v_stage2, 7)],
        },
        {n: [(gather_k, n)] for n in range(NZ)},
    )

    def run_plan(i, plans):
        for core in range(2):
            for j, todo in plans[core].items():
                @pl.when((i == j) & (c == core))
                def _():
                    for stage, n in todo:
                        stage(n)

    def gather_step(i, _):
        run_plan(i, plans)

        @pl.when(i == LAG)
        def _():
            for kind in range(2):
                for j in range(2):
                    swap_rows(j, kind).wait_recv()
                    lay_rows((qq, oo)[kind], ROWS, (pq, pg)[kind].at[j], 0, j)

            @pl.when(c == half)
            def _():
                diagonal()

        @pl.when(i >= LAG)
        def _():
            softmax_row(i - LAG)

        return 0

    lax.fori_loop(0, NZ + LAG, gather_step, 0)

    for j in range(2):
        for i in range(3):
            sums_out[j, i:i + 1] = state[2 * i + j:2 * i + j + 1]
        swap_sums(j).start()
    for j in range(2):
        swap_sums(j).wait_recv()
        m, l, d = (state[2 * i + j:2 * i + j + 1] for i in range(3))
        m2, l2, d2 = (
            jnp.concatenate([sums_in[j, i:i + 1, ROWS:], sums_in[j, i:i + 1, :ROWS]], axis=1)
            for i in range(3)
        )
        top = jnp.maximum(m, m2)
        a, a2 = jnp.exp2(m - top), jnp.exp2(m2 - top)
        r = 1.0 / (l * a + l2 * a2)
        state[j:j + 1] = top
        state[2 + j:3 + j] = r
        state[4 + j:5 + j] = (d * a + d2 * a2) * r

    @pl.when(c == half)
    def _():
        for j in range(2):
            part = slice(j * HALF, (j + 1) * HALF)
            cols = slice(j * HD, (j + 1) * HD)
            m, r, d = state[j:j + 1], state[2 + j:3 + j], state[4 + j:5 + j]
            p = diag[2 * j] * (jnp.exp2(tops[NZ, j:j + 1] - m) * r)
            ds = (p * (diag[2 * j + 1] - d)).astype(BF16)
            dq2[cols] = dot_tn(k_ref[0, part], ds)
            diag[2 * j, :, :HD] = dot_nn(ds, qq[:, cols]) * INV_ROOT
            diag[2 * j, :, HD:2 * HD] = dot_nn(p.astype(BF16), oo[:, cols])

    def give(buf, m):
        b = row_of(NZ - 1 - m)
        return remote(buf.at[b], sib.at[b], sibs.at[m], sibr.at[m], sibling)

    def gradient_row(m):
        b = row_of(NZ - 1 - m)
        r_e, r_l, d_e, d_l = state[2:3], state[3:4], state[4:5], state[5:6]
        f_e = jnp.exp2(tops[b, 0:1] - state[0:1]) * r_e
        f_l = jnp.exp2(tops[b, 1:2] - state[1:2]) * r_l
        ke = jnp.concatenate([kbuf[b, i, :HALF] for i in range(NX)], axis=0)
        ksel = kselbuf[b]
        p1 = s1[b] * f_l
        ds1 = (p1 * (dp1[b] - d_l)).astype(BF16)
        p1 = p1.astype(BF16)
        p2s, ds2s = [], []
        for i in range(NX):
            part = slice(i * HALF, (i + 1) * HALF)
            s = early(b, i)
            p = s2[b, part] * jnp.where(s, f_e, f_l)
            ds2s.append((p * (dp2[b, part] - jnp.where(s, d_e, d_l))).astype(BF16))
            p2s.append(p.astype(BF16))
        p2 = jnp.concatenate(p2s, axis=0)
        ds2 = jnp.concatenate(ds2s, axis=0)
        v1 = dot_nn(p1, oo[:, HD:])
        v2 = dot_nn(p2, oo[...])
        k1 = dot_nn(ds1, qq[:, HD:]) * INV_ROOT
        k2 = dot_nn(ds2, qq[...]) * INV_ROOT
        dql[...] += dot_tn(ke, ds1)
        dq2[...] += dot_tn(ksel, ds2)
        for i in range(NX):
            part = slice(i * HALF, (i + 1) * HALF)
            s = early(b, i)
            zero = jnp.zeros((HALF, HD), F32)
            cell = (b, i)
            lo, hi = slice(0, HALF), slice(HALF, 2 * HALF)
            pv[(*cell, lo)] = (v1[part] + jnp.where(s, v2[part, :HD], zero)).astype(BF16)
            pv[(*cell, hi)] = jnp.where(s, zero, v2[part, HD:]).astype(BF16)
            pk[(*cell, lo)] = (k1[part] + jnp.where(s, k2[part, :HD], zero)).astype(BF16)
            pk[(*cell, hi)] = jnp.where(s, zero, k2[part, HD:]).astype(BF16)

        @pl.when((m == NZ - 1) & (c == half))
        def _():
            for j in range(2):
                part = slice(j * HALF, (j + 1) * HALF)
                pk[z, x, part] = (pk[z, x, part].astype(F32) + diag[2 * j, :, :HD]).astype(BF16)
                pv[z, x, part] = (pv[z, x, part].astype(F32) + diag[2 * j, :, HD:2 * HD]).astype(BF16)

        @pl.when(c == 1)
        def _():
            give(pv, m).start()

        @pl.when(c == 0)
        def _():
            give(pk, m).start()

    def add_into(dst, idx, *terms):
        total = dst[idx].astype(F32)
        for ref, i in terms:
            total = total + ref[i].astype(F32)
        dst[idx] = total.astype(BF16)

    def k_back(way, k, j):
        step = 1 if way == 0 else -1
        far = 2 if k == 4 else 1
        return remote(pk.at[zoff(step * k), xoff(j)], rr.at[way, k - 1, j],
                      rs.at[way, k - 1, j], rrsem.at[way, k - 1, j], at(zoff(step * far), x, 1))

    def k_across(j):
        return remote(pk.at[z, xoff(j)], xr.at[j], xs.at[j], xrsem.at[j], at(z, xoff(j), 1))

    def k_hop(m):
        give(pk, m).wait_recv()
        d = ORDER[NZ - 1 - m]
        k = abs(d)
        if k == 4:
            plan = [(w, j, ()) for i in range(2) for w, j in ((0, SETS[0][i]), (1, SETS[1][i]))]
        else:
            w = 0 if d > 0 else 1
            if k == 3:
                plan = [(w, j, ()) for j in ACROSS]
            elif k == 2:
                plan = [(w, j, (3, 4) if j in SETS[w] else (3,)) for j in SETS[1 - w] + SETS[w]]
            else:
                plan = [(w, j, (2,)) for j in SETS[1 - w] + SETS[w]]
        for w, j, has in plan:
            cell = (zoff(d), xoff(j))
            terms = [(sib, cell)]
            for q in has:
                k_back(w, q, j).wait_recv()
                terms.append((rr, (w, q - 1, j)))
            add_into(pk, cell, *terms)
            k_back(w, k, j).start()

    def k_last():
        give(pk, NZ - 1).wait_recv()
        for j in (2, 1, 3, 0):
            for w in range(2):
                k_back(w, 1, j).wait_recv()
            cell = (z, xoff(j))
            add_into(pk, cell, (sib, cell), (rr, (0, 0, j)), (rr, (1, 0, j)))
            if j:
                k_across(j).start()
        total = pk[z, x].astype(F32)
        for j in range(1, NX):
            k_across(j).wait_recv()
            total = total + xr[j].astype(F32)
        ysum[...] = total.astype(BF16)

    def v_back(d, m):
        return remote(pv.at[zoff(ORDER[NZ - 1 - m]), xoff(d)], cx.at[d, m], c1s.at[d, m],
                      c1r.at[d, m], at(z, xoff(d), 0))

    def v_z(m):
        d = ORDER[NZ - 1 - m]
        return remote(pv.at[zoff(d), x], zr.at[m], zs.at[m], zrsem.at[m], at(zoff(d), x, 0))

    def v_out(m):
        give(pv, m).wait_recv()
        for d in (2, 1, 3):
            cell = (zoff(ORDER[NZ - 1 - m]), xoff(d))
            add_into(pv, cell, (sib, cell))
            v_back(d, m).start()

    def v_in(m):
        cell = (zoff(ORDER[NZ - 1 - m]), x)
        terms = [(sib, cell)]
        for d in range(1, NX):
            v_back(d, m).wait_recv()
            terms.append((cx, (d, m)))
        add_into(pv, cell, *terms)
        if m < NZ - 1:
            v_z(m).start()

    def v_last():
        total = pv[z, x].astype(F32)
        for m in range(NZ - 1):
            v_z(m).wait_recv()
            total = total + zr[m].astype(F32)
        ysum[...] = total.astype(BF16)

    back = (
        {m: [(v_out, m - 2)] + ([(v_in, m - 6)] if m >= 6 else []) for m in range(2, NZ)},
        {2: [(k_hop, 0)], 3: [(k_hop, 1)], 4: [(k_hop, 2)]},
    )

    def drain_scatter():
        @pl.when(c == 1)
        def _():
            for w in range(2):
                for k in range(1, 5):
                    for j in range(NX):
                        if k < 4 or j in SETS[w]:
                            k_back(w, k, j).wait_send()
            for n in range(NZ):
                give(pv, n).wait_send()
            for j in range(1, NX):
                k_across(j).wait_send()

        @pl.when(c == 0)
        def _():
            for m in range(NZ):
                for d in range(1, NX):
                    v_back(d, m).wait_send()
                if m < NZ - 1:
                    v_z(m).wait_send()
                give(pk, m).wait_send()

    def scatter_step(m, _):
        gradient_row(m)
        run_plan(m, back)
        return 0

    lax.fori_loop(0, NZ, scatter_step, 0)

    @pl.when(c == 0)
    def _():
        v_out(6)
        v_out(7)

    for j, acc in enumerate((dq2[0:HD], dq2[HD:2 * HD] + dql[...])):
        g = (acc * INV_ROOT).T.astype(BF16)
        for i in range(2):
            for h in range(HEADS):
                at_row = i * ROWS + h * HALF
                dqst[i, j * HALF:(j + 1) * HALF, h * HD:(h + 1) * HD] = g[at_row:at_row + HALF]

    def dq_copy(i):
        if i == 0:
            return remote(dqst.at[0], dqr.at[0], dqs.at[0], dqsr.at[0], other(t, c))
        part = pl.ds((i - 1) * HALF, HALF)
        return remote(dqst.at[1, part], dqr.at[1, part], dqs.at[i], dqsr.at[i],
                      other(mates[i - 1], c))

    for i in range(3):
        dq_copy(i).start()

    @pl.when(c == 1)
    def _():
        for m in range(3, NZ - 1):
            k_hop(m)
        k_last()

    @pl.when(c == 0)
    def _():
        for m in range(2, NZ):
            v_in(m)
        v_last()

    def last(tt):
        return remote(ysum, yr.at[1 - c, t // 2], ys.at[tt], yrsem.at[1 - c, t // 2],
                      other(tt, half))

    for tt in range(NT):
        last(tt).start()

    drain_gather()
    drain_scatter()

    for i in range(3):
        dq_copy(i).wait()
    dq_out[0] = (dqr[0].astype(F32) + dqr[1].astype(F32)).astype(BF16)
    for kind, out in ((0, dk_out), (1, dv_out)):
        for i in range(2):
            landed(yrsem.at[kind, i])
        out[0] = (yr[kind, 0].astype(F32) + yr[kind, 1].astype(F32)).astype(BF16)
    for tt in range(NT):
        last(tt).wait_send()


def per_device(queries, keys, values, grad_out, span_order):
    vmem = pl.BlockSpec(memory_space=pltpu.VMEM)
    dma = pltpu.SemaphoreType.DMA

    def plane():
        return pltpu.VMEM((NZ, NX, 128, HD), BF16)

    scratch = [
        plane(),
        plane(),
        pltpu.VMEM((NZ, KEYS, SLOTS), F32),
        pltpu.VMEM((NZ, KEYS, SLOTS), F32),
        pltpu.VMEM((NZ, KEYS, SLOTS), F32),
        pltpu.VMEM((NZ, KEYS, SLOTS), F32),
        pltpu.VMEM((NZ, KEYS, 2 * HD), BF16),
        pltpu.VMEM((SLOTS, 2 * HD), BF16),
        pltpu.VMEM((SLOTS, 2 * HD), BF16),
        pltpu.VMEM((2, HALF, HEADS * HD), BF16),
        pltpu.VMEM((2, HALF, HEADS * HD), BF16),
        pltpu.VMEM((HD, SLOTS), F32),
        pltpu.VMEM((2 * HD, SLOTS), F32),
        pltpu.VMEM((2, 128, HEADS * HD), BF16),
        pltpu.VMEM((2, 128, HEADS * HD), BF16),
        pltpu.VMEM((8, SLOTS), F32),
        pltpu.VMEM((NZ + 1, 8, SLOTS), F32),
        pltpu.VMEM((4, HALF, SLOTS), F32),
        pltpu.VMEM((2, 8, SLOTS), F32),
        pltpu.VMEM((2, 8, SLOTS), F32),
        plane(),
        plane(),
        plane(),
        pltpu.VMEM((2, 4, NX, 128, HD), BF16),
        pltpu.VMEM((NX, NZ, 128, HD), BF16),
        pltpu.VMEM((NZ, 128, HD), BF16),
        pltpu.VMEM((NX, 128, HD), BF16),
        pltpu.VMEM((128, HD), BF16),
        pltpu.VMEM((2, 2, 128, HD), BF16),
        dma((NX,)), dma((NX,)), dma((NZ,)), dma((NZ,)),
        dma((2, 4, NX)), dma((2, 4, NX)), dma((NX, NZ)), dma((NX, NZ)),
        dma((NZ,)), dma((NZ,)),
        dma((2, 2)), dma((2, 2)), dma((2,)), dma((2,)),
        dma((NZ,)), dma((NZ,)),
        dma((2, 4, NX)), dma((2, 4, NX)),
        dma((NX, NZ)), dma((NX, NZ)),
        dma((NZ,)), dma((NZ,)), dma((NX,)), dma((NX,)),
        dma((NT,)), dma((2, 2)), dma((3,)), dma((3,)),
    ]
    return pl.pallas_call(
        kernel,
        out_shape=(
            jax.ShapeDtypeStruct(queries.shape, BF16),
            jax.ShapeDtypeStruct(keys.shape, BF16),
            jax.ShapeDtypeStruct(values.shape, BF16),
        ),
        in_specs=[vmem, vmem, vmem, vmem, pl.BlockSpec(memory_space=pltpu.SMEM)],
        out_specs=(vmem, vmem, vmem),
        scratch_shapes=scratch,
        compiler_params=pltpu.CompilerParams(
            collective_id=1, has_side_effects=True, vmem_limit_bytes=56 * 2**20
        ),
        name="attention_backward",
    )(queries, keys, values, grad_out, jnp.swapaxes(span_order, 1, 2))


def solution(mesh):
    return jax.shard_map(
        per_device,
        mesh=mesh,
        in_specs=(
            P("pipe", "ctx", "tp"),
            P("pipe", "ctx", None),
            P("pipe", "ctx", None),
            P("pipe", "ctx", "tp"),
            P("pipe", None, None),
        ),
        out_specs=(P("pipe", "ctx", "tp"), P("pipe", "ctx", None), P("pipe", "ctx", None)),
        check_vma=False,
    )
```

```python
import functools

import jax
import jax.numpy as jnp
from jax import lax
from jax.experimental import pallas as pl
from jax.experimental.pallas import tpu as pltpu
from jax.sharding import PartitionSpec as P

MESH = pl.DeviceIdType.MESH
F32 = jnp.float32
BF16 = jnp.bfloat16

NZ = 8
NX = 4
NT = 4
HEADS = 4
HALF = 64
HD = 128
ROWS = HEADS * HALF
SLOTS = 2 * ROWS
KEYS = NX * HALF
INV_ROOT = HD ** (-0.5)
LOG2E = 1.4426950408889634
NEG = -1e30
POS = 1e30
ORDER = (0, 1, -1, 2, -2, 3, -3, 4)
ACROSS = (0, 1, 3, 2)
SETS = ((0, 1), (3, 2))


def dot_nt(a, b):
    return lax.dot_general(a, b, (((1,), (1,)), ((), ())), preferred_element_type=F32)


def dot_nn(a, b):
    return jnp.dot(a, b, preferred_element_type=F32)


def dot_tn(a, b):
    return lax.dot_general(a, b, (((0,), (0,)), ((), ())), preferred_element_type=F32)


def col_sum(v):
    return jnp.sum(v, axis=0, keepdims=True)


def col_max(v):
    return jnp.max(v, axis=0, keepdims=True)


def kernel(
    q_hbm, k_hbm, v_hbm, g_hbm, span_ref,
    dq_out, dk_out, dv_out,
    q_ref, k_ref, v_ref, g_ref, kbuf, vbuf, s1, s2, dp1, dp2, kselbuf, qq, oo, pq, pg, dql, dq2, dqst, dqr,
    state, tops, diag, sums_out, sums_in,
    pk, pv, sib, rr, cx, zr, xr, ysum, yr,
    insem, sent, p1kr, p1vr, zkr, x1r, d2dr, pqr, sums_r, sibr, rrsem, c1r, zrsem, xrsem,
    yrsem, dqsr,
):
    pipe = lax.axis_index("pipe")
    me = lax.axis_index("ctx")
    t = lax.axis_index("tp")
    z = me // (2 * NX)
    x = (me // 2) % NX
    c = me % 2
    half = t % 2
    mates = (t + 1 - 2 * half, lax.rem(t + 2 * half + NT - 1, NT))

    def at(zz, xx, cc):
        return (pipe, (zz * NX + xx) * 2 + cc, t)

    def zoff(d):
        return lax.rem(z + d + NZ, NZ)

    def xoff(d):
        return lax.rem(x + d + NX, NX)

    def row_of(n):
        return zoff(((n + 1) // 2) * (2 * (n % 2) - 1))

    def mate(j):
        return (pipe, me, mates[j])

    def other(tt, cc):
        return (1 - pipe, (z * NX + x) * 2 + cc, tt)

    sibling = at(z, x, 1 - c)

    def remote(src, dst, ssem, rsem, dev):
        return pltpu.make_async_remote_copy(
            src_ref=src, dst_ref=dst, send_sem=ssem, recv_sem=rsem,
            device_id=dev, device_id_type=MESH,
        )

    def take(i):
        src = (q_hbm, g_hbm, k_hbm, v_hbm)[i]
        return pltpu.make_async_copy(src, (q_ref, g_ref, k_ref, v_ref)[i], insem.at[0])

    for i in range(4):
        take(i).start()

    barrier = pltpu.get_barrier_semaphore()
    count = 0

    def greet(dev):
        pl.semaphore_signal(barrier, inc=1, device_id=dev, device_id_type=MESH)

    greet(sibling)
    count += 1
    for cc in range(2):
        for d in range(1, NX):
            greet(at(z, xoff(d), cc))
            count += 1
        for d in range(1, NZ):
            greet(at(zoff(d), x, cc))
            count += 1
        for tt in range(NT):
            greet(other(tt, cc))
            count += 1
    for j in range(2):
        greet(mate(j))
        count += 1

    def lay_rows(dst, base, src, lo, j):
        for h in range(HEADS):
            dst[base + h * HALF:base + (h + 1) * HALF, j * HD:(j + 1) * HD] = src[
                lo:lo + HALF, h * HD:(h + 1) * HD]

    low = jnp.full((1, SLOTS), NEG, F32)
    state[...] = jnp.zeros_like(state)
    sums_out[...] = jnp.zeros_like(sums_out)
    for j in range(2):
        state[j:j + 1] = low
    dql[...] = jnp.zeros_like(dql)
    dq2[...] = jnp.zeros_like(dq2)
    scale = INV_ROOT * LOG2E

    pl.semaphore_wait(barrier, count)

    def swap_rows(j, kind):
        src = (q_hbm, g_hbm)[kind].at[0, pl.ds(j * HALF, HALF)]
        dst = (pq, pg)[kind].at[j]
        return remote(src, dst, sent.at[4], pqr.at[0], mate(j))

    for kind in range(2):
        for j in range(2):
            swap_rows(j, kind).start()

    def first_k(d):
        return remote(k_hbm.at[0], kbuf.at[z, x], sent.at[0], p1kr.at[d], at(z, xoff(d), 1))

    def first_v(d):
        return remote(v_hbm.at[0], vbuf.at[z, x], sent.at[0], p1vr.at[d], at(zoff(d), x, 0))

    def k_slot(way, k, j):
        return {1: way, 2: 5 + way * 4 + j, 3: 2 + way, 4: 4}[k]

    def k_send(way, k, j):
        step = 1 if way == 0 else -1
        back, far = ((0, 1), (0, 2), (2, 1), (2, 2))[k - 1]
        ref = kbuf.at[zoff(-step * back), xoff(j)]
        return remote(ref, ref, sent.at[1], zkr.at[k_slot(way, k, j)],
                      at(zoff(step * far), x, 1))

    def v_x(d, n):
        ref = vbuf.at[zoff(ORDER[n]), x]
        return remote(ref, ref, sent.at[2], x1r.at[n], at(z, xoff(d), 0))

    def hand_over(buf, n):
        ref = buf.at[row_of(n)]
        return remote(ref, ref, sent.at[3], d2dr.at[n], sibling)

    def landed(sem, n=1):
        ref = cx.at[pl.ds(0, n)]
        pltpu.make_async_copy(ref, ref, sem).wait()

    def gather_k(n):
        d = ORDER[n]
        k = abs(d)
        if k == 0:
            for j in ACROSS:
                src = (NX - j) % NX
                if src:
                    landed(p1kr.at[src])
                else:
                    @pl.when(half == 0)
                    def _():
                        landed(p1kr.at[0])
                for w in range(2):
                    k_send(w, 2, j).start()
                    k_send(w, 1, j).start()
        elif k == 2:
            w = 1 if d > 0 else 0
            for j in ACROSS:
                landed(zkr.at[k_slot(w, 2, j)])
                if j in SETS[w]:
                    k_send(w, 4, j).start()
                k_send(w, 3, j).start()
        else:
            landed(zkr.at[k_slot(1 if d > 0 else 0, k, 0)], NX)
        hand_over(kbuf, n).start()

    def v_stage1(n):
        d = ORDER[n]
        if d:
            landed(p1vr.at[-d % NZ])
        else:
            @pl.when(half == 1)
            def _():
                landed(p1vr.at[0])
        for dx in (1, 3, 2):
            v_x(dx, n).start()

    def v_stage2(n):
        landed(x1r.at[n], NX - 1)
        hand_over(vbuf, n).start()

    def keep(src, buf):
        return pltpu.make_async_copy(src.at[0], buf.at[z, x], insem.at[1])

    @pl.when(c == half)
    def _():
        for d in (1, 3, 2):
            first_k(d).start()

        @pl.when(c == 0)
        def _():
            first_k(0).start()
            keep(v_hbm, vbuf).start()

        @pl.when(c == 1)
        def _():
            first_v(0).start()
            keep(k_hbm, kbuf).start()

        for d in (1, 7, 2, 6, 3, 5, 4):
            first_v(d).start()

        keep(k_hbm, kbuf).wait()

    landed(insem.at[0], 10)
    for j in range(2):
        lay_rows(qq, 0, q_ref.at[0], j * HALF, j)
        lay_rows(oo, 0, g_ref.at[0], j * HALF, j)

    def drain_gather():
        @pl.when(c == 1)
        def _():
            landed(sent.at[1], 28)

        @pl.when(c == 0)
        def _():
            landed(sent.at[2], 24)

        @pl.when(c == half)
        def _():
            landed(sent.at[0], 11)

        landed(sent.at[3], 32)
        landed(sent.at[4], 8)
        landed(sent.at[5], 1)

    my_block = span_ref[0, 0, me]

    def index(b, i):
        return (b * NX + i) * 2 + half

    def early(b, i):
        return span_ref[0, 0, index(b, i)] < my_block

    def pick(buf, b):
        e, both = [], []
        for i in range(NX):
            blk = buf[b, i]
            lo, hi = blk[:HALF], blk[HALF:]
            s = early(b, i)
            zero = jnp.zeros_like(lo)
            e.append(lo)
            both.append(jnp.concatenate([jnp.where(s, lo, zero), jnp.where(s, zero, hi)], axis=1))
        return jnp.concatenate(e, axis=0), jnp.concatenate(both, axis=0)

    def softmax_row(n):
        b = row_of(n)

        @pl.when(c == 1)
        def _():
            hand_over(vbuf, n).wait_recv()

        @pl.when(c == 0)
        def _():
            hand_over(kbuf, n).wait_recv()

        ke, ksel = pick(kbuf, b)
        kselbuf[b] = ksel
        s1[b] = dot_nt(ke, qq[:, HD:]) * scale
        s2[b] = dot_nt(ksel, qq[...]) * scale
        ve, vsel = pick(vbuf, b)
        dp1[b] = dot_nt(ve, oo[:, HD:])
        dp2[b] = dot_nt(vsel, oo[...])
        old_e, old_l = state[0:1], state[1:2]
        m_e, m_l = old_e, jnp.maximum(old_l, col_max(s1[b]))
        low = jnp.full((1, SLOTS), NEG, F32)
        high = jnp.full((1, SLOTS), POS, F32)
        for i in range(NX):
            top = col_max(s2[b, i * HALF:(i + 1) * HALF])
            s = early(b, i)
            top = jnp.where(index(b, i) == me, low, top)
            m_e = jnp.maximum(m_e, jnp.where(s, top, low))
            m_l = jnp.maximum(m_l, jnp.where(s, low, top))
        a_e = jnp.exp2(old_e - m_e)
        a_l = jnp.exp2(old_l - m_l)
        l_e, l_l = state[2:3] * a_e, state[3:4] * a_l
        d_e, d_l = state[4:5] * a_e, state[5:6] * a_l
        for i in range(NX):
            part = slice(i * HALF, (i + 1) * HALF)
            p = jnp.exp2(s1[b, part] - m_l)
            s1[b, part] = p
            l_l = l_l + col_sum(p)
            d_l = d_l + col_sum(p * dp1[b, part])
            s = early(b, i)
            top = jnp.where(s, m_e, m_l)
            top = jnp.where(index(b, i) == me, high, top)
            p = jnp.exp2(s2[b, part] - top)
            s2[b, part] = p
            ps = col_sum(p)
            pd = col_sum(p * dp2[b, part])
            zero = jnp.zeros_like(ps)
            l_e = l_e + jnp.where(s, ps, zero)
            l_l = l_l + jnp.where(s, zero, ps)
            d_e = d_e + jnp.where(s, pd, zero)
            d_l = d_l + jnp.where(s, zero, pd)
        for i, v in enumerate((m_e, m_l, l_e, l_l, d_e, d_l)):
            state[i:i + 1] = v
        tops[b, 0:1] = m_e
        tops[b, 1:2] = m_l

    def diagonal():
        key_no = lax.broadcasted_iota(jnp.int32, (HALF, SLOTS), 0)
        tok_no = lax.broadcasted_iota(jnp.int32, (HALF, SLOTS), 1) % HALF
        seen = key_no <= tok_no
        for j in range(2):
            part = slice(j * HALF, (j + 1) * HALF)
            cols = slice(j * HD, (j + 1) * HD)
            s = jnp.where(seen, dot_nt(k_ref[0, part], qq[:, cols]) * scale, NEG)
            top = col_max(s)
            p = jnp.exp2(s - top)
            dp = dot_nt(v_ref[0, part], oo[:, cols])
            diag[2 * j] = p
            diag[2 * j + 1] = dp
            state[j:j + 1] = top
            state[2 + j:3 + j] = col_sum(p)
            state[4 + j:5 + j] = col_sum(p * dp)
            tops[NZ, j:j + 1] = top

    def swap_sums(j):
        return remote(sums_out.at[j], sums_in.at[j], sent.at[5], sums_r.at[0], mate(j))

    LAG = 2
    plans = (
        {
            0: [(v_stage1, n) for n in range(5)],
            1: [(v_stage1, 5), (v_stage1, 6), (v_stage1, 7)] + [(v_stage2, n) for n in range(3)],
            3: [(v_stage2, 3), (v_stage2, 4)],
            5: [(v_stage2, 5), (v_stage2, 6), (v_stage2, 7)],
        },
        {
            0: [(gather_k, 0), (gather_k, 3), (gather_k, 4)],
            1: [(gather_k, 1), (gather_k, 2)],
            6: [(gather_k, 5), (gather_k, 6), (gather_k, 7)],
        },
    )

    def run_plan(i, plans):
        for core in range(2):
            for j, todo in plans[core].items():
                @pl.when((i == j) & (c == core))
                def _():
                    for stage, n in todo:
                        stage(n)

    def gather_step(i, _):
        run_plan(i, plans)

        @pl.when(i == LAG)
        def _():
            landed(pqr.at[0], 8)
            for kind in range(2):
                for j in range(2):
                    lay_rows((qq, oo)[kind], ROWS, (pq, pg)[kind].at[j], 0, j)

            @pl.when(c == half)
            def _():
                diagonal()

        @pl.when(i >= LAG)
        def _():
            softmax_row(i - LAG)

        return 0

    lax.fori_loop(0, NZ + LAG, gather_step, 0)

    for j in range(2):
        for i in range(3):
            sums_out[j, i:i + 1] = state[2 * i + j:2 * i + j + 1]
        swap_sums(j).start()
    landed(sums_r.at[0])
    for j in range(2):
        m, l, d = (state[2 * i + j:2 * i + j + 1] for i in range(3))
        m2, l2, d2 = (
            jnp.concatenate([sums_in[j, i:i + 1, ROWS:], sums_in[j, i:i + 1, :ROWS]], axis=1)
            for i in range(3)
        )
        top = jnp.maximum(m, m2)
        a, a2 = jnp.exp2(m - top), jnp.exp2(m2 - top)
        r = 1.0 / (l * a + l2 * a2)
        state[j:j + 1] = top
        state[2 + j:3 + j] = r
        state[4 + j:5 + j] = (d * a + d2 * a2) * r

    @pl.when(c == half)
    def _():
        for j in range(2):
            part = slice(j * HALF, (j + 1) * HALF)
            cols = slice(j * HD, (j + 1) * HD)
            m, r, d = state[j:j + 1], state[2 + j:3 + j], state[4 + j:5 + j]
            p = diag[2 * j] * (jnp.exp2(tops[NZ, j:j + 1] - m) * r)
            ds = (p * (diag[2 * j + 1] - d)).astype(BF16)
            dq2[cols] = dot_tn(k_ref[0, part], ds)
            diag[2 * j, :, :HD] = dot_nn(ds, qq[:, cols]) * INV_ROOT
            diag[2 * j, :, HD:2 * HD] = dot_nn(p.astype(BF16), oo[:, cols])

    def give(buf, m):
        b = row_of(NZ - 1 - m)
        return remote(buf.at[b], sib.at[b], sent.at[6], sibr.at[m], sibling)

    def gradient_row(m):
        b = row_of(NZ - 1 - m)
        r_e, r_l, d_e, d_l = state[2:3], state[3:4], state[4:5], state[5:6]
        f_e = jnp.exp2(tops[b, 0:1] - state[0:1]) * r_e
        f_l = jnp.exp2(tops[b, 1:2] - state[1:2]) * r_l
        ke = jnp.concatenate([kbuf[b, i, :HALF] for i in range(NX)], axis=0)
        ksel = kselbuf[b]
        p1 = s1[b] * f_l
        ds1 = (p1 * (dp1[b] - d_l)).astype(BF16)
        p1 = p1.astype(BF16)
        p2s, ds2s = [], []
        for i in range(NX):
            part = slice(i * HALF, (i + 1) * HALF)
            s = early(b, i)
            p = s2[b, part] * jnp.where(s, f_e, f_l)
            ds2s.append((p * (dp2[b, part] - jnp.where(s, d_e, d_l))).astype(BF16))
            p2s.append(p.astype(BF16))
        p2 = jnp.concatenate(p2s, axis=0)
        ds2 = jnp.concatenate(ds2s, axis=0)
        v1 = dot_nn(p1, oo[:, HD:])
        v2 = dot_nn(p2, oo[...])
        k1 = dot_nn(ds1, qq[:, HD:]) * INV_ROOT
        k2 = dot_nn(ds2, qq[...]) * INV_ROOT
        dql[...] += dot_tn(ke, ds1)
        dq2[...] += dot_tn(ksel, ds2)
        for i in range(NX):
            part = slice(i * HALF, (i + 1) * HALF)
            s = early(b, i)
            zero = jnp.zeros((HALF, HD), F32)
            cell = (b, i)
            lo, hi = slice(0, HALF), slice(HALF, 2 * HALF)
            pv[(*cell, lo)] = (v1[part] + jnp.where(s, v2[part, :HD], zero)).astype(BF16)
            pv[(*cell, hi)] = jnp.where(s, zero, v2[part, HD:]).astype(BF16)
            pk[(*cell, lo)] = (k1[part] + jnp.where(s, k2[part, :HD], zero)).astype(BF16)
            pk[(*cell, hi)] = jnp.where(s, zero, k2[part, HD:]).astype(BF16)

        @pl.when((m == NZ - 1) & (c == half))
        def _():
            for j in range(2):
                part = slice(j * HALF, (j + 1) * HALF)
                pk[z, x, part] = (pk[z, x, part].astype(F32) + diag[2 * j, :, :HD]).astype(BF16)
                pv[z, x, part] = (pv[z, x, part].astype(F32) + diag[2 * j, :, HD:2 * HD]).astype(BF16)

        @pl.when(c == 1)
        def _():
            give(pv, m).start()

        @pl.when(c == 0)
        def _():
            give(pk, m).start()

    def add_into(dst, idx, *terms):
        total = dst[idx].astype(F32)
        for ref, i in terms:
            total = total + ref[i].astype(F32)
        dst[idx] = total.astype(BF16)

    def k_back(way, k, j):
        step = 1 if way == 0 else -1
        far = (1, 2, 1, 2)[k - 1]
        return remote(pk.at[zoff(step * k), xoff(j)], rr.at[way, k - 1, j],
                      sent.at[7], rrsem.at[8 + j if k < 3 else way * 4 + j], at(zoff(step * far), x, 1))

    def k_across(j):
        return remote(pk.at[z, xoff(j)], xr.at[j], sent.at[10], xrsem.at[0], at(z, xoff(j), 1))

    def k_hop(m):
        give(pk, m).wait_recv()
        d = ORDER[NZ - 1 - m]
        k = abs(d)
        if k == 4:
            plan = [(w, j, ()) for i in range(2) for w, j in ((0, SETS[0][i]), (1, SETS[1][i]))]
        else:
            w = 0 if d > 0 else 1
            if k == 3:
                plan = [(w, j, ()) for j in ACROSS]
            elif k == 2:
                plan = [(w, j, (3, 4) if j in SETS[w] else (3,)) for j in SETS[1 - w] + SETS[w]]
            else:
                plan = [(w, j, ()) for j in ACROSS]
        for w, j, has in plan:
            cell = (zoff(d), xoff(j))
            terms = [(sib, cell)]
            if has:
                landed(rrsem.at[w * 4 + j], len(has))
            for q in has:
                terms.append((rr, (w, q - 1, j)))
            add_into(pk, cell, *terms)
            k_back(w, k, j).start()

    def k_last():
        give(pk, NZ - 1).wait_recv()
        for j in (2, 1, 3, 0):
            landed(rrsem.at[8 + j], 4)
            cell = (z, xoff(j))
            terms = [(sib, cell)]
            for w in range(2):
                for k in (1, 2):
                    terms.append((rr, (w, k - 1, j)))
            add_into(pk, cell, *terms)
            if j:
                k_across(j).start()
        total = pk[z, x].astype(F32)
        landed(xrsem.at[0], NX - 1)
        for j in range(1, NX):
            total = total + xr[j].astype(F32)
        ysum[...] = total.astype(BF16)

    def v_back(d, m):
        return remote(pv.at[zoff(ORDER[NZ - 1 - m]), xoff(d)], cx.at[d * NZ + m], sent.at[8],
                      c1r.at[m], at(z, xoff(d), 0))

    def v_z(m):
        d = ORDER[NZ - 1 - m]
        return remote(pv.at[zoff(d), x], zr.at[m], sent.at[9], zrsem.at[0], at(zoff(d), x, 0))

    def v_out(m):
        give(pv, m).wait_recv()
        for d in (2, 1, 3):
            cell = (zoff(ORDER[NZ - 1 - m]), xoff(d))
            add_into(pv, cell, (sib, cell))
            v_back(d, m).start()

    def v_in(m):
        cell = (zoff(ORDER[NZ - 1 - m]), x)
        terms = [(sib, cell)]
        landed(c1r.at[m], NX - 1)
        for d in range(1, NX):
            terms.append((cx, d * NZ + m))
        add_into(pv, cell, *terms)
        if m < NZ - 1:
            v_z(m).start()

    def v_last():
        total = pv[z, x].astype(F32)
        landed(zrsem.at[0], NZ - 1)
        for m in range(NZ - 1):
            total = total + zr[m].astype(F32)
        ysum[...] = total.astype(BF16)

    back = (
        {m: [(v_out, m - 2)] + ([(v_in, m - 6)] if m >= 6 else []) for m in range(2, NZ)},
        {2: [(k_hop, 0)], 3: [(k_hop, 1)], 4: [(k_hop, 2)]},
    )

    def drain_scatter():
        @pl.when(c == 1)
        def _():
            landed(sent.at[7], 28)
            landed(sent.at[10], 3)

        @pl.when(c == 0)
        def _():
            landed(sent.at[8], 24)
            landed(sent.at[9], 7)

        landed(sent.at[6], 32)

    def scatter_step(m, _):
        gradient_row(m)
        run_plan(m, back)
        return 0

    lax.fori_loop(0, NZ, scatter_step, 0)

    @pl.when(c == 0)
    def _():
        v_out(6)
        v_out(7)
        for m in range(2, 5):
            v_in(m)

    @pl.when(c == 1)
    def _():
        for m in range(3, NZ - 1):
            k_hop(m)

    for j, acc in enumerate((dq2[0:HD], dq2[HD:2 * HD] + dql[...])):
        g = (acc * INV_ROOT).T.astype(BF16)
        for i in range(2):
            for h in range(HEADS):
                at_row = i * ROWS + h * HALF
                dqst[i, j * HALF:(j + 1) * HALF, h * HD:(h + 1) * HD] = g[at_row:at_row + HALF]

    def dq_copy(i):
        if i == 0:
            return remote(dqst.at[0], dqr.at[0], sent.at[12], dqsr.at[0], other(t, c))
        part = pl.ds((i - 1) * HALF, HALF)
        return remote(dqst.at[1, part], dqr.at[1, part], sent.at[12], dqsr.at[0],
                      other(mates[i - 1], c))

    for i in range(3):
        dq_copy(i).start()

    @pl.when(c == 1)
    def _():
        k_last()

    @pl.when(c == 0)
    def _():
        for m in range(5, NZ):
            v_in(m)
        v_last()

    def last(tt):
        return remote(ysum, yr.at[1 - c, t // 2], sent.at[11], yrsem.at[0],
                      other(tt, half))

    for tt in range(NT):
        last(tt).start()

    drain_gather()
    drain_scatter()

    landed(dqsr.at[0], 8)
    dq_out[0] = (dqr[0].astype(F32) + dqr[1].astype(F32)).astype(BF16)
    landed(yrsem.at[0], 4)
    for kind, out in ((0, dk_out), (1, dv_out)):
        out[0] = (yr[kind, 0].astype(F32) + yr[kind, 1].astype(F32)).astype(BF16)
    landed(sent.at[11], 4)
    landed(sent.at[12], 8)


def per_device(queries, keys, values, grad_out, span_order):
    vmem = pl.BlockSpec(memory_space=pltpu.VMEM)
    hbm = pl.BlockSpec(memory_space=pl.ANY)
    dma = pltpu.SemaphoreType.DMA

    def plane():
        return pltpu.VMEM((NZ, NX, 128, HD), BF16)

    scratch = [
        pltpu.VMEM(queries.shape, BF16),
        pltpu.VMEM(keys.shape, BF16),
        pltpu.VMEM(values.shape, BF16),
        pltpu.VMEM(grad_out.shape, BF16),
        plane(),
        plane(),
        pltpu.VMEM((NZ, KEYS, SLOTS), F32),
        pltpu.VMEM((NZ, KEYS, SLOTS), F32),
        pltpu.VMEM((NZ, KEYS, SLOTS), F32),
        pltpu.VMEM((NZ, KEYS, SLOTS), F32),
        pltpu.VMEM((NZ, KEYS, 2 * HD), BF16),
        pltpu.VMEM((SLOTS, 2 * HD), BF16),
        pltpu.VMEM((SLOTS, 2 * HD), BF16),
        pltpu.VMEM((2, HALF, HEADS * HD), BF16),
        pltpu.VMEM((2, HALF, HEADS * HD), BF16),
        pltpu.VMEM((HD, SLOTS), F32),
        pltpu.VMEM((2 * HD, SLOTS), F32),
        pltpu.VMEM((2, 128, HEADS * HD), BF16),
        pltpu.VMEM((2, 128, HEADS * HD), BF16),
        pltpu.VMEM((8, SLOTS), F32),
        pltpu.VMEM((NZ + 1, 8, SLOTS), F32),
        pltpu.VMEM((4, HALF, SLOTS), F32),
        pltpu.VMEM((2, 8, SLOTS), F32),
        pltpu.VMEM((2, 8, SLOTS), F32),
        plane(),
        plane(),
        plane(),
        pltpu.VMEM((2, 4, NX, 128, HD), BF16),
        pltpu.VMEM((NX * NZ, 128, HD), BF16),
        pltpu.VMEM((NZ, 128, HD), BF16),
        pltpu.VMEM((NX, 128, HD), BF16),
        pltpu.VMEM((128, HD), BF16),
        pltpu.VMEM((2, 2, 128, HD), BF16),
        dma((2,)), dma((13,)),
        dma((NX,)), dma((NZ,)), dma((13,)), dma((NZ,)), dma((NZ,)),
        dma((1,)), dma((1,)),
        dma((NZ,)), dma((12,)), dma((NZ,)), dma((1,)), dma((1,)),
        dma((1,)), dma((1,)),
    ]
    return pl.pallas_call(
        kernel,
        out_shape=(
            jax.ShapeDtypeStruct(queries.shape, BF16),
            jax.ShapeDtypeStruct(keys.shape, BF16),
            jax.ShapeDtypeStruct(values.shape, BF16),
        ),
        in_specs=[hbm, hbm, hbm, hbm, pl.BlockSpec(memory_space=pltpu.SMEM)],
        out_specs=(vmem, vmem, vmem),
        scratch_shapes=scratch,
        compiler_params=pltpu.CompilerParams(
            collective_id=1, has_side_effects=True, vmem_limit_bytes=56 * 2**20
        ),
        name="attention_backward",
    )(queries, keys, values, grad_out, jnp.swapaxes(span_order, 1, 2))


def solution(mesh):
    return jax.shard_map(
        per_device,
        mesh=mesh,
        in_specs=(
            P("pipe", "ctx", "tp"),
            P("pipe", "ctx", None),
            P("pipe", "ctx", None),
            P("pipe", "ctx", "tp"),
            P("pipe", None, None),
        ),
        out_specs=(P("pipe", "ctx", "tp"), P("pipe", "ctx", None), P("pipe", "ctx", None)),
        check_vma=False,
    )
```

```python
import functools

import jax
import jax.numpy as jnp
from jax import lax
from jax.experimental import pallas as pl
from jax.experimental.pallas import tpu as pltpu
from jax.sharding import PartitionSpec as P

MESH = pl.DeviceIdType.MESH
F32 = jnp.float32
BF16 = jnp.bfloat16

NZ = 8
NX = 4
NT = 4
HEADS = 4
HALF = 64
HD = 128
ROWS = HEADS * HALF
SLOTS = 2 * ROWS
KEYS = NX * HALF
BLOCK = 256
SPLIT = 112
REST = BLOCK - SPLIT
FIRST = pl.ds(0, SPLIT)
SECOND = pl.ds(SPLIT, REST)
INV_ROOT = HD ** (-0.5)
LOG2E = 1.4426950408889634
NEG = -1e30
POS = 1e30
ORDER = (0, 1, -1, 2, -2, 3, -3, 4)
BACK = (4, -3, 3, -1, 1, -2, 2, 0)
ACROSS = (0, 1, 3, 2)
SETS = ((0, 1), (3, 2))


def dot_nt(a, b):
    return lax.dot_general(a, b, (((1,), (1,)), ((), ())), preferred_element_type=F32)


def dot_nn(a, b):
    return jnp.dot(a, b, preferred_element_type=F32)


def dot_tn(a, b):
    return lax.dot_general(a, b, (((0,), (0,)), ((), ())), preferred_element_type=F32)


def col_sum(v):
    return jnp.sum(v, axis=0, keepdims=True)


def col_max(v):
    return jnp.max(v, axis=0, keepdims=True)


def kernel(
    q_hbm, k_hbm, v_hbm, g_hbm, span_ref,
    dq_out, dk_out, dv_out,
    q_ref, k_ref, v_ref, g_ref, kv, s1, s2, dp1, dp2, kselbuf, qq, oo, pq, pg, dql, dq2, dqst, dqr,
    state, tops, diag, sums_out, sums_in,
    pkv, sib, rr, cx, zr, xr, ysum, yr,
    insem, sent, p1kr, p1vr, zkr, x1r, d2dr, pqr, sums_r, sibr, rrsem, c1r, zrsem, xrsem,
    yrsem, dqsr,
):
    pipe = lax.axis_index("pipe")
    me = lax.axis_index("ctx")
    t = lax.axis_index("tp")
    z = me // (2 * NX)
    x = (me // 2) % NX
    c = me % 2
    half = t % 2
    mates = (t + 1 - 2 * half, lax.rem(t + 2 * half + NT - 1, NT))

    def at(zz, xx, cc):
        return (pipe, (zz * NX + xx) * 2 + cc, t)

    def zoff(d):
        return lax.rem(z + d + NZ, NZ)

    def xoff(d):
        return lax.rem(x + d + NX, NX)

    def row_of(n):
        return zoff(((n + 1) // 2) * (2 * (n % 2) - 1))

    def mate(j):
        return (pipe, me, mates[j])

    def back_row(m):
        d = 0
        for i, far in enumerate(BACK):
            d = jnp.where(m == i, far, d)
        return zoff(d)

    def other(tt, cc):
        return (1 - pipe, (z * NX + x) * 2 + cc, tt)

    sibling = at(z, x, 1 - c)

    def remote(src, dst, ssem, rsem, dev):
        return pltpu.make_async_remote_copy(
            src_ref=src, dst_ref=dst, send_sem=ssem, recv_sem=rsem,
            device_id=dev, device_id_type=MESH,
        )

    def take(i):
        src = (q_hbm, g_hbm, k_hbm, v_hbm)[i]
        return pltpu.make_async_copy(src, (q_ref, g_ref, k_ref, v_ref)[i], insem.at[0])

    for i in range(4):
        take(i).start()

    barrier = pltpu.get_barrier_semaphore()
    count = 0

    def greet(dev):
        pl.semaphore_signal(barrier, inc=1, device_id=dev, device_id_type=MESH)

    greet(sibling)
    count += 1
    for cc in range(2):
        for d in range(1, NX):
            greet(at(z, xoff(d), cc))
            count += 1
        for d in range(1, NZ):
            greet(at(zoff(d), x, cc))
            count += 1
        for tt in range(NT):
            greet(other(tt, cc))
            count += 1
    for j in range(2):
        greet(mate(j))
        count += 1

    def lay_rows(dst, base, src, lo, j):
        for h in range(HEADS):
            dst[base + h * HALF:base + (h + 1) * HALF, j * HD:(j + 1) * HD] = src[
                lo:lo + HALF, h * HD:(h + 1) * HD]

    low = jnp.full((1, SLOTS), NEG, F32)
    state[...] = jnp.zeros_like(state)
    sums_out[...] = jnp.zeros_like(sums_out)
    for j in range(2):
        state[j:j + 1] = low
    dql[...] = jnp.zeros_like(dql)
    dq2[...] = jnp.zeros_like(dq2)
    scale = INV_ROOT * LOG2E

    pl.semaphore_wait(barrier, count)

    def swap_rows(j, kind):
        src = (q_hbm, g_hbm)[kind].at[0, pl.ds(j * HALF, HALF)]
        dst = (pq, pg)[kind].at[j]
        return remote(src, dst, sent.at[4], pqr.at[0], mate(j))

    for kind in range(2):
        for j in range(2):
            swap_rows(j, kind).start()

    def first_k(d):
        return remote(k_hbm.at[0, FIRST], kv.at[z, x, FIRST], sent.at[0], p1kr.at[d],
                      at(z, xoff(d), 1))

    def first_v(d):
        there = at(zoff(d), x, 0)
        keys = remote(k_hbm.at[0, pl.ds(SPLIT, 128 - SPLIT)], kv.at[z, x, pl.ds(SPLIT, 128 - SPLIT)],
                      sent.at[0], p1vr.at[d], there)
        values = remote(v_hbm.at[0], kv.at[z, x, pl.ds(128, 128)], sent.at[0], p1vr.at[d], there)
        return keys, values

    def k_slot(way, k, j):
        return {1: way, 2: 5 + way * 4 + j, 3: 2 + way, 4: 4}[k]

    def k_send(way, k, j):
        step = 1 if way == 0 else -1
        back, far = ((0, 1), (0, 2), (2, 1), (2, 2))[k - 1]
        ref = kv.at[zoff(-step * back), xoff(j), FIRST]
        return remote(ref, ref, sent.at[1], zkr.at[k_slot(way, k, j)],
                      at(zoff(step * far), x, 1))

    def v_x(d, n):
        ref = kv.at[zoff(ORDER[n]), x, SECOND]
        return remote(ref, ref, sent.at[2], x1r.at[n], at(z, xoff(d), 0))

    def hand_over(part, n):
        ref = kv.at[row_of(n), :, part]
        return remote(ref, ref, sent.at[3], d2dr.at[n], sibling)

    def landed(sem, rows):
        ref = cx.at[pl.ds(0, rows)]
        pltpu.make_async_copy(ref, ref, sem).wait()

    def gather_k(n):
        d = ORDER[n]
        k = abs(d)
        if k == 0:
            for j in ACROSS:
                src = (NX - j) % NX
                if src:
                    landed(p1kr.at[src], SPLIT)
                else:
                    @pl.when(half == 0)
                    def _():
                        landed(p1kr.at[0], SPLIT)
                for w in range(2):
                    k_send(w, 2, j).start()
                    k_send(w, 1, j).start()
        elif k == 2:
            w = 1 if d > 0 else 0
            for j in ACROSS:
                landed(zkr.at[k_slot(w, 2, j)], SPLIT)
                if j in SETS[w]:
                    k_send(w, 4, j).start()
                k_send(w, 3, j).start()
        else:
            landed(zkr.at[k_slot(1 if d > 0 else 0, k, 0)], NX * SPLIT)
        hand_over(FIRST, n).start()

    def v_stage1(n):
        d = ORDER[n]
        if d:
            landed(p1vr.at[-d % NZ], REST)
        else:
            @pl.when(half == 1)
            def _():
                landed(p1vr.at[0], REST)
        for dx in (1, 3, 2):
            v_x(dx, n).start()

    def v_stage2(n):
        landed(x1r.at[n], (NX - 1) * REST)
        hand_over(SECOND, n).start()

    def keep(i):
        part = pl.ds(0, SPLIT) if i == 0 else pl.ds(SPLIT, 128 - SPLIT)
        if i == 2:
            src, dst = v_hbm.at[0], kv.at[z, x, pl.ds(128, 128)]
        else:
            src, dst = k_hbm.at[0, part], kv.at[z, x, part]
        return pltpu.make_async_copy(src, dst, insem.at[1])

    @pl.when(c == half)
    def _():
        for d in (1, 3, 2):
            first_k(d).start()

        @pl.when(c == 0)
        def _():
            first_k(0).start()
            keep(1).start()
            keep(2).start()

        @pl.when(c == 1)
        def _():
            for cp in first_v(0):
                cp.start()
            keep(0).start()

        for d in (1, 7, 2, 6, 3, 5, 4):
            for cp in first_v(d):
                cp.start()

        @pl.when(c == 0)
        def _():
            landed(insem.at[1], REST)

        @pl.when(c == 1)
        def _():
            landed(insem.at[1], SPLIT)

    landed(insem.at[0], 10 * 128)
    for j in range(2):
        lay_rows(qq, 0, q_ref.at[0], j * HALF, j)
        lay_rows(oo, 0, g_ref.at[0], j * HALF, j)

    def drain_gather():
        @pl.when(c == 1)
        def _():
            landed(sent.at[1], 28 * SPLIT)
            landed(sent.at[3], NZ * NX * SPLIT)

        @pl.when(c == 0)
        def _():
            landed(sent.at[2], NZ * (NX - 1) * REST)
            landed(sent.at[3], NZ * NX * REST)

        @pl.when((c == half) & (c == 0))
        def _():
            landed(sent.at[0], NX * SPLIT + (NZ - 1) * REST)

        @pl.when((c == half) & (c == 1))
        def _():
            landed(sent.at[0], (NX - 1) * SPLIT + NZ * REST)

        landed(sent.at[4], 8 * 128)
        landed(sent.at[5], 128)

    my_block = span_ref[0, 0, me]

    def index(b, i):
        return (b * NX + i) * 2 + half

    def early(b, i):
        return span_ref[0, 0, index(b, i)] < my_block

    def pick(at_row, b):
        e, both = [], []
        for i in range(NX):
            lo = kv[b, i, at_row:at_row + HALF]
            hi = kv[b, i, at_row + HALF:at_row + 2 * HALF]
            s = early(b, i)
            zero = jnp.zeros_like(lo)
            e.append(lo)
            both.append(jnp.concatenate([jnp.where(s, lo, zero), jnp.where(s, zero, hi)], axis=1))
        return jnp.concatenate(e, axis=0), jnp.concatenate(both, axis=0)

    def softmax_row(n):
        b = row_of(n)

        @pl.when(c == 1)
        def _():
            hand_over(SECOND, n).wait_recv()

        @pl.when(c == 0)
        def _():
            hand_over(FIRST, n).wait_recv()

        ke, ksel = pick(0, b)
        kselbuf[b] = ksel
        s1[b] = dot_nt(ke, qq[:, HD:]) * scale
        s2[b] = dot_nt(ksel, qq[...]) * scale
        ve, vsel = pick(128, b)
        dp1[b] = dot_nt(ve, oo[:, HD:])
        dp2[b] = dot_nt(vsel, oo[...])
        old_e, old_l = state[0:1], state[1:2]
        m_e, m_l = old_e, jnp.maximum(old_l, col_max(s1[b]))
        low = jnp.full((1, SLOTS), NEG, F32)
        high = jnp.full((1, SLOTS), POS, F32)
        for i in range(NX):
            top = col_max(s2[b, i * HALF:(i + 1) * HALF])
            s = early(b, i)
            top = jnp.where(index(b, i) == me, low, top)
            m_e = jnp.maximum(m_e, jnp.where(s, top, low))
            m_l = jnp.maximum(m_l, jnp.where(s, low, top))
        a_e = jnp.exp2(old_e - m_e)
        a_l = jnp.exp2(old_l - m_l)
        l_e, l_l = state[2:3] * a_e, state[3:4] * a_l
        d_e, d_l = state[4:5] * a_e, state[5:6] * a_l
        for i in range(NX):
            part = slice(i * HALF, (i + 1) * HALF)
            p = jnp.exp2(s1[b, part] - m_l)
            s1[b, part] = p
            l_l = l_l + col_sum(p)
            d_l = d_l + col_sum(p * dp1[b, part])
            s = early(b, i)
            top = jnp.where(s, m_e, m_l)
            top = jnp.where(index(b, i) == me, high, top)
            p = jnp.exp2(s2[b, part] - top)
            s2[b, part] = p
            ps = col_sum(p)
            pd = col_sum(p * dp2[b, part])
            zero = jnp.zeros_like(ps)
            l_e = l_e + jnp.where(s, ps, zero)
            l_l = l_l + jnp.where(s, zero, ps)
            d_e = d_e + jnp.where(s, pd, zero)
            d_l = d_l + jnp.where(s, zero, pd)
        for i, v in enumerate((m_e, m_l, l_e, l_l, d_e, d_l)):
            state[i:i + 1] = v
        tops[b, 0:1] = m_e
        tops[b, 1:2] = m_l

    def diagonal():
        key_no = lax.broadcasted_iota(jnp.int32, (HALF, SLOTS), 0)
        tok_no = lax.broadcasted_iota(jnp.int32, (HALF, SLOTS), 1) % HALF
        seen = key_no <= tok_no
        for j in range(2):
            part = slice(j * HALF, (j + 1) * HALF)
            cols = slice(j * HD, (j + 1) * HD)
            s = jnp.where(seen, dot_nt(k_ref[0, part], qq[:, cols]) * scale, NEG)
            top = col_max(s)
            p = jnp.exp2(s - top)
            dp = dot_nt(v_ref[0, part], oo[:, cols])
            diag[2 * j] = p
            diag[2 * j + 1] = dp
            state[j:j + 1] = top
            state[2 + j:3 + j] = col_sum(p)
            state[4 + j:5 + j] = col_sum(p * dp)
            tops[NZ, j:j + 1] = top

    def swap_sums(j):
        return remote(sums_out.at[j], sums_in.at[j], sent.at[5], sums_r.at[0], mate(j))

    LAG = 2
    plans = (
        {
            0: [(v_stage1, n) for n in range(5)],
            1: [(v_stage1, 5), (v_stage1, 6), (v_stage1, 7)] + [(v_stage2, n) for n in range(3)],
            3: [(v_stage2, 3), (v_stage2, 4)],
            5: [(v_stage2, 5), (v_stage2, 6), (v_stage2, 7)],
        },
        {
            0: [(gather_k, 0), (gather_k, 3), (gather_k, 4)],
            1: [(gather_k, 1), (gather_k, 2)],
            6: [(gather_k, 5), (gather_k, 6), (gather_k, 7)],
        },
    )

    def run_plan(i, plans):
        for core in range(2):
            for j, todo in plans[core].items():
                @pl.when((i == j) & (c == core))
                def _():
                    for stage, n in todo:
                        stage(n)

    def gather_step(i, _):
        run_plan(i, plans)

        @pl.when(i == LAG)
        def _():
            landed(pqr.at[0], 8 * 128)
            for kind in range(2):
                for j in range(2):
                    lay_rows((qq, oo)[kind], ROWS, (pq, pg)[kind].at[j], 0, j)

            @pl.when(c == half)
            def _():
                diagonal()

        @pl.when(i >= LAG)
        def _():
            softmax_row(i - LAG)

        return 0

    lax.fori_loop(0, NZ + LAG, gather_step, 0)

    for j in range(2):
        for i in range(3):
            sums_out[j, i:i + 1] = state[2 * i + j:2 * i + j + 1]
        swap_sums(j).start()
    landed(sums_r.at[0], 128)
    for j in range(2):
        m, l, d = (state[2 * i + j:2 * i + j + 1] for i in range(3))
        m2, l2, d2 = (
            jnp.concatenate([sums_in[j, i:i + 1, ROWS:], sums_in[j, i:i + 1, :ROWS]], axis=1)
            for i in range(3)
        )
        top = jnp.maximum(m, m2)
        a, a2 = jnp.exp2(m - top), jnp.exp2(m2 - top)
        r = 1.0 / (l * a + l2 * a2)
        state[j:j + 1] = top
        state[2 + j:3 + j] = r
        state[4 + j:5 + j] = (d * a + d2 * a2) * r

    @pl.when(c == half)
    def _():
        for j in range(2):
            part = slice(j * HALF, (j + 1) * HALF)
            cols = slice(j * HD, (j + 1) * HD)
            m, r, d = state[j:j + 1], state[2 + j:3 + j], state[4 + j:5 + j]
            p = diag[2 * j] * (jnp.exp2(tops[NZ, j:j + 1] - m) * r)
            ds = (p * (diag[2 * j + 1] - d)).astype(BF16)
            dq2[cols] = dot_tn(k_ref[0, part], ds)
            diag[2 * j, :, :HD] = dot_nn(ds, qq[:, cols]) * INV_ROOT
            diag[2 * j, :, HD:2 * HD] = dot_nn(p.astype(BF16), oo[:, cols])

    def give(part, m):
        b = back_row(m)
        return remote(pkv.at[b, :, part], sib.at[b, :, part], sent.at[6], sibr.at[m], sibling)

    def gradient_row(m):
        b = back_row(m)
        r_e, r_l, d_e, d_l = state[2:3], state[3:4], state[4:5], state[5:6]
        f_e = jnp.exp2(tops[b, 0:1] - state[0:1]) * r_e
        f_l = jnp.exp2(tops[b, 1:2] - state[1:2]) * r_l
        ke = jnp.concatenate([kv[b, i, :HALF] for i in range(NX)], axis=0)
        ksel = kselbuf[b]
        p1 = s1[b] * f_l
        ds1 = (p1 * (dp1[b] - d_l)).astype(BF16)
        p1 = p1.astype(BF16)
        p2s, ds2s = [], []
        for i in range(NX):
            part = slice(i * HALF, (i + 1) * HALF)
            s = early(b, i)
            p = s2[b, part] * jnp.where(s, f_e, f_l)
            ds2s.append((p * (dp2[b, part] - jnp.where(s, d_e, d_l))).astype(BF16))
            p2s.append(p.astype(BF16))
        p2 = jnp.concatenate(p2s, axis=0)
        ds2 = jnp.concatenate(ds2s, axis=0)
        v1 = dot_nn(p1, oo[:, HD:])
        v2 = dot_nn(p2, oo[...])
        k1 = dot_nn(ds1, qq[:, HD:]) * INV_ROOT
        k2 = dot_nn(ds2, qq[...]) * INV_ROOT
        dql[...] += dot_tn(ke, ds1)
        dq2[...] += dot_tn(ksel, ds2)
        for i in range(NX):
            part = slice(i * HALF, (i + 1) * HALF)
            s = early(b, i)
            zero = jnp.zeros((HALF, HD), F32)
            k_lo, k_hi, v_lo, v_hi = (slice(j * HALF, (j + 1) * HALF) for j in range(4))
            pkv[b, i, v_lo] = (v1[part] + jnp.where(s, v2[part, :HD], zero)).astype(BF16)
            pkv[b, i, v_hi] = jnp.where(s, zero, v2[part, HD:]).astype(BF16)
            pkv[b, i, k_lo] = (k1[part] + jnp.where(s, k2[part, :HD], zero)).astype(BF16)
            pkv[b, i, k_hi] = jnp.where(s, zero, k2[part, HD:]).astype(BF16)

        @pl.when((m == NZ - 1) & (c == half))
        def _():
            for j in range(2):
                part = slice(j * HALF, (j + 1) * HALF)
                v_part = slice(128 + j * HALF, 128 + (j + 1) * HALF)
                pkv[z, x, part] = (
                    pkv[z, x, part].astype(F32) + diag[2 * j, :, :HD]).astype(BF16)
                pkv[z, x, v_part] = (
                    pkv[z, x, v_part].astype(F32) + diag[2 * j, :, HD:2 * HD]).astype(BF16)

        @pl.when(c == 1)
        def _():
            give(SECOND, m).start()

        @pl.when(c == 0)
        def _():
            give(FIRST, m).start()

    def add_up(row, col, part, *terms):
        total = pkv[row, col, part].astype(F32) + sib[row, col, part].astype(F32)
        for ref, i in terms:
            total = total + ref[i].astype(F32)
        return total

    def k_back(way, k, j):
        step = 1 if way == 0 else -1
        far = (1, 2, 1, 2)[k - 1]
        return remote(pkv.at[zoff(step * k), xoff(j), FIRST], rr.at[way, k - 1, j],
                      sent.at[7], rrsem.at[8 + j if k < 3 else way * 4 + j], at(zoff(step * far), x, 1))

    def k_across(j):
        return remote(pkv.at[z, xoff(j), FIRST], xr.at[j], sent.at[10], xrsem.at[0], at(z, xoff(j), 1))

    def k_hop(m):
        give(FIRST, m).wait_recv()
        d = BACK[m]
        k = abs(d)
        if k == 4:
            plan = [(w, j, ()) for i in range(2) for w, j in ((0, SETS[0][i]), (1, SETS[1][i]))]
        else:
            w = 0 if d > 0 else 1
            if k == 3:
                plan = [(w, j, ()) for j in ACROSS]
            elif k == 2:
                plan = [(w, j, (3, 4) if j in SETS[w] else (3,)) for j in SETS[1 - w] + SETS[w]]
            else:
                plan = [(w, j, ()) for j in ACROSS]
        for w, j, has in plan:
            row, col = zoff(d), xoff(j)
            terms = []
            if has:
                landed(rrsem.at[w * 4 + j], len(has) * SPLIT)
            for q in has:
                terms.append((rr, (w, q - 1, j)))
            pkv[row, col, FIRST] = add_up(row, col, FIRST, *terms).astype(BF16)
            k_back(w, k, j).start()

    def k_last():
        give(FIRST, NZ - 1).wait_recv()
        for j in (2, 1, 3, 0):
            landed(rrsem.at[8 + j], 4 * SPLIT)
            terms = []
            for w in range(2):
                for k in (1, 2):
                    terms.append((rr, (w, k - 1, j)))
            total = add_up(z, xoff(j), FIRST, *terms)
            if j:
                pkv[z, xoff(j), FIRST] = total.astype(BF16)
                k_across(j).start()
        landed(xrsem.at[0], (NX - 1) * SPLIT)
        for j in range(1, NX):
            total = total + xr[j].astype(F32)
        ysum[FIRST] = total.astype(BF16)

    def cx_part(d, m):
        return pl.ds((d * NZ + m) * REST, REST)

    def v_back(d, m):
        return remote(pkv.at[zoff(BACK[m]), xoff(d), SECOND], cx.at[cx_part(d, m)], sent.at[8],
                      c1r.at[m], at(z, xoff(d), 0))

    def v_z(m):
        d = BACK[m]
        return remote(pkv.at[zoff(d), x, SECOND], zr.at[m], sent.at[9], zrsem.at[0], at(zoff(d), x, 0))

    def v_out(m):
        give(SECOND, m).wait_recv()
        for d in (2, 1, 3):
            row, col = zoff(BACK[m]), xoff(d)
            pkv[row, col, SECOND] = add_up(row, col, SECOND).astype(BF16)
            v_back(d, m).start()

    def v_in(m):
        row = zoff(BACK[m])
        landed(c1r.at[m], (NX - 1) * REST)
        terms = [(cx, cx_part(d, m)) for d in range(1, NX)]
        pkv[row, x, SECOND] = add_up(row, x, SECOND, *terms).astype(BF16)
        if m < NZ - 1:
            v_z(m).start()

    def v_last():
        total = pkv[z, x, SECOND].astype(F32)
        landed(zrsem.at[0], (NZ - 1) * REST)
        for m in range(NZ - 1):
            total = total + zr[m].astype(F32)
        ysum[SECOND] = total.astype(BF16)

    back = (
        {m: [(v_out, m - 2)] + ([(v_in, m - 6)] if m >= 6 else []) for m in range(2, NZ)},
        {m: [(k_hop, m - 2)] for m in range(2, NZ - 1)},
    )

    def drain_scatter():
        @pl.when(c == 1)
        def _():
            landed(sent.at[7], 28 * SPLIT)
            landed(sent.at[10], (NX - 1) * SPLIT)
            landed(sent.at[6], NZ * NX * REST)
            landed(sent.at[11], NT * SPLIT)

        @pl.when(c == 0)
        def _():
            landed(sent.at[8], NZ * (NX - 1) * REST)
            landed(sent.at[9], (NZ - 1) * REST)
            landed(sent.at[6], NZ * NX * SPLIT)
            landed(sent.at[11], NT * REST)

    def scatter_step(m, _):
        gradient_row(m)
        run_plan(m, back)
        return 0

    lax.fori_loop(0, NZ, scatter_step, 0)

    @pl.when(c == 0)
    def _():
        v_out(6)
        v_out(7)
        for m in range(2, 5):
            v_in(m)

    @pl.when(c == 1)
    def _():
        k_hop(5)
        k_hop(6)

    for j, acc in enumerate((dq2[0:HD], dq2[HD:2 * HD] + dql[...])):
        g = (acc * INV_ROOT).T.astype(BF16)
        for i in range(2):
            for h in range(HEADS):
                at_row = i * ROWS + h * HALF
                dqst[i, j * HALF:(j + 1) * HALF, h * HD:(h + 1) * HD] = g[at_row:at_row + HALF]

    def dq_copy(i):
        if i == 0:
            return remote(dqst.at[0], dqr.at[0], sent.at[12], dqsr.at[0], other(t, c))
        part = pl.ds((i - 1) * HALF, HALF)
        return remote(dqst.at[1, part], dqr.at[1, part], sent.at[12], dqsr.at[0],
                      other(mates[i - 1], c))

    for i in range(3):
        dq_copy(i).start()

    @pl.when(c == 1)
    def _():
        k_last()

    @pl.when(c == 0)
    def _():
        for m in range(5, NZ):
            v_in(m)
        v_last()

    def last(tt, part):
        return remote(ysum.at[part], yr.at[t // 2, part], sent.at[11], yrsem.at[0],
                      other(tt, half))

    for core, part in ((0, SECOND), (1, FIRST)):
        @pl.when(c == core)
        def _():
            for tt in range(NT):
                last(tt, part).start()

    drain_gather()
    drain_scatter()

    landed(dqsr.at[0], 8 * 128)
    dq_out[0] = (dqr[0].astype(F32) + dqr[1].astype(F32)).astype(BF16)
    landed(yrsem.at[0], 2 * BLOCK)
    for kind, out in ((0, dk_out), (1, dv_out)):
        part = slice(kind * 128, (kind + 1) * 128)
        out[0] = (yr[0, part].astype(F32) + yr[1, part].astype(F32)).astype(BF16)
    landed(sent.at[12], 8 * 128)


def per_device(queries, keys, values, grad_out, span_order):
    vmem = pl.BlockSpec(memory_space=pltpu.VMEM)
    hbm = pl.BlockSpec(memory_space=pl.ANY)
    dma = pltpu.SemaphoreType.DMA

    def plane():
        return pltpu.VMEM((NZ, NX, BLOCK, HD), BF16)

    scratch = [
        pltpu.VMEM(queries.shape, BF16),
        pltpu.VMEM(keys.shape, BF16),
        pltpu.VMEM(values.shape, BF16),
        pltpu.VMEM(grad_out.shape, BF16),
        plane(),
        pltpu.VMEM((NZ, KEYS, SLOTS), F32),
        pltpu.VMEM((NZ, KEYS, SLOTS), F32),
        pltpu.VMEM((NZ, KEYS, SLOTS), F32),
        pltpu.VMEM((NZ, KEYS, SLOTS), F32),
        pltpu.VMEM((NZ, KEYS, 2 * HD), BF16),
        pltpu.VMEM((SLOTS, 2 * HD), BF16),
        pltpu.VMEM((SLOTS, 2 * HD), BF16),
        pltpu.VMEM((2, HALF, HEADS * HD), BF16),
        pltpu.VMEM((2, HALF, HEADS * HD), BF16),
        pltpu.VMEM((HD, SLOTS), F32),
        pltpu.VMEM((2 * HD, SLOTS), F32),
        pltpu.VMEM((2, 128, HEADS * HD), BF16),
        pltpu.VMEM((2, 128, HEADS * HD), BF16),
        pltpu.VMEM((8, SLOTS), F32),
        pltpu.VMEM((NZ + 1, 8, SLOTS), F32),
        pltpu.VMEM((4, HALF, SLOTS), F32),
        pltpu.VMEM((2, 8, SLOTS), F32),
        pltpu.VMEM((2, 8, SLOTS), F32),
        plane(),
        plane(),
        pltpu.VMEM((2, 4, NX, SPLIT, HD), BF16),
        pltpu.VMEM((NX * NZ * REST, HD), BF16),
        pltpu.VMEM((NZ, REST, HD), BF16),
        pltpu.VMEM((NX, SPLIT, HD), BF16),
        pltpu.VMEM((BLOCK, HD), BF16),
        pltpu.VMEM((2, BLOCK, HD), BF16),
        dma((2,)), dma((13,)),
        dma((NX,)), dma((NZ,)), dma((13,)), dma((NZ,)), dma((NZ,)),
        dma((1,)), dma((1,)),
        dma((NZ,)), dma((12,)), dma((NZ,)), dma((1,)), dma((1,)),
        dma((1,)), dma((1,)),
    ]
    return pl.pallas_call(
        kernel,
        out_shape=(
            jax.ShapeDtypeStruct(queries.shape, BF16),
            jax.ShapeDtypeStruct(keys.shape, BF16),
            jax.ShapeDtypeStruct(values.shape, BF16),
        ),
        in_specs=[hbm, hbm, hbm, hbm, pl.BlockSpec(memory_space=pltpu.SMEM)],
        out_specs=(vmem, vmem, vmem),
        scratch_shapes=scratch,
        compiler_params=pltpu.CompilerParams(
            collective_id=1, has_side_effects=True, vmem_limit_bytes=56 * 2**20
        ),
        name="attention_backward",
    )(queries, keys, values, grad_out, jnp.swapaxes(span_order, 1, 2))


def solution(mesh):
    return jax.shard_map(
        per_device,
        mesh=mesh,
        in_specs=(
            P("pipe", "ctx", "tp"),
            P("pipe", "ctx", None),
            P("pipe", "ctx", None),
            P("pipe", "ctx", "tp"),
            P("pipe", None, None),
        ),
        out_specs=(P("pipe", "ctx", "tp"), P("pipe", "ctx", None), P("pipe", "ctx", None)),
        check_vma=False,
    )
```

```python
import functools

import jax
import jax.numpy as jnp
from jax import lax
from jax.experimental import pallas as pl
from jax.experimental.pallas import tpu as pltpu
from jax.sharding import PartitionSpec as P

MESH = pl.DeviceIdType.MESH
F32 = jnp.float32
BF16 = jnp.bfloat16

NZ = 8
NX = 4
NT = 4
HEADS = 4
HALF = 64
HD = 128
ROWS = HEADS * HALF
SLOTS = 2 * ROWS
KEYS = NX * HALF
BLOCK = 256
SPLIT = 112
REST = BLOCK - SPLIT
FIRST = pl.ds(0, SPLIT)
SECOND = pl.ds(SPLIT, REST)
INV_ROOT = HD ** (-0.5)
LOG2E = 1.4426950408889634
NEG = -1e30
POS = 1e30
ORDER = (0, 1, -1, 2, -2, 3, -3, 4)
BACK = (4, -3, 3, -1, 1, -2, 2, 0)
ACROSS = (0, 1, 3, 2)
SETS = ((0, 1), (3, 2))


def dot_nt(a, b):
    return lax.dot_general(a, b, (((1,), (1,)), ((), ())), preferred_element_type=F32)


def dot_nn(a, b):
    return jnp.dot(a, b, preferred_element_type=F32)


def dot_tn(a, b):
    return lax.dot_general(a, b, (((0,), (0,)), ((), ())), preferred_element_type=F32)


def col_sum(v):
    return jnp.sum(v, axis=0, keepdims=True)


def col_max(v):
    return jnp.max(v, axis=0, keepdims=True)


def kernel(
    q_hbm, k_hbm, v_hbm, g_hbm, span_ref,
    dqr, yr,
    q_ref, k_ref, v_ref, g_ref, kv, s1, s2, dp1, dp2, kselbuf, qq, oo, pq, pg, dql, dq2, dqst,
    state, tops, diag, sums_out, sums_in,
    pkv, sib, rr, cx, zr, xr, ysum,
    insem, sent, p1kr, p1vr, zkr, x1r, d2dr, pqr, sums_r, sibr, rrsem, c1r, zrsem, xrsem,
    yrsem, dqsr,
):
    pipe = lax.axis_index("pipe")
    me = lax.axis_index("ctx")
    t = lax.axis_index("tp")
    z = me // (2 * NX)
    x = (me // 2) % NX
    c = me % 2
    half = t % 2
    mates = (t + 1 - 2 * half, lax.rem(t + 2 * half + NT - 1, NT))

    def at(zz, xx, cc):
        return (pipe, (zz * NX + xx) * 2 + cc, t)

    def zoff(d):
        return lax.rem(z + d + NZ, NZ)

    def xoff(d):
        return lax.rem(x + d + NX, NX)

    def row_of(n):
        return zoff(((n + 1) // 2) * (2 * (n % 2) - 1))

    def mate(j):
        return (pipe, me, mates[j])

    def back_row(m):
        d = 0
        for i, far in enumerate(BACK):
            d = jnp.where(m == i, far, d)
        return zoff(d)

    def other(tt, cc):
        return (1 - pipe, (z * NX + x) * 2 + cc, tt)

    sibling = at(z, x, 1 - c)

    def remote(src, dst, ssem, rsem, dev):
        return pltpu.make_async_remote_copy(
            src_ref=src, dst_ref=dst, send_sem=ssem, recv_sem=rsem,
            device_id=dev, device_id_type=MESH,
        )

    def take(i):
        src = (q_hbm, g_hbm, k_hbm, v_hbm)[i]
        return pltpu.make_async_copy(src, (q_ref, g_ref, k_ref, v_ref)[i], insem.at[0])

    for i in range(4):
        take(i).start()

    barrier = pltpu.get_barrier_semaphore()
    count = 0

    def greet(dev):
        pl.semaphore_signal(barrier, inc=1, device_id=dev, device_id_type=MESH)

    greet(sibling)
    count += 1
    for cc in range(2):
        for d in range(1, NX):
            greet(at(z, xoff(d), cc))
            count += 1
        for d in range(1, NZ):
            greet(at(zoff(d), x, cc))
            count += 1
        for tt in range(NT):
            greet(other(tt, cc))
            count += 1
    for j in range(2):
        greet(mate(j))
        count += 1

    def lay_rows(dst, base, src, lo, j):
        for h in range(HEADS):
            dst[base + h * HALF:base + (h + 1) * HALF, j * HD:(j + 1) * HD] = src[
                lo:lo + HALF, h * HD:(h + 1) * HD]

    low = jnp.full((1, SLOTS), NEG, F32)
    state[...] = jnp.zeros_like(state)
    sums_out[...] = jnp.zeros_like(sums_out)
    for j in range(2):
        state[j:j + 1] = low
    dql[...] = jnp.zeros_like(dql)
    dq2[...] = jnp.zeros_like(dq2)
    scale = INV_ROOT * LOG2E

    pl.semaphore_wait(barrier, count)

    def swap_rows(j, kind):
        src = (q_hbm, g_hbm)[kind].at[0, pl.ds(j * HALF, HALF)]
        dst = (pq, pg)[kind].at[j]
        return remote(src, dst, sent.at[4], pqr.at[0], mate(j))

    for kind in range(2):
        for j in range(2):
            swap_rows(j, kind).start()

    def first_k(d):
        return remote(k_hbm.at[0, FIRST], kv.at[z, x, FIRST], sent.at[0], p1kr.at[d],
                      at(z, xoff(d), 1))

    def first_v(d):
        there = at(zoff(d), x, 0)
        keys = remote(k_hbm.at[0, pl.ds(SPLIT, 128 - SPLIT)], kv.at[z, x, pl.ds(SPLIT, 128 - SPLIT)],
                      sent.at[0], p1vr.at[d], there)
        values = remote(v_hbm.at[0], kv.at[z, x, pl.ds(128, 128)], sent.at[0], p1vr.at[d], there)
        return keys, values

    def k_slot(way, k, j):
        return {1: way, 2: 5 + way * 4 + j, 3: 2 + way, 4: 4}[k]

    def k_send(way, k, j):
        step = 1 if way == 0 else -1
        back, far = ((0, 1), (0, 2), (2, 1), (2, 2))[k - 1]
        ref = kv.at[zoff(-step * back), xoff(j), FIRST]
        return remote(ref, ref, sent.at[1], zkr.at[k_slot(way, k, j)],
                      at(zoff(step * far), x, 1))

    def v_x(d, n):
        ref = kv.at[zoff(ORDER[n]), x, SECOND]
        return remote(ref, ref, sent.at[2], x1r.at[n], at(z, xoff(d), 0))

    def hand_over(part, n):
        ref = kv.at[row_of(n), :, part]
        return remote(ref, ref, sent.at[3], d2dr.at[n], sibling)

    def landed(sem, rows):
        ref = cx.at[pl.ds(0, rows)]
        pltpu.make_async_copy(ref, ref, sem).wait()

    def gather_k(n):
        d = ORDER[n]
        k = abs(d)
        if k == 0:
            for j in ACROSS:
                src = (NX - j) % NX
                if src:
                    landed(p1kr.at[src], SPLIT)
                else:
                    @pl.when(half == 0)
                    def _():
                        landed(p1kr.at[0], SPLIT)
                for w in range(2):
                    k_send(w, 2, j).start()
                    k_send(w, 1, j).start()
        elif k == 2:
            w = 1 if d > 0 else 0
            for j in ACROSS:
                landed(zkr.at[k_slot(w, 2, j)], SPLIT)
                if j in SETS[w]:
                    k_send(w, 4, j).start()
                k_send(w, 3, j).start()
        else:
            landed(zkr.at[k_slot(1 if d > 0 else 0, k, 0)], NX * SPLIT)
        hand_over(FIRST, n).start()

    def v_stage1(n):
        d = ORDER[n]
        if d:
            landed(p1vr.at[-d % NZ], REST)
        else:
            @pl.when(half == 1)
            def _():
                landed(p1vr.at[0], REST)
        for dx in (1, 3, 2):
            v_x(dx, n).start()

    def v_stage2(n):
        landed(x1r.at[n], (NX - 1) * REST)
        hand_over(SECOND, n).start()

    def keep(i):
        part = pl.ds(0, SPLIT) if i == 0 else pl.ds(SPLIT, 128 - SPLIT)
        if i == 2:
            src, dst = v_hbm.at[0], kv.at[z, x, pl.ds(128, 128)]
        else:
            src, dst = k_hbm.at[0, part], kv.at[z, x, part]
        return pltpu.make_async_copy(src, dst, insem.at[1])

    @pl.when(c == half)
    def _():
        for d in (1, 3, 2):
            first_k(d).start()

        @pl.when(c == 0)
        def _():
            first_k(0).start()
            keep(1).start()
            keep(2).start()

        @pl.when(c == 1)
        def _():
            for cp in first_v(0):
                cp.start()
            keep(0).start()

        for d in (1, 7, 2, 6, 3, 5, 4):
            for cp in first_v(d):
                cp.start()

        @pl.when(c == 0)
        def _():
            landed(insem.at[1], REST)

        @pl.when(c == 1)
        def _():
            landed(insem.at[1], SPLIT)

    landed(insem.at[0], 10 * 128)
    for j in range(2):
        lay_rows(qq, 0, q_ref.at[0], j * HALF, j)
        lay_rows(oo, 0, g_ref.at[0], j * HALF, j)

    def drain_gather():
        @pl.when(c == 1)
        def _():
            landed(sent.at[1], 28 * SPLIT)
            landed(sent.at[3], NZ * NX * SPLIT)

        @pl.when(c == 0)
        def _():
            landed(sent.at[2], NZ * (NX - 1) * REST)
            landed(sent.at[3], NZ * NX * REST)

        @pl.when((c == half) & (c == 0))
        def _():
            landed(sent.at[0], NX * SPLIT + (NZ - 1) * REST)

        @pl.when((c == half) & (c == 1))
        def _():
            landed(sent.at[0], (NX - 1) * SPLIT + NZ * REST)

        landed(sent.at[4], 8 * 128)
        landed(sent.at[5], 128)

    my_block = span_ref[0, 0, me]

    def index(b, i):
        return (b * NX + i) * 2 + half

    def early(b, i):
        return span_ref[0, 0, index(b, i)] < my_block

    def pick(at_row, b):
        e, both = [], []
        for i in range(NX):
            lo = kv[b, i, at_row:at_row + HALF]
            hi = kv[b, i, at_row + HALF:at_row + 2 * HALF]
            s = early(b, i)
            zero = jnp.zeros_like(lo)
            e.append(lo)
            both.append(jnp.concatenate([jnp.where(s, lo, zero), jnp.where(s, zero, hi)], axis=1))
        return jnp.concatenate(e, axis=0), jnp.concatenate(both, axis=0)

    def softmax_row(n):
        b = row_of(n)

        @pl.when(c == 1)
        def _():
            hand_over(SECOND, n).wait_recv()

        @pl.when(c == 0)
        def _():
            hand_over(FIRST, n).wait_recv()

        ke, ksel = pick(0, b)
        kselbuf[b] = ksel
        s1[b] = dot_nt(ke, qq[:, HD:]) * scale
        s2[b] = dot_nt(ksel, qq[...]) * scale
        ve, vsel = pick(128, b)
        dp1[b] = dot_nt(ve, oo[:, HD:])
        dp2[b] = dot_nt(vsel, oo[...])
        old_e, old_l = state[0:1], state[1:2]
        m_e, m_l = old_e, jnp.maximum(old_l, col_max(s1[b]))
        low = jnp.full((1, SLOTS), NEG, F32)
        high = jnp.full((1, SLOTS), POS, F32)
        for i in range(NX):
            top = col_max(s2[b, i * HALF:(i + 1) * HALF])
            s = early(b, i)
            top = jnp.where(index(b, i) == me, low, top)
            m_e = jnp.maximum(m_e, jnp.where(s, top, low))
            m_l = jnp.maximum(m_l, jnp.where(s, low, top))
        a_e = jnp.exp2(old_e - m_e)
        a_l = jnp.exp2(old_l - m_l)
        l_e, l_l = state[2:3] * a_e, state[3:4] * a_l
        d_e, d_l = state[4:5] * a_e, state[5:6] * a_l
        for i in range(NX):
            part = slice(i * HALF, (i + 1) * HALF)
            p = jnp.exp2(s1[b, part] - m_l)
            s1[b, part] = p
            l_l = l_l + col_sum(p)
            d_l = d_l + col_sum(p * dp1[b, part])
            s = early(b, i)
            top = jnp.where(s, m_e, m_l)
            top = jnp.where(index(b, i) == me, high, top)
            p = jnp.exp2(s2[b, part] - top)
            s2[b, part] = p
            ps = col_sum(p)
            pd = col_sum(p * dp2[b, part])
            zero = jnp.zeros_like(ps)
            l_e = l_e + jnp.where(s, ps, zero)
            l_l = l_l + jnp.where(s, zero, ps)
            d_e = d_e + jnp.where(s, pd, zero)
            d_l = d_l + jnp.where(s, zero, pd)
        for i, v in enumerate((m_e, m_l, l_e, l_l, d_e, d_l)):
            state[i:i + 1] = v
        tops[b, 0:1] = m_e
        tops[b, 1:2] = m_l

    def diagonal():
        key_no = lax.broadcasted_iota(jnp.int32, (HALF, SLOTS), 0)
        tok_no = lax.broadcasted_iota(jnp.int32, (HALF, SLOTS), 1) % HALF
        seen = key_no <= tok_no
        for j in range(2):
            part = slice(j * HALF, (j + 1) * HALF)
            cols = slice(j * HD, (j + 1) * HD)
            s = jnp.where(seen, dot_nt(k_ref[0, part], qq[:, cols]) * scale, NEG)
            top = col_max(s)
            p = jnp.exp2(s - top)
            dp = dot_nt(v_ref[0, part], oo[:, cols])
            diag[2 * j] = p
            diag[2 * j + 1] = dp
            state[j:j + 1] = top
            state[2 + j:3 + j] = col_sum(p)
            state[4 + j:5 + j] = col_sum(p * dp)
            tops[NZ, j:j + 1] = top

    def swap_sums(j):
        return remote(sums_out.at[j], sums_in.at[j], sent.at[5], sums_r.at[0], mate(j))

    LAG = 2
    plans = (
        {
            0: [(v_stage1, n) for n in range(5)],
            1: [(v_stage1, 5), (v_stage1, 6), (v_stage1, 7)] + [(v_stage2, n) for n in range(3)],
            3: [(v_stage2, 3), (v_stage2, 4)],
            5: [(v_stage2, 5), (v_stage2, 6), (v_stage2, 7)],
        },
        {
            0: [(gather_k, 0), (gather_k, 3), (gather_k, 4)],
            1: [(gather_k, 1), (gather_k, 2)],
            6: [(gather_k, 5), (gather_k, 6), (gather_k, 7)],
        },
    )

    def run_plan(i, plans):
        for core in range(2):
            for j, todo in plans[core].items():
                @pl.when((i == j) & (c == core))
                def _():
                    for stage, n in todo:
                        stage(n)

    def gather_step(i, _):
        run_plan(i, plans)

        @pl.when(i == LAG)
        def _():
            landed(pqr.at[0], 8 * 128)
            for kind in range(2):
                for j in range(2):
                    lay_rows((qq, oo)[kind], ROWS, (pq, pg)[kind].at[j], 0, j)

            @pl.when(c == half)
            def _():
                diagonal()

        @pl.when(i >= LAG)
        def _():
            softmax_row(i - LAG)

        return 0

    lax.fori_loop(0, NZ + LAG, gather_step, 0)

    for j in range(2):
        for i in range(3):
            sums_out[j, i:i + 1] = state[2 * i + j:2 * i + j + 1]
        swap_sums(j).start()
    landed(sums_r.at[0], 128)
    for j in range(2):
        m, l, d = (state[2 * i + j:2 * i + j + 1] for i in range(3))
        m2, l2, d2 = (
            jnp.concatenate([sums_in[j, i:i + 1, ROWS:], sums_in[j, i:i + 1, :ROWS]], axis=1)
            for i in range(3)
        )
        top = jnp.maximum(m, m2)
        a, a2 = jnp.exp2(m - top), jnp.exp2(m2 - top)
        r = 1.0 / (l * a + l2 * a2)
        state[j:j + 1] = top
        state[2 + j:3 + j] = r
        state[4 + j:5 + j] = (d * a + d2 * a2) * r

    @pl.when(c == half)
    def _():
        for j in range(2):
            part = slice(j * HALF, (j + 1) * HALF)
            cols = slice(j * HD, (j + 1) * HD)
            m, r, d = state[j:j + 1], state[2 + j:3 + j], state[4 + j:5 + j]
            p = diag[2 * j] * (jnp.exp2(tops[NZ, j:j + 1] - m) * r)
            ds = (p * (diag[2 * j + 1] - d)).astype(BF16)
            dq2[cols] = dot_tn(k_ref[0, part], ds)
            diag[2 * j, :, :HD] = dot_nn(ds, qq[:, cols]) * INV_ROOT
            diag[2 * j, :, HD:2 * HD] = dot_nn(p.astype(BF16), oo[:, cols])

    def give(part, m):
        b = back_row(m)
        return remote(pkv.at[b, :, part], sib.at[b, :, part], sent.at[6], sibr.at[m], sibling)

    def gradient_row(m):
        b = back_row(m)
        r_e, r_l, d_e, d_l = state[2:3], state[3:4], state[4:5], state[5:6]
        f_e = jnp.exp2(tops[b, 0:1] - state[0:1]) * r_e
        f_l = jnp.exp2(tops[b, 1:2] - state[1:2]) * r_l
        ke = jnp.concatenate([kv[b, i, :HALF] for i in range(NX)], axis=0)
        ksel = kselbuf[b]
        p1 = s1[b] * f_l
        ds1 = (p1 * (dp1[b] - d_l)).astype(BF16)
        p1 = p1.astype(BF16)
        p2s, ds2s = [], []
        for i in range(NX):
            part = slice(i * HALF, (i + 1) * HALF)
            s = early(b, i)
            p = s2[b, part] * jnp.where(s, f_e, f_l)
            ds2s.append((p * (dp2[b, part] - jnp.where(s, d_e, d_l))).astype(BF16))
            p2s.append(p.astype(BF16))
        p2 = jnp.concatenate(p2s, axis=0)
        ds2 = jnp.concatenate(ds2s, axis=0)
        v1 = dot_nn(p1, oo[:, HD:])
        v2 = dot_nn(p2, oo[...])
        k1 = dot_nn(ds1, qq[:, HD:]) * INV_ROOT
        k2 = dot_nn(ds2, qq[...]) * INV_ROOT
        dql[...] += dot_tn(ke, ds1)
        dq2[...] += dot_tn(ksel, ds2)
        for i in range(NX):
            part = slice(i * HALF, (i + 1) * HALF)
            s = early(b, i)
            zero = jnp.zeros((HALF, HD), F32)
            k_lo, k_hi, v_lo, v_hi = (slice(j * HALF, (j + 1) * HALF) for j in range(4))
            pkv[b, i, v_lo] = (v1[part] + jnp.where(s, v2[part, :HD], zero)).astype(BF16)
            pkv[b, i, v_hi] = jnp.where(s, zero, v2[part, HD:]).astype(BF16)
            pkv[b, i, k_lo] = (k1[part] + jnp.where(s, k2[part, :HD], zero)).astype(BF16)
            pkv[b, i, k_hi] = jnp.where(s, zero, k2[part, HD:]).astype(BF16)

        @pl.when((m == NZ - 1) & (c == half))
        def _():
            for j in range(2):
                part = slice(j * HALF, (j + 1) * HALF)
                v_part = slice(128 + j * HALF, 128 + (j + 1) * HALF)
                pkv[z, x, part] = (
                    pkv[z, x, part].astype(F32) + diag[2 * j, :, :HD]).astype(BF16)
                pkv[z, x, v_part] = (
                    pkv[z, x, v_part].astype(F32) + diag[2 * j, :, HD:2 * HD]).astype(BF16)

        @pl.when(c == 1)
        def _():
            give(SECOND, m).start()

        @pl.when(c == 0)
        def _():
            give(FIRST, m).start()

    def add_up(row, col, part, *terms):
        total = pkv[row, col, part].astype(F32) + sib[row, col, part].astype(F32)
        for ref, i in terms:
            total = total + ref[i].astype(F32)
        return total

    def k_back(way, k, j):
        step = 1 if way == 0 else -1
        far = (1, 2, 1, 2)[k - 1]
        return remote(pkv.at[zoff(step * k), xoff(j), FIRST], rr.at[way, k - 1, j],
                      sent.at[7], rrsem.at[8 + j if k < 3 else way * 4 + j], at(zoff(step * far), x, 1))

    def k_across(j):
        return remote(pkv.at[z, xoff(j), FIRST], xr.at[j], sent.at[10], xrsem.at[0], at(z, xoff(j), 1))

    def k_hop(m):
        give(FIRST, m).wait_recv()
        d = BACK[m]
        k = abs(d)
        if k == 4:
            plan = [(w, j, ()) for i in range(2) for w, j in ((0, SETS[0][i]), (1, SETS[1][i]))]
        else:
            w = 0 if d > 0 else 1
            if k == 3:
                plan = [(w, j, ()) for j in ACROSS]
            elif k == 2:
                plan = [(w, j, (3, 4) if j in SETS[w] else (3,)) for j in SETS[1 - w] + SETS[w]]
            else:
                plan = [(w, j, ()) for j in ACROSS]
        for w, j, has in plan:
            row, col = zoff(d), xoff(j)
            terms = []
            if has:
                landed(rrsem.at[w * 4 + j], len(has) * SPLIT)
            for q in has:
                terms.append((rr, (w, q - 1, j)))
            pkv[row, col, FIRST] = add_up(row, col, FIRST, *terms).astype(BF16)
            k_back(w, k, j).start()

    def k_last():
        give(FIRST, NZ - 1).wait_recv()
        for j in (2, 1, 3, 0):
            landed(rrsem.at[8 + j], 4 * SPLIT)
            terms = []
            for w in range(2):
                for k in (1, 2):
                    terms.append((rr, (w, k - 1, j)))
            total = add_up(z, xoff(j), FIRST, *terms)
            if j:
                pkv[z, xoff(j), FIRST] = total.astype(BF16)
                k_across(j).start()
        landed(xrsem.at[0], (NX - 1) * SPLIT)
        for j in range(1, NX):
            total = total + xr[j].astype(F32)
        ysum[FIRST] = total.astype(BF16)

    def cx_part(d, m):
        return pl.ds((d * NZ + m) * REST, REST)

    def v_back(d, m):
        return remote(pkv.at[zoff(BACK[m]), xoff(d), SECOND], cx.at[cx_part(d, m)], sent.at[8],
                      c1r.at[m], at(z, xoff(d), 0))

    def v_z(m):
        d = BACK[m]
        return remote(pkv.at[zoff(d), x, SECOND], zr.at[m], sent.at[9], zrsem.at[0], at(zoff(d), x, 0))

    def v_out(m):
        give(SECOND, m).wait_recv()
        for d in (2, 1, 3):
            row, col = zoff(BACK[m]), xoff(d)
            pkv[row, col, SECOND] = add_up(row, col, SECOND).astype(BF16)
            v_back(d, m).start()

    def v_in(m):
        row = zoff(BACK[m])
        landed(c1r.at[m], (NX - 1) * REST)
        terms = [(cx, cx_part(d, m)) for d in range(1, NX)]
        pkv[row, x, SECOND] = add_up(row, x, SECOND, *terms).astype(BF16)
        if m < NZ - 1:
            v_z(m).start()

    def v_last():
        total = pkv[z, x, SECOND].astype(F32)
        landed(zrsem.at[0], (NZ - 1) * REST)
        for m in range(NZ - 1):
            total = total + zr[m].astype(F32)
        ysum[SECOND] = total.astype(BF16)

    back = (
        {m: [(v_out, m - 2)] + ([(v_in, m - 6)] if m >= 6 else []) for m in range(2, NZ)},
        {m: [(k_hop, m - 2)] for m in range(2, NZ - 1)},
    )

    def drain_scatter():
        @pl.when(c == 1)
        def _():
            landed(sent.at[7], 28 * SPLIT)
            landed(sent.at[10], (NX - 1) * SPLIT)
            landed(sent.at[6], NZ * NX * REST)
            landed(sent.at[11], NT * SPLIT)

        @pl.when(c == 0)
        def _():
            landed(sent.at[8], NZ * (NX - 1) * REST)
            landed(sent.at[9], (NZ - 1) * REST)
            landed(sent.at[6], NZ * NX * SPLIT)
            landed(sent.at[11], NT * REST)

    def scatter_step(m, _):
        gradient_row(m)
        run_plan(m, back)
        return 0

    lax.fori_loop(0, NZ, scatter_step, 0)

    @pl.when(c == 0)
    def _():
        v_out(6)
        v_out(7)
        for m in range(2, 5):
            v_in(m)

    @pl.when(c == 1)
    def _():
        k_hop(5)
        k_hop(6)

    for j, acc in enumerate((dq2[0:HD], dq2[HD:2 * HD] + dql[...])):
        g = (acc * INV_ROOT).T.astype(BF16)
        for i in range(2):
            for h in range(HEADS):
                at_row = i * ROWS + h * HALF
                dqst[i, j * HALF:(j + 1) * HALF, h * HD:(h + 1) * HD] = g[at_row:at_row + HALF]

    def dq_copy(i):
        if i == 0:
            return remote(dqst.at[0], dqr.at[0], sent.at[12], dqsr.at[0], other(t, c))
        part = pl.ds((i - 1) * HALF, HALF)
        return remote(dqst.at[1, part], dqr.at[1, part], sent.at[12], dqsr.at[0],
                      other(mates[i - 1], c))

    for i in range(3):
        dq_copy(i).start()

    @pl.when(c == 1)
    def _():
        k_last()

    @pl.when(c == 0)
    def _():
        for m in range(5, NZ):
            v_in(m)
        v_last()

    def last(tt, part):
        return remote(ysum.at[part], yr.at[t // 2, part], sent.at[11], yrsem.at[0],
                      other(tt, half))

    for core, part in ((0, SECOND), (1, FIRST)):
        @pl.when(c == core)
        def _():
            for tt in range(NT):
                last(tt, part).start()

    drain_gather()
    drain_scatter()

    landed(dqsr.at[0], 8 * 128)
    landed(yrsem.at[0], 2 * BLOCK)
    landed(sent.at[12], 8 * 128)


def last_sums(dqr, yr, dq_out, dk_out, dv_out):
    dq_out[0] = (dqr[0].astype(F32) + dqr[1].astype(F32)).astype(BF16)
    for kind, out in ((0, dk_out), (1, dv_out)):
        part = slice(kind * 128, (kind + 1) * 128)
        out[0] = (yr[0, part].astype(F32) + yr[1, part].astype(F32)).astype(BF16)


def per_device(queries, keys, values, grad_out, span_order):
    vmem = pl.BlockSpec(memory_space=pltpu.VMEM)
    hbm = pl.BlockSpec(memory_space=pl.ANY)
    dma = pltpu.SemaphoreType.DMA

    def plane():
        return pltpu.VMEM((NZ, NX, BLOCK, HD), BF16)

    scratch = [
        pltpu.VMEM(queries.shape, BF16),
        pltpu.VMEM(keys.shape, BF16),
        pltpu.VMEM(values.shape, BF16),
        pltpu.VMEM(grad_out.shape, BF16),
        plane(),
        pltpu.VMEM((NZ, KEYS, SLOTS), F32),
        pltpu.VMEM((NZ, KEYS, SLOTS), F32),
        pltpu.VMEM((NZ, KEYS, SLOTS), F32),
        pltpu.VMEM((NZ, KEYS, SLOTS), F32),
        pltpu.VMEM((NZ, KEYS, 2 * HD), BF16),
        pltpu.VMEM((SLOTS, 2 * HD), BF16),
        pltpu.VMEM((SLOTS, 2 * HD), BF16),
        pltpu.VMEM((2, HALF, HEADS * HD), BF16),
        pltpu.VMEM((2, HALF, HEADS * HD), BF16),
        pltpu.VMEM((HD, SLOTS), F32),
        pltpu.VMEM((2 * HD, SLOTS), F32),
        pltpu.VMEM((2, 128, HEADS * HD), BF16),
        pltpu.VMEM((8, SLOTS), F32),
        pltpu.VMEM((NZ + 1, 8, SLOTS), F32),
        pltpu.VMEM((4, HALF, SLOTS), F32),
        pltpu.VMEM((2, 8, SLOTS), F32),
        pltpu.VMEM((2, 8, SLOTS), F32),
        plane(),
        plane(),
        pltpu.VMEM((2, 4, NX, SPLIT, HD), BF16),
        pltpu.VMEM((NX * NZ * REST, HD), BF16),
        pltpu.VMEM((NZ, REST, HD), BF16),
        pltpu.VMEM((NX, SPLIT, HD), BF16),
        pltpu.VMEM((BLOCK, HD), BF16),
        dma((2,)), dma((13,)),
        dma((NX,)), dma((NZ,)), dma((13,)), dma((NZ,)), dma((NZ,)),
        dma((1,)), dma((1,)),
        dma((NZ,)), dma((12,)), dma((NZ,)), dma((1,)), dma((1,)),
        dma((1,)), dma((1,)),
    ]
    arrived = pl.pallas_call(
        kernel,
        out_shape=(
            jax.ShapeDtypeStruct((2, 128, HEADS * HD), BF16),
            jax.ShapeDtypeStruct((2, BLOCK, HD), BF16),
        ),
        in_specs=[hbm, hbm, hbm, hbm, pl.BlockSpec(memory_space=pltpu.SMEM)],
        out_specs=(hbm, hbm),
        scratch_shapes=scratch,
        compiler_params=pltpu.CompilerParams(
            collective_id=1, has_side_effects=True, vmem_limit_bytes=56 * 2**20
        ),
        name="attention_backward",
    )(queries, keys, values, grad_out, jnp.swapaxes(span_order, 1, 2))
    return pl.pallas_call(
        last_sums,
        out_shape=tuple(jax.ShapeDtypeStruct(a.shape, BF16) for a in (queries, keys, values)),
        in_specs=[vmem, vmem],
        out_specs=(vmem, vmem, vmem),
        name="last_sums",
    )(*arrived)


def solution(mesh):
    return jax.shard_map(
        per_device,
        mesh=mesh,
        in_specs=(
            P("pipe", "ctx", "tp"),
            P("pipe", "ctx", None),
            P("pipe", "ctx", None),
            P("pipe", "ctx", "tp"),
            P("pipe", None, None),
        ),
        out_specs=(P("pipe", "ctx", "tp"), P("pipe", "ctx", None), P("pipe", "ctx", None)),
        check_vma=False,
    )
```

```python
import functools

import jax
import jax.numpy as jnp
from jax import lax
from jax.experimental import pallas as pl
from jax.experimental.pallas import tpu as pltpu
from jax.sharding import PartitionSpec as P

MESH = pl.DeviceIdType.MESH
F32 = jnp.float32
BF16 = jnp.bfloat16

NZ = 8
NX = 4
NT = 4
HEADS = 4
HALF = 64
HD = 128
ROWS = HEADS * HALF
SLOTS = 2 * ROWS
KEYS = NX * HALF
BLOCK = 256
SPLIT = 112
REST = BLOCK - SPLIT
FIRST = pl.ds(0, SPLIT)
SECOND = pl.ds(SPLIT, REST)
INV_ROOT = HD ** (-0.5)
LOG2E = 1.4426950408889634
NEG = -1e30
POS = 1e30
ORDER = (0, 1, -1, 2, -2, 3, -3, 4)
BACK = (4, -3, 3, -1, 1, -2, 2, 0)
ACROSS = (0, 1, 3, 2)
SETS = ((0, 1), (3, 2))


def dot_nt(a, b):
    return lax.dot_general(a, b, (((1,), (1,)), ((), ())), preferred_element_type=F32)


def dot_nn(a, b):
    return jnp.dot(a, b, preferred_element_type=F32)


def dot_tn(a, b):
    return lax.dot_general(a, b, (((0,), (0,)), ((), ())), preferred_element_type=F32)


def col_sum(v):
    return jnp.sum(v, axis=0, keepdims=True)


def col_max(v):
    return jnp.max(v, axis=0, keepdims=True)


def kernel(
    q_hbm, k_hbm, v_hbm, g_hbm, span_ref,
    dqr, yr,
    q_ref, k_ref, v_ref, g_ref, kv, s1, s2, dp1, dp2, kselbuf, qq, oo, pq, pg, dql, dq2, dqst,
    state, tops, diag, sums_out, sums_in,
    pkv, sib, rr, cx, zr, xr, ysum,
    insem, sent, p1kr, p1vr, zkr, x1r, d2dr, pqr, sums_r, sibr, rrsem, c1r, zrsem, xrsem,
    yrsem, dqsr,
):
    pipe = lax.axis_index("pipe")
    me = lax.axis_index("ctx")
    t = lax.axis_index("tp")
    z = me // (2 * NX)
    x = (me // 2) % NX
    c = me % 2
    half = t % 2
    mates = (t + 1 - 2 * half, lax.rem(t + 2 * half + NT - 1, NT))

    def at(zz, xx, cc):
        return (pipe, (zz * NX + xx) * 2 + cc, t)

    def zoff(d):
        return lax.rem(z + d + NZ, NZ)

    def xoff(d):
        return lax.rem(x + d + NX, NX)

    def row_of(n):
        return zoff(((n + 1) // 2) * (2 * (n % 2) - 1))

    def mate(j):
        return (pipe, me, mates[j])

    def back_row(m):
        d = 0
        for i, far in enumerate(BACK):
            d = jnp.where(m == i, far, d)
        return zoff(d)

    def other(tt, cc):
        return (1 - pipe, (z * NX + x) * 2 + cc, tt)

    sibling = at(z, x, 1 - c)

    def remote(src, dst, ssem, rsem, dev):
        return pltpu.make_async_remote_copy(
            src_ref=src, dst_ref=dst, send_sem=ssem, recv_sem=rsem,
            device_id=dev, device_id_type=MESH,
        )

    def take(i):
        src = (q_hbm, g_hbm, k_hbm, v_hbm)[i]
        return pltpu.make_async_copy(src, (q_ref, g_ref, k_ref, v_ref)[i], insem.at[0])

    for i in range(4):
        take(i).start()

    barrier = pltpu.get_barrier_semaphore()
    count = 0

    def greet(dev):
        pl.semaphore_signal(barrier, inc=1, device_id=dev, device_id_type=MESH)

    greet(sibling)
    count += 1
    for cc in range(2):
        for d in range(1, NX):
            greet(at(z, xoff(d), cc))
            count += 1
        for d in range(1, NZ):
            greet(at(zoff(d), x, cc))
            count += 1
        for tt in range(NT):
            greet(other(tt, cc))
            count += 1
    for j in range(2):
        greet(mate(j))
        count += 1

    def lay_rows(dst, base, src, lo, j):
        for h in range(HEADS):
            dst[base + h * HALF:base + (h + 1) * HALF, j * HD:(j + 1) * HD] = src[
                lo:lo + HALF, h * HD:(h + 1) * HD]

    low = jnp.full((1, SLOTS), NEG, F32)
    state[...] = jnp.zeros_like(state)
    sums_out[...] = jnp.zeros_like(sums_out)
    for j in range(2):
        state[j:j + 1] = low
    dql[...] = jnp.zeros_like(dql)
    dq2[...] = jnp.zeros_like(dq2)
    scale = INV_ROOT * LOG2E

    pl.semaphore_wait(barrier, count)

    def swap_rows(j, kind):
        src = (q_hbm, g_hbm)[kind].at[0, pl.ds(j * HALF, HALF)]
        dst = (pq, pg)[kind].at[j]
        return remote(src, dst, sent.at[4], pqr.at[0], mate(j))

    for kind in range(2):
        for j in range(2):
            swap_rows(j, kind).start()

    def first_k(d):
        return remote(k_hbm.at[0, FIRST], kv.at[z, x, FIRST], sent.at[0], p1kr.at[d],
                      at(z, xoff(d), 1))

    def first_v(d):
        there = at(zoff(d), x, 0)
        keys = remote(k_hbm.at[0, pl.ds(SPLIT, 128 - SPLIT)], kv.at[z, x, pl.ds(SPLIT, 128 - SPLIT)],
                      sent.at[0], p1vr.at[d], there)
        values = remote(v_hbm.at[0], kv.at[z, x, pl.ds(128, 128)], sent.at[0], p1vr.at[d], there)
        return keys, values

    def k_slot(way, k, j):
        return {1: way, 2: 5 + way * 4 + j, 3: 2 + way, 4: 4}[k]

    def k_send(way, k, j):
        step = 1 if way == 0 else -1
        back, far = ((0, 1), (0, 2), (2, 1), (2, 2))[k - 1]
        ref = kv.at[zoff(-step * back), xoff(j), FIRST]
        return remote(ref, ref, sent.at[1], zkr.at[k_slot(way, k, j)],
                      at(zoff(step * far), x, 1))

    def v_x(d, n):
        ref = kv.at[zoff(ORDER[n]), x, SECOND]
        return remote(ref, ref, sent.at[2], x1r.at[n], at(z, xoff(d), 0))

    def hand_over(part, n):
        ref = kv.at[row_of(n), :, part]
        return remote(ref, ref, sent.at[3], d2dr.at[n], sibling)

    def landed(sem, rows):
        ref = cx.at[pl.ds(0, rows)]
        pltpu.make_async_copy(ref, ref, sem).wait()

    def gather_k(n):
        d = ORDER[n]
        k = abs(d)
        if k == 0:
            for j in ACROSS:
                src = (NX - j) % NX
                if src:
                    landed(p1kr.at[src], SPLIT)
                else:
                    @pl.when(half == 0)
                    def _():
                        landed(p1kr.at[0], SPLIT)
                for w in range(2):
                    k_send(w, 2, j).start()
                    k_send(w, 1, j).start()
        elif k == 2:
            w = 1 if d > 0 else 0
            for j in ACROSS:
                landed(zkr.at[k_slot(w, 2, j)], SPLIT)
                if j in SETS[w]:
                    k_send(w, 4, j).start()
                k_send(w, 3, j).start()
        else:
            landed(zkr.at[k_slot(1 if d > 0 else 0, k, 0)], NX * SPLIT)
        hand_over(FIRST, n).start()

    def v_stage1(n):
        d = ORDER[n]
        if d:
            landed(p1vr.at[-d % NZ], REST)
        else:
            @pl.when(half == 1)
            def _():
                landed(p1vr.at[0], REST)
        for dx in (1, 3, 2):
            v_x(dx, n).start()

    def v_stage2(n):
        landed(x1r.at[n], (NX - 1) * REST)
        hand_over(SECOND, n).start()

    def keep(i):
        part = pl.ds(0, SPLIT) if i == 0 else pl.ds(SPLIT, 128 - SPLIT)
        if i == 2:
            src, dst = v_hbm.at[0], kv.at[z, x, pl.ds(128, 128)]
        else:
            src, dst = k_hbm.at[0, part], kv.at[z, x, part]
        return pltpu.make_async_copy(src, dst, insem.at[1])

    @pl.when(c == half)
    def _():
        for d in (1, 3, 2):
            first_k(d).start()

        @pl.when(c == 0)
        def _():
            first_k(0).start()
            keep(1).start()
            keep(2).start()

        @pl.when(c == 1)
        def _():
            for cp in first_v(0):
                cp.start()
            keep(0).start()

        for d in (1, 7, 2, 6, 3, 5, 4):
            for cp in first_v(d):
                cp.start()

        @pl.when(c == 0)
        def _():
            landed(insem.at[1], REST)

        @pl.when(c == 1)
        def _():
            landed(insem.at[1], SPLIT)

    landed(insem.at[0], 10 * 128)
    for j in range(2):
        lay_rows(qq, 0, q_ref.at[0], j * HALF, j)
        lay_rows(oo, 0, g_ref.at[0], j * HALF, j)

    def drain_gather():
        @pl.when(c == 1)
        def _():
            landed(sent.at[1], 28 * SPLIT)
            landed(sent.at[3], NZ * NX * SPLIT)

        @pl.when(c == 0)
        def _():
            landed(sent.at[2], NZ * (NX - 1) * REST)
            landed(sent.at[3], NZ * NX * REST)

        @pl.when((c == half) & (c == 0))
        def _():
            landed(sent.at[0], NX * SPLIT + (NZ - 1) * REST)

        @pl.when((c == half) & (c == 1))
        def _():
            landed(sent.at[0], (NX - 1) * SPLIT + NZ * REST)

        landed(sent.at[4], 8 * 128)
        landed(sent.at[5], 128)

    my_block = span_ref[0, 0, me]

    def index(b, i):
        return (b * NX + i) * 2 + half

    def early(b, i):
        return span_ref[0, 0, index(b, i)] < my_block

    def pick(at_row, b):
        e, both = [], []
        for i in range(NX):
            lo = kv[b, i, at_row:at_row + HALF]
            hi = kv[b, i, at_row + HALF:at_row + 2 * HALF]
            s = early(b, i)
            zero = jnp.zeros_like(lo)
            e.append(lo)
            both.append(jnp.concatenate([jnp.where(s, lo, zero), jnp.where(s, zero, hi)], axis=1))
        return jnp.concatenate(e, axis=0), jnp.concatenate(both, axis=0)

    def softmax_row(n):
        b = row_of(n)

        @pl.when(c == 1)
        def _():
            hand_over(SECOND, n).wait_recv()

        @pl.when(c == 0)
        def _():
            hand_over(FIRST, n).wait_recv()

        ke, ksel = pick(0, b)
        kselbuf[b] = ksel
        s1[b] = dot_nt(ke, qq[:, HD:]) * scale
        s2[b] = dot_nt(ksel, qq[...]) * scale
        ve, vsel = pick(128, b)
        dp1[b] = dot_nt(ve, oo[:, HD:])
        dp2[b] = dot_nt(vsel, oo[...])
        old_e, old_l = state[0:1], state[1:2]
        m_e, m_l = old_e, jnp.maximum(old_l, col_max(s1[b]))
        low = jnp.full((1, SLOTS), NEG, F32)
        high = jnp.full((1, SLOTS), POS, F32)
        for i in range(NX):
            top = col_max(s2[b, i * HALF:(i + 1) * HALF])
            s = early(b, i)
            top = jnp.where(index(b, i) == me, low, top)
            m_e = jnp.maximum(m_e, jnp.where(s, top, low))
            m_l = jnp.maximum(m_l, jnp.where(s, low, top))
        a_e = jnp.exp2(old_e - m_e)
        a_l = jnp.exp2(old_l - m_l)
        l_e, l_l = state[2:3] * a_e, state[3:4] * a_l
        d_e, d_l = state[4:5] * a_e, state[5:6] * a_l
        for i in range(NX):
            part = slice(i * HALF, (i + 1) * HALF)
            p = jnp.exp2(s1[b, part] - m_l)
            s1[b, part] = p
            l_l = l_l + col_sum(p)
            d_l = d_l + col_sum(p * dp1[b, part])
            s = early(b, i)
            top = jnp.where(s, m_e, m_l)
            top = jnp.where(index(b, i) == me, high, top)
            p = jnp.exp2(s2[b, part] - top)
            s2[b, part] = p
            ps = col_sum(p)
            pd = col_sum(p * dp2[b, part])
            zero = jnp.zeros_like(ps)
            l_e = l_e + jnp.where(s, ps, zero)
            l_l = l_l + jnp.where(s, zero, ps)
            d_e = d_e + jnp.where(s, pd, zero)
            d_l = d_l + jnp.where(s, zero, pd)
        for i, v in enumerate((m_e, m_l, l_e, l_l, d_e, d_l)):
            state[i:i + 1] = v
        tops[b, 0:1] = m_e
        tops[b, 1:2] = m_l

    def diagonal():
        key_no = lax.broadcasted_iota(jnp.int32, (HALF, SLOTS), 0)
        tok_no = lax.broadcasted_iota(jnp.int32, (HALF, SLOTS), 1) % HALF
        seen = key_no <= tok_no
        for j in range(2):
            part = slice(j * HALF, (j + 1) * HALF)
            cols = slice(j * HD, (j + 1) * HD)
            s = jnp.where(seen, dot_nt(k_ref[0, part], qq[:, cols]) * scale, NEG)
            top = col_max(s)
            p = jnp.exp2(s - top)
            dp = dot_nt(v_ref[0, part], oo[:, cols])
            diag[2 * j] = p
            diag[2 * j + 1] = dp
            state[j:j + 1] = top
            state[2 + j:3 + j] = col_sum(p)
            state[4 + j:5 + j] = col_sum(p * dp)
            tops[NZ, j:j + 1] = top

    def swap_sums(j):
        return remote(sums_out.at[j], sums_in.at[j], sent.at[5], sums_r.at[0], mate(j))

    LAG = 2
    plans = (
        {
            0: [(v_stage1, n) for n in range(5)],
            1: [(v_stage1, 5), (v_stage1, 6), (v_stage1, 7)] + [(v_stage2, n) for n in range(3)],
            3: [(v_stage2, 3), (v_stage2, 4)],
            5: [(v_stage2, 5), (v_stage2, 6), (v_stage2, 7)],
        },
        {
            0: [(gather_k, 0), (gather_k, 3), (gather_k, 4)],
            1: [(gather_k, 1), (gather_k, 2)],
            5: [(gather_k, 5), (gather_k, 6), (gather_k, 7)],
        },
    )

    def run_plan(i, plans):
        for core in range(2):
            for j, todo in plans[core].items():
                @pl.when((i == j) & (c == core))
                def _():
                    for stage, n in todo:
                        stage(n)

    def gather_step(i, _):
        run_plan(i, plans)

        @pl.when(i == LAG)
        def _():
            landed(pqr.at[0], 8 * 128)
            for kind in range(2):
                for j in range(2):
                    lay_rows((qq, oo)[kind], ROWS, (pq, pg)[kind].at[j], 0, j)

            @pl.when(c == half)
            def _():
                diagonal()

        @pl.when(i >= LAG)
        def _():
            softmax_row(i - LAG)

        return 0

    lax.fori_loop(0, NZ + LAG, gather_step, 0)

    for j in range(2):
        for i in range(3):
            sums_out[j, i:i + 1] = state[2 * i + j:2 * i + j + 1]
        swap_sums(j).start()
    landed(sums_r.at[0], 128)
    for j in range(2):
        m, l, d = (state[2 * i + j:2 * i + j + 1] for i in range(3))
        m2, l2, d2 = (
            jnp.concatenate([sums_in[j, i:i + 1, ROWS:], sums_in[j, i:i + 1, :ROWS]], axis=1)
            for i in range(3)
        )
        top = jnp.maximum(m, m2)
        a, a2 = jnp.exp2(m - top), jnp.exp2(m2 - top)
        r = 1.0 / (l * a + l2 * a2)
        state[j:j + 1] = top
        state[2 + j:3 + j] = r
        state[4 + j:5 + j] = (d * a + d2 * a2) * r

    @pl.when(c == half)
    def _():
        for j in range(2):
            part = slice(j * HALF, (j + 1) * HALF)
            cols = slice(j * HD, (j + 1) * HD)
            m, r, d = state[j:j + 1], state[2 + j:3 + j], state[4 + j:5 + j]
            p = diag[2 * j] * (jnp.exp2(tops[NZ, j:j + 1] - m) * r)
            ds = (p * (diag[2 * j + 1] - d)).astype(BF16)
            dq2[cols] = dot_tn(k_ref[0, part], ds)
            diag[2 * j, :, :HD] = dot_nn(ds, qq[:, cols]) * INV_ROOT
            diag[2 * j, :, HD:2 * HD] = dot_nn(p.astype(BF16), oo[:, cols])

    def give(part, m):
        b = back_row(m)
        return remote(pkv.at[b, :, part], sib.at[b, :, part], sent.at[6], sibr.at[m], sibling)

    def gradient_row(m):
        b = back_row(m)
        r_e, r_l, d_e, d_l = state[2:3], state[3:4], state[4:5], state[5:6]
        f_e = jnp.exp2(tops[b, 0:1] - state[0:1]) * r_e
        f_l = jnp.exp2(tops[b, 1:2] - state[1:2]) * r_l
        ke = jnp.concatenate([kv[b, i, :HALF] for i in range(NX)], axis=0)
        ksel = kselbuf[b]
        p1 = s1[b] * f_l
        ds1 = (p1 * (dp1[b] - d_l)).astype(BF16)
        p1 = p1.astype(BF16)
        p2s, ds2s = [], []
        for i in range(NX):
            part = slice(i * HALF, (i + 1) * HALF)
            s = early(b, i)
            p = s2[b, part] * jnp.where(s, f_e, f_l)
            ds2s.append((p * (dp2[b, part] - jnp.where(s, d_e, d_l))).astype(BF16))
            p2s.append(p.astype(BF16))
        p2 = jnp.concatenate(p2s, axis=0)
        ds2 = jnp.concatenate(ds2s, axis=0)
        v1 = dot_nn(p1, oo[:, HD:])
        v2 = dot_nn(p2, oo[...])
        k1 = dot_nn(ds1, qq[:, HD:]) * INV_ROOT
        k2 = dot_nn(ds2, qq[...]) * INV_ROOT
        dql[...] += dot_tn(ke, ds1)
        dq2[...] += dot_tn(ksel, ds2)
        for i in range(NX):
            part = slice(i * HALF, (i + 1) * HALF)
            s = early(b, i)
            zero = jnp.zeros((HALF, HD), F32)
            k_lo, k_hi, v_lo, v_hi = (slice(j * HALF, (j + 1) * HALF) for j in range(4))
            pkv[b, i, v_lo] = (v1[part] + jnp.where(s, v2[part, :HD], zero)).astype(BF16)
            pkv[b, i, v_hi] = jnp.where(s, zero, v2[part, HD:]).astype(BF16)
            pkv[b, i, k_lo] = (k1[part] + jnp.where(s, k2[part, :HD], zero)).astype(BF16)
            pkv[b, i, k_hi] = jnp.where(s, zero, k2[part, HD:]).astype(BF16)

        @pl.when((m == NZ - 1) & (c == half))
        def _():
            for j in range(2):
                part = slice(j * HALF, (j + 1) * HALF)
                v_part = slice(128 + j * HALF, 128 + (j + 1) * HALF)
                pkv[z, x, part] = (
                    pkv[z, x, part].astype(F32) + diag[2 * j, :, :HD]).astype(BF16)
                pkv[z, x, v_part] = (
                    pkv[z, x, v_part].astype(F32) + diag[2 * j, :, HD:2 * HD]).astype(BF16)

        @pl.when(c == 1)
        def _():
            give(SECOND, m).start()

        @pl.when(c == 0)
        def _():
            give(FIRST, m).start()

    def add_up(row, col, part, *terms):
        total = pkv[row, col, part].astype(F32) + sib[row, col, part].astype(F32)
        for ref, i in terms:
            total = total + ref[i].astype(F32)
        return total

    def k_back(way, k, j):
        step = 1 if way == 0 else -1
        far = (1, 2, 1, 2)[k - 1]
        return remote(pkv.at[zoff(step * k), xoff(j), FIRST], rr.at[way, k - 1, j],
                      sent.at[7], rrsem.at[8 + j if k < 3 else way * 4 + j], at(zoff(step * far), x, 1))

    def k_across(j):
        return remote(pkv.at[z, xoff(j), FIRST], xr.at[j], sent.at[10], xrsem.at[0], at(z, xoff(j), 1))

    def k_hop(m):
        give(FIRST, m).wait_recv()
        d = BACK[m]
        k = abs(d)
        if k == 4:
            plan = [(w, j, ()) for i in range(2) for w, j in ((0, SETS[0][i]), (1, SETS[1][i]))]
        else:
            w = 0 if d > 0 else 1
            if k == 3:
                plan = [(w, j, ()) for j in ACROSS]
            elif k == 2:
                plan = [(w, j, (3, 4) if j in SETS[w] else (3,)) for j in SETS[1 - w] + SETS[w]]
            else:
                plan = [(w, j, ()) for j in ACROSS]
        for w, j, has in plan:
            row, col = zoff(d), xoff(j)
            terms = []
            if has:
                landed(rrsem.at[w * 4 + j], len(has) * SPLIT)
            for q in has:
                terms.append((rr, (w, q - 1, j)))
            pkv[row, col, FIRST] = add_up(row, col, FIRST, *terms).astype(BF16)
            k_back(w, k, j).start()

    def k_last():
        give(FIRST, NZ - 1).wait_recv()
        for j in (2, 1, 3, 0):
            landed(rrsem.at[8 + j], 4 * SPLIT)
            terms = []
            for w in range(2):
                for k in (1, 2):
                    terms.append((rr, (w, k - 1, j)))
            total = add_up(z, xoff(j), FIRST, *terms)
            if j:
                pkv[z, xoff(j), FIRST] = total.astype(BF16)
                k_across(j).start()
        landed(xrsem.at[0], (NX - 1) * SPLIT)
        for j in range(1, NX):
            total = total + xr[j].astype(F32)
        ysum[FIRST] = total.astype(BF16)

    def cx_part(d, m):
        return pl.ds((d * NZ + m) * REST, REST)

    def v_back(d, m):
        return remote(pkv.at[zoff(BACK[m]), xoff(d), SECOND], cx.at[cx_part(d, m)], sent.at[8],
                      c1r.at[m], at(z, xoff(d), 0))

    def v_z(m):
        d = BACK[m]
        return remote(pkv.at[zoff(d), x, SECOND], zr.at[m], sent.at[9], zrsem.at[0], at(zoff(d), x, 0))

    def v_out(m):
        give(SECOND, m).wait_recv()
        for d in (2, 1, 3):
            row, col = zoff(BACK[m]), xoff(d)
            pkv[row, col, SECOND] = add_up(row, col, SECOND).astype(BF16)
            v_back(d, m).start()

    def v_in(m):
        row = zoff(BACK[m])
        landed(c1r.at[m], (NX - 1) * REST)
        terms = [(cx, cx_part(d, m)) for d in range(1, NX)]
        pkv[row, x, SECOND] = add_up(row, x, SECOND, *terms).astype(BF16)
        if m < NZ - 1:
            v_z(m).start()

    def v_last():
        total = pkv[z, x, SECOND].astype(F32)
        landed(zrsem.at[0], (NZ - 1) * REST)
        for m in range(NZ - 1):
            total = total + zr[m].astype(F32)
        ysum[SECOND] = total.astype(BF16)

    back = (
        {m: [(v_out, m - 2)] + ([(v_in, m - 6)] if m >= 6 else []) for m in range(2, NZ)},
        {m: [(k_hop, m - 2)] for m in range(2, NZ - 1)},
    )

    def drain_scatter():
        @pl.when(c == 1)
        def _():
            landed(sent.at[7], 28 * SPLIT)
            landed(sent.at[10], (NX - 1) * SPLIT)
            landed(sent.at[6], NZ * NX * REST)
            landed(sent.at[11], NT * SPLIT)

        @pl.when(c == 0)
        def _():
            landed(sent.at[8], NZ * (NX - 1) * REST)
            landed(sent.at[9], (NZ - 1) * REST)
            landed(sent.at[6], NZ * NX * SPLIT)
            landed(sent.at[11], NT * REST)

    def scatter_step(m, _):
        gradient_row(m)
        run_plan(m, back)
        return 0

    lax.fori_loop(0, NZ, scatter_step, 0)

    @pl.when(c == 0)
    def _():
        v_out(6)
        v_out(7)
        for m in range(2, 5):
            v_in(m)

    @pl.when(c == 1)
    def _():
        k_hop(5)
        k_hop(6)

    for j, acc in enumerate((dq2[0:HD], dq2[HD:2 * HD] + dql[...])):
        g = (acc * INV_ROOT).T.astype(BF16)
        for i in range(2):
            for h in range(HEADS):
                at_row = i * ROWS + h * HALF
                dqst[i, j * HALF:(j + 1) * HALF, h * HD:(h + 1) * HD] = g[at_row:at_row + HALF]

    def dq_copy(i):
        if i == 0:
            return remote(dqst.at[0], dqr.at[0], sent.at[12], dqsr.at[0], other(t, c))
        part = pl.ds((i - 1) * HALF, HALF)
        return remote(dqst.at[1, part], dqr.at[1, part], sent.at[12], dqsr.at[0],
                      other(mates[i - 1], c))

    for i in range(3):
        dq_copy(i).start()

    @pl.when(c == 1)
    def _():
        k_last()

    @pl.when(c == 0)
    def _():
        for m in range(5, NZ):
            v_in(m)
        v_last()

    def last(tt, part):
        return remote(ysum.at[part], yr.at[t // 2, part], sent.at[11], yrsem.at[0],
                      other(tt, half))

    for core, part in ((0, SECOND), (1, FIRST)):
        @pl.when(c == core)
        def _():
            for tt in range(NT):
                last(tt, part).start()

    drain_gather()
    drain_scatter()

    landed(dqsr.at[0], 8 * 128)
    landed(yrsem.at[0], 2 * BLOCK)
    landed(sent.at[12], 8 * 128)


def last_sums(dqr, yr, dq_out, dk_out, dv_out):
    dq_out[0] = (dqr[0].astype(F32) + dqr[1].astype(F32)).astype(BF16)
    for kind, out in ((0, dk_out), (1, dv_out)):
        part = slice(kind * 128, (kind + 1) * 128)
        out[0] = (yr[0, part].astype(F32) + yr[1, part].astype(F32)).astype(BF16)


def per_device(queries, keys, values, grad_out, span_order):
    vmem = pl.BlockSpec(memory_space=pltpu.VMEM)
    hbm = pl.BlockSpec(memory_space=pl.ANY)
    dma = pltpu.SemaphoreType.DMA

    def plane():
        return pltpu.VMEM((NZ, NX, BLOCK, HD), BF16)

    scratch = [
        pltpu.VMEM(queries.shape, BF16),
        pltpu.VMEM(keys.shape, BF16),
        pltpu.VMEM(values.shape, BF16),
        pltpu.VMEM(grad_out.shape, BF16),
        plane(),
        pltpu.VMEM((NZ, KEYS, SLOTS), F32),
        pltpu.VMEM((NZ, KEYS, SLOTS), F32),
        pltpu.VMEM((NZ, KEYS, SLOTS), F32),
        pltpu.VMEM((NZ, KEYS, SLOTS), F32),
        pltpu.VMEM((NZ, KEYS, 2 * HD), BF16),
        pltpu.VMEM((SLOTS, 2 * HD), BF16),
        pltpu.VMEM((SLOTS, 2 * HD), BF16),
        pltpu.VMEM((2, HALF, HEADS * HD), BF16),
        pltpu.VMEM((2, HALF, HEADS * HD), BF16),
        pltpu.VMEM((HD, SLOTS), F32),
        pltpu.VMEM((2 * HD, SLOTS), F32),
        pltpu.VMEM((2, 128, HEADS * HD), BF16),
        pltpu.VMEM((8, SLOTS), F32),
        pltpu.VMEM((NZ + 1, 8, SLOTS), F32),
        pltpu.VMEM((4, HALF, SLOTS), F32),
        pltpu.VMEM((2, 8, SLOTS), F32),
        pltpu.VMEM((2, 8, SLOTS), F32),
        plane(),
        plane(),
        pltpu.VMEM((2, 4, NX, SPLIT, HD), BF16),
        pltpu.VMEM((NX * NZ * REST, HD), BF16),
        pltpu.VMEM((NZ, REST, HD), BF16),
        pltpu.VMEM((NX, SPLIT, HD), BF16),
        pltpu.VMEM((BLOCK, HD), BF16),
        dma((2,)), dma((13,)),
        dma((NX,)), dma((NZ,)), dma((13,)), dma((NZ,)), dma((NZ,)),
        dma((1,)), dma((1,)),
        dma((NZ,)), dma((12,)), dma((NZ,)), dma((1,)), dma((1,)),
        dma((1,)), dma((1,)),
    ]
    arrived = pl.pallas_call(
        kernel,
        out_shape=(
            jax.ShapeDtypeStruct((2, 128, HEADS * HD), BF16),
            jax.ShapeDtypeStruct((2, BLOCK, HD), BF16),
        ),
        in_specs=[hbm, hbm, hbm, hbm, pl.BlockSpec(memory_space=pltpu.SMEM)],
        out_specs=(hbm, hbm),
        scratch_shapes=scratch,
        compiler_params=pltpu.CompilerParams(
            collective_id=1, has_side_effects=True, vmem_limit_bytes=56 * 2**20
        ),
        name="attention_backward",
    )(queries, keys, values, grad_out, jnp.swapaxes(span_order, 1, 2))
    return pl.pallas_call(
        last_sums,
        out_shape=tuple(jax.ShapeDtypeStruct(a.shape, BF16) for a in (queries, keys, values)),
        in_specs=[vmem, vmem],
        out_specs=(vmem, vmem, vmem),
        name="last_sums",
    )(*arrived)


def solution(mesh):
    return jax.shard_map(
        per_device,
        mesh=mesh,
        in_specs=(
            P("pipe", "ctx", "tp"),
            P("pipe", "ctx", None),
            P("pipe", "ctx", None),
            P("pipe", "ctx", "tp"),
            P("pipe", None, None),
        ),
        out_specs=(P("pipe", "ctx", "tp"), P("pipe", "ctx", None), P("pipe", "ctx", None)),
        check_vma=False,
    )
```

```python
import functools

import jax
import jax.numpy as jnp
from jax import lax
from jax.experimental import pallas as pl
from jax.experimental.pallas import tpu as pltpu
from jax.sharding import PartitionSpec as P

MESH = pl.DeviceIdType.MESH
F32 = jnp.float32
BF16 = jnp.bfloat16

NZ = 8
NX = 4
NT = 4
HEADS = 4
HALF = 64
HD = 128
ROWS = HEADS * HALF
SLOTS = 2 * ROWS
KEYS = NX * HALF
BLOCK = 256
SPLIT = 112
REST = BLOCK - SPLIT
FIRST = pl.ds(0, SPLIT)
SECOND = pl.ds(SPLIT, REST)
INV_ROOT = HD ** (-0.5)
LOG2E = 1.4426950408889634
NEG = -1e30
POS = 1e30
ORDER = (0, 1, -1, 2, -2, 3, -3, 4)
BACK = (4, -3, 3, -1, 1, -2, 2, 0)
ACROSS = (0, 1, 3, 2)
SETS = ((0, 1), (3, 2))


def dot_nt(a, b):
    return lax.dot_general(a, b, (((1,), (1,)), ((), ())), preferred_element_type=F32)


def dot_nn(a, b):
    return jnp.dot(a, b, preferred_element_type=F32)


def dot_tn(a, b):
    return lax.dot_general(a, b, (((0,), (0,)), ((), ())), preferred_element_type=F32)


def col_sum(v):
    return jnp.sum(v, axis=0, keepdims=True)


def col_max(v):
    return jnp.max(v, axis=0, keepdims=True)


def kernel(
    q_hbm, k_hbm, v_hbm, g_hbm, span_ref,
    dqr, yr,
    q_ref, k_ref, v_ref, g_ref, kv, s1, s2, dp1, dp2, kselbuf, qq, oo, pq, pg, dql, dq2, dqst,
    state, tops, diag, sums_out, sums_in,
    pkv, sib, rr, cx, zr, xr, ysum,
    insem, sent, p1kr, p1vr, zkr, x1r, d2dr, pqr, sums_r, sibr, rrsem, c1r, zrsem, xrsem,
    yrsem, dqsr,
):
    pipe = lax.axis_index("pipe")
    me = lax.axis_index("ctx")
    t = lax.axis_index("tp")
    z = me // (2 * NX)
    x = (me // 2) % NX
    c = me % 2
    half = t % 2
    mates = (t + 1 - 2 * half, lax.rem(t + 2 * half + NT - 1, NT))

    def at(zz, xx, cc):
        return (pipe, (zz * NX + xx) * 2 + cc, t)

    def zoff(d):
        return lax.rem(z + d + NZ, NZ)

    def xoff(d):
        return lax.rem(x + d + NX, NX)

    def row_of(n):
        return zoff(((n + 1) // 2) * (2 * (n % 2) - 1))

    def mate(j):
        return (pipe, me, mates[j])

    def back_row(m):
        d = 0
        for i, far in enumerate(BACK):
            d = jnp.where(m == i, far, d)
        return zoff(d)

    def other(tt, cc):
        return (1 - pipe, (z * NX + x) * 2 + cc, tt)

    sibling = at(z, x, 1 - c)

    def remote(src, dst, ssem, rsem, dev):
        return pltpu.make_async_remote_copy(
            src_ref=src, dst_ref=dst, send_sem=ssem, recv_sem=rsem,
            device_id=dev, device_id_type=MESH,
        )

    def take(i):
        src = (q_hbm, g_hbm, k_hbm, v_hbm)[i]
        return pltpu.make_async_copy(src, (q_ref, g_ref, k_ref, v_ref)[i], insem.at[0])

    for i in range(4):
        take(i).start()

    barrier = pltpu.get_barrier_semaphore()
    count = 0

    def greet(dev):
        pl.semaphore_signal(barrier, inc=1, device_id=dev, device_id_type=MESH)

    greet(sibling)
    count += 1
    for cc in range(2):
        for d in range(1, NX):
            greet(at(z, xoff(d), cc))
            count += 1
        for d in range(1, NZ):
            greet(at(zoff(d), x, cc))
            count += 1
        for tt in range(NT):
            greet(other(tt, cc))
            count += 1
    for j in range(2):
        greet(mate(j))
        count += 1

    def lay_rows(dst, base, src, lo, j):
        for h in range(HEADS):
            dst[base + h * HALF:base + (h + 1) * HALF, j * HD:(j + 1) * HD] = src[
                lo:lo + HALF, h * HD:(h + 1) * HD]

    low = jnp.full((1, SLOTS), NEG, F32)
    state[...] = jnp.zeros_like(state)
    sums_out[...] = jnp.zeros_like(sums_out)
    for j in range(2):
        state[j:j + 1] = low
    dql[...] = jnp.zeros_like(dql)
    dq2[...] = jnp.zeros_like(dq2)
    scale = INV_ROOT * LOG2E

    pl.semaphore_wait(barrier, count)

    def swap_rows(j, kind):
        src = (q_hbm, g_hbm)[kind].at[0, pl.ds(j * HALF, HALF)]
        dst = (pq, pg)[kind].at[j]
        return remote(src, dst, sent.at[4], pqr.at[0], mate(j))

    def first_k(d):
        return remote(k_hbm.at[0, FIRST], kv.at[z, x, FIRST], sent.at[0], p1kr.at[d],
                      at(z, xoff(d), 1))

    def first_v(d):
        there = at(zoff(d), x, 0)
        keys = remote(k_hbm.at[0, pl.ds(SPLIT, 128 - SPLIT)], kv.at[z, x, pl.ds(SPLIT, 128 - SPLIT)],
                      sent.at[0], p1vr.at[d], there)
        values = remote(v_hbm.at[0], kv.at[z, x, pl.ds(128, 128)], sent.at[0], p1vr.at[d], there)
        return keys, values

    def k_slot(way, k, j):
        return {1: way, 2: 5 + way * 4 + j, 3: 2 + way, 4: 4}[k]

    def k_send(way, k, j):
        step = 1 if way == 0 else -1
        back, far = ((0, 1), (0, 2), (2, 1), (2, 2))[k - 1]
        ref = kv.at[zoff(-step * back), xoff(j), FIRST]
        return remote(ref, ref, sent.at[1], zkr.at[k_slot(way, k, j)],
                      at(zoff(step * far), x, 1))

    def v_x(d, n):
        ref = kv.at[zoff(ORDER[n]), x, SECOND]
        return remote(ref, ref, sent.at[2], x1r.at[n], at(z, xoff(d), 0))

    def hand_over(part, n):
        ref = kv.at[row_of(n), :, part]
        return remote(ref, ref, sent.at[3], d2dr.at[n], sibling)

    def landed(sem, rows):
        ref = cx.at[pl.ds(0, rows)]
        pltpu.make_async_copy(ref, ref, sem).wait()

    def gather_k(n):
        d = ORDER[n]
        k = abs(d)
        if k == 0:
            for j in ACROSS:
                src = (NX - j) % NX
                if src:
                    landed(p1kr.at[src], SPLIT)
                else:
                    @pl.when(half == 0)
                    def _():
                        landed(p1kr.at[0], SPLIT)
                for w in range(2):
                    k_send(w, 2, j).start()
                    k_send(w, 1, j).start()
        elif k == 2:
            w = 1 if d > 0 else 0
            for j in ACROSS:
                landed(zkr.at[k_slot(w, 2, j)], SPLIT)
                if j in SETS[w]:
                    k_send(w, 4, j).start()
                k_send(w, 3, j).start()
        else:
            landed(zkr.at[k_slot(1 if d > 0 else 0, k, 0)], NX * SPLIT)
        hand_over(FIRST, n).start()

    def v_stage1(n):
        d = ORDER[n]
        if d:
            landed(p1vr.at[-d % NZ], REST)
        else:
            @pl.when(half == 1)
            def _():
                landed(p1vr.at[0], REST)
        for dx in (1, 3, 2):
            v_x(dx, n).start()

    def v_stage2(n):
        landed(x1r.at[n], (NX - 1) * REST)
        hand_over(SECOND, n).start()

    def keep(i):
        part = pl.ds(0, SPLIT) if i == 0 else pl.ds(SPLIT, 128 - SPLIT)
        if i == 2:
            src, dst = v_hbm.at[0], kv.at[z, x, pl.ds(128, 128)]
        else:
            src, dst = k_hbm.at[0, part], kv.at[z, x, part]
        return pltpu.make_async_copy(src, dst, insem.at[1])

    @pl.when(c == half)
    def _():
        for d in (1, 3, 2):
            first_k(d).start()

        @pl.when(c == 0)
        def _():
            first_k(0).start()
            keep(1).start()
            keep(2).start()

        @pl.when(c == 1)
        def _():
            for cp in first_v(0):
                cp.start()
            keep(0).start()

        for d in (1, 7, 2, 6, 3, 5, 4):
            for cp in first_v(d):
                cp.start()

    for kind in range(2):
        for j in range(2):
            swap_rows(j, kind).start()

    @pl.when(c == half)
    def _():
        @pl.when(c == 0)
        def _():
            landed(insem.at[1], REST)

        @pl.when(c == 1)
        def _():
            landed(insem.at[1], SPLIT)

    landed(insem.at[0], 10 * 128)
    for j in range(2):
        lay_rows(qq, 0, q_ref.at[0], j * HALF, j)
        lay_rows(oo, 0, g_ref.at[0], j * HALF, j)

    def drain_gather():
        @pl.when(c == 1)
        def _():
            landed(sent.at[1], 28 * SPLIT)
            landed(sent.at[3], NZ * NX * SPLIT)

        @pl.when(c == 0)
        def _():
            landed(sent.at[2], NZ * (NX - 1) * REST)
            landed(sent.at[3], NZ * NX * REST)

        @pl.when((c == half) & (c == 0))
        def _():
            landed(sent.at[0], NX * SPLIT + (NZ - 1) * REST)

        @pl.when((c == half) & (c == 1))
        def _():
            landed(sent.at[0], (NX - 1) * SPLIT + NZ * REST)

        landed(sent.at[4], 8 * 128)
        landed(sent.at[5], 128)

    my_block = span_ref[0, 0, me]

    def index(b, i):
        return (b * NX + i) * 2 + half

    def early(b, i):
        return span_ref[0, 0, index(b, i)] < my_block

    def pick(at_row, b):
        e, both = [], []
        for i in range(NX):
            lo = kv[b, i, at_row:at_row + HALF]
            hi = kv[b, i, at_row + HALF:at_row + 2 * HALF]
            s = early(b, i)
            zero = jnp.zeros_like(lo)
            e.append(lo)
            both.append(jnp.concatenate([jnp.where(s, lo, zero), jnp.where(s, zero, hi)], axis=1))
        return jnp.concatenate(e, axis=0), jnp.concatenate(both, axis=0)

    def softmax_row(n):
        b = row_of(n)

        @pl.when(c == 1)
        def _():
            hand_over(SECOND, n).wait_recv()

        @pl.when(c == 0)
        def _():
            hand_over(FIRST, n).wait_recv()

        ke, ksel = pick(0, b)
        kselbuf[b] = ksel
        s1[b] = dot_nt(ke, qq[:, HD:]) * scale
        s2[b] = dot_nt(ksel, qq[...]) * scale
        ve, vsel = pick(128, b)
        dp1[b] = dot_nt(ve, oo[:, HD:])
        dp2[b] = dot_nt(vsel, oo[...])
        old_e, old_l = state[0:1], state[1:2]
        m_e, m_l = old_e, jnp.maximum(old_l, col_max(s1[b]))
        low = jnp.full((1, SLOTS), NEG, F32)
        high = jnp.full((1, SLOTS), POS, F32)
        for i in range(NX):
            top = col_max(s2[b, i * HALF:(i + 1) * HALF])
            s = early(b, i)
            top = jnp.where(index(b, i) == me, low, top)
            m_e = jnp.maximum(m_e, jnp.where(s, top, low))
            m_l = jnp.maximum(m_l, jnp.where(s, low, top))
        a_e = jnp.exp2(old_e - m_e)
        a_l = jnp.exp2(old_l - m_l)
        l_e, l_l = state[2:3] * a_e, state[3:4] * a_l
        d_e, d_l = state[4:5] * a_e, state[5:6] * a_l
        for i in range(NX):
            part = slice(i * HALF, (i + 1) * HALF)
            p = jnp.exp2(s1[b, part] - m_l)
            s1[b, part] = p
            l_l = l_l + col_sum(p)
            d_l = d_l + col_sum(p * dp1[b, part])
            s = early(b, i)
            top = jnp.where(s, m_e, m_l)
            top = jnp.where(index(b, i) == me, high, top)
            p = jnp.exp2(s2[b, part] - top)
            s2[b, part] = p
            ps = col_sum(p)
            pd = col_sum(p * dp2[b, part])
            zero = jnp.zeros_like(ps)
            l_e = l_e + jnp.where(s, ps, zero)
            l_l = l_l + jnp.where(s, zero, ps)
            d_e = d_e + jnp.where(s, pd, zero)
            d_l = d_l + jnp.where(s, zero, pd)
        for i, v in enumerate((m_e, m_l, l_e, l_l, d_e, d_l)):
            state[i:i + 1] = v
        tops[b, 0:1] = m_e
        tops[b, 1:2] = m_l

    def diagonal():
        key_no = lax.broadcasted_iota(jnp.int32, (HALF, SLOTS), 0)
        tok_no = lax.broadcasted_iota(jnp.int32, (HALF, SLOTS), 1) % HALF
        seen = key_no <= tok_no
        for j in range(2):
            part = slice(j * HALF, (j + 1) * HALF)
            cols = slice(j * HD, (j + 1) * HD)
            s = jnp.where(seen, dot_nt(k_ref[0, part], qq[:, cols]) * scale, NEG)
            top = col_max(s)
            p = jnp.exp2(s - top)
            dp = dot_nt(v_ref[0, part], oo[:, cols])
            diag[2 * j] = p
            diag[2 * j + 1] = dp
            state[j:j + 1] = top
            state[2 + j:3 + j] = col_sum(p)
            state[4 + j:5 + j] = col_sum(p * dp)
            tops[NZ, j:j + 1] = top

    def swap_sums(j):
        return remote(sums_out.at[j], sums_in.at[j], sent.at[5], sums_r.at[0], mate(j))

    LAG = 2
    plans = (
        {
            0: [(v_stage1, n) for n in range(5)],
            1: [(v_stage1, 5), (v_stage1, 6), (v_stage1, 7)] + [(v_stage2, n) for n in range(3)],
            3: [(v_stage2, 3), (v_stage2, 4)],
            5: [(v_stage2, 5), (v_stage2, 6), (v_stage2, 7)],
        },
        {
            0: [(gather_k, 0), (gather_k, 3), (gather_k, 4)],
            1: [(gather_k, 1), (gather_k, 2)],
            6: [(gather_k, 5), (gather_k, 6), (gather_k, 7)],
        },
    )

    def run_plan(i, plans):
        for core in range(2):
            for j, todo in plans[core].items():
                @pl.when((i == j) & (c == core))
                def _():
                    for stage, n in todo:
                        stage(n)

    def gather_step(i, _):
        run_plan(i, plans)

        @pl.when(i == LAG)
        def _():
            landed(pqr.at[0], 8 * 128)
            for kind in range(2):
                for j in range(2):
                    lay_rows((qq, oo)[kind], ROWS, (pq, pg)[kind].at[j], 0, j)

            @pl.when(c == half)
            def _():
                diagonal()

        @pl.when(i >= LAG)
        def _():
            softmax_row(i - LAG)

        return 0

    lax.fori_loop(0, NZ + LAG, gather_step, 0)

    for j in range(2):
        for i in range(3):
            sums_out[j, i:i + 1] = state[2 * i + j:2 * i + j + 1]
        swap_sums(j).start()
    landed(sums_r.at[0], 128)
    for j in range(2):
        m, l, d = (state[2 * i + j:2 * i + j + 1] for i in range(3))
        m2, l2, d2 = (
            jnp.concatenate([sums_in[j, i:i + 1, ROWS:], sums_in[j, i:i + 1, :ROWS]], axis=1)
            for i in range(3)
        )
        top = jnp.maximum(m, m2)
        a, a2 = jnp.exp2(m - top), jnp.exp2(m2 - top)
        r = 1.0 / (l * a + l2 * a2)
        state[j:j + 1] = top
        state[2 + j:3 + j] = r
        state[4 + j:5 + j] = (d * a + d2 * a2) * r

    @pl.when(c == half)
    def _():
        for j in range(2):
            part = slice(j * HALF, (j + 1) * HALF)
            cols = slice(j * HD, (j + 1) * HD)
            m, r, d = state[j:j + 1], state[2 + j:3 + j], state[4 + j:5 + j]
            p = diag[2 * j] * (jnp.exp2(tops[NZ, j:j + 1] - m) * r)
            ds = (p * (diag[2 * j + 1] - d)).astype(BF16)
            dq2[cols] = dot_tn(k_ref[0, part], ds)
            diag[2 * j, :, :HD] = dot_nn(ds, qq[:, cols]) * INV_ROOT
            diag[2 * j, :, HD:2 * HD] = dot_nn(p.astype(BF16), oo[:, cols])

    def give(part, m):
        b = back_row(m)
        return remote(pkv.at[b, :, part], sib.at[b, :, part], sent.at[6], sibr.at[m], sibling)

    def gradient_row(m):
        b = back_row(m)
        r_e, r_l, d_e, d_l = state[2:3], state[3:4], state[4:5], state[5:6]
        f_e = jnp.exp2(tops[b, 0:1] - state[0:1]) * r_e
        f_l = jnp.exp2(tops[b, 1:2] - state[1:2]) * r_l
        ke = jnp.concatenate([kv[b, i, :HALF] for i in range(NX)], axis=0)
        ksel = kselbuf[b]
        p1 = s1[b] * f_l
        ds1 = (p1 * (dp1[b] - d_l)).astype(BF16)
        p1 = p1.astype(BF16)
        p2s, ds2s = [], []
        for i in range(NX):
            part = slice(i * HALF, (i + 1) * HALF)
            s = early(b, i)
            p = s2[b, part] * jnp.where(s, f_e, f_l)
            ds2s.append((p * (dp2[b, part] - jnp.where(s, d_e, d_l))).astype(BF16))
            p2s.append(p.astype(BF16))
        p2 = jnp.concatenate(p2s, axis=0)
        ds2 = jnp.concatenate(ds2s, axis=0)
        v1 = dot_nn(p1, oo[:, HD:])
        v2 = dot_nn(p2, oo[...])
        k1 = dot_nn(ds1, qq[:, HD:]) * INV_ROOT
        k2 = dot_nn(ds2, qq[...]) * INV_ROOT
        dql[...] += dot_tn(ke, ds1)
        dq2[...] += dot_tn(ksel, ds2)
        for i in range(NX):
            part = slice(i * HALF, (i + 1) * HALF)
            s = early(b, i)
            zero = jnp.zeros((HALF, HD), F32)
            k_lo, k_hi, v_lo, v_hi = (slice(j * HALF, (j + 1) * HALF) for j in range(4))
            pkv[b, i, v_lo] = (v1[part] + jnp.where(s, v2[part, :HD], zero)).astype(BF16)
            pkv[b, i, v_hi] = jnp.where(s, zero, v2[part, HD:]).astype(BF16)
            pkv[b, i, k_lo] = (k1[part] + jnp.where(s, k2[part, :HD], zero)).astype(BF16)
            pkv[b, i, k_hi] = jnp.where(s, zero, k2[part, HD:]).astype(BF16)

        @pl.when((m == NZ - 1) & (c == half))
        def _():
            for j in range(2):
                part = slice(j * HALF, (j + 1) * HALF)
                v_part = slice(128 + j * HALF, 128 + (j + 1) * HALF)
                pkv[z, x, part] = (
                    pkv[z, x, part].astype(F32) + diag[2 * j, :, :HD]).astype(BF16)
                pkv[z, x, v_part] = (
                    pkv[z, x, v_part].astype(F32) + diag[2 * j, :, HD:2 * HD]).astype(BF16)

        @pl.when(c == 1)
        def _():
            give(SECOND, m).start()

        @pl.when(c == 0)
        def _():
            give(FIRST, m).start()

    def add_up(row, col, part, *terms):
        total = pkv[row, col, part].astype(F32) + sib[row, col, part].astype(F32)
        for ref, i in terms:
            total = total + ref[i].astype(F32)
        return total

    def k_back(way, k, j):
        step = 1 if way == 0 else -1
        far = (1, 2, 1, 2)[k - 1]
        return remote(pkv.at[zoff(step * k), xoff(j), FIRST], rr.at[way, k - 1, j],
                      sent.at[7], rrsem.at[8 + j if k < 3 else way * 4 + j], at(zoff(step * far), x, 1))

    def k_across(j):
        return remote(pkv.at[z, xoff(j), FIRST], xr.at[j], sent.at[10], xrsem.at[0], at(z, xoff(j), 1))

    def k_hop(m):
        give(FIRST, m).wait_recv()
        d = BACK[m]
        k = abs(d)
        if k == 4:
            plan = [(w, j, ()) for i in range(2) for w, j in ((0, SETS[0][i]), (1, SETS[1][i]))]
        else:
            w = 0 if d > 0 else 1
            if k == 3:
                plan = [(w, j, ()) for j in ACROSS]
            elif k == 2:
                plan = [(w, j, (3, 4) if j in SETS[w] else (3,)) for j in SETS[1 - w] + SETS[w]]
            else:
                plan = [(w, j, ()) for j in ACROSS]
        for w, j, has in plan:
            row, col = zoff(d), xoff(j)
            terms = []
            if has:
                landed(rrsem.at[w * 4 + j], len(has) * SPLIT)
            for q in has:
                terms.append((rr, (w, q - 1, j)))
            pkv[row, col, FIRST] = add_up(row, col, FIRST, *terms).astype(BF16)
            k_back(w, k, j).start()

    def k_last():
        give(FIRST, NZ - 1).wait_recv()
        for j in (2, 1, 3, 0):
            landed(rrsem.at[8 + j], 4 * SPLIT)
            terms = []
            for w in range(2):
                for k in (1, 2):
                    terms.append((rr, (w, k - 1, j)))
            total = add_up(z, xoff(j), FIRST, *terms)
            if j:
                pkv[z, xoff(j), FIRST] = total.astype(BF16)
                k_across(j).start()
        landed(xrsem.at[0], (NX - 1) * SPLIT)
        for j in range(1, NX):
            total = total + xr[j].astype(F32)
        ysum[FIRST] = total.astype(BF16)

    def cx_part(d, m):
        return pl.ds((d * NZ + m) * REST, REST)

    def v_back(d, m):
        return remote(pkv.at[zoff(BACK[m]), xoff(d), SECOND], cx.at[cx_part(d, m)], sent.at[8],
                      c1r.at[m], at(z, xoff(d), 0))

    def v_z(m):
        d = BACK[m]
        return remote(pkv.at[zoff(d), x, SECOND], zr.at[m], sent.at[9], zrsem.at[0], at(zoff(d), x, 0))

    def v_out(m):
        give(SECOND, m).wait_recv()
        for d in (2, 1, 3):
            row, col = zoff(BACK[m]), xoff(d)
            pkv[row, col, SECOND] = add_up(row, col, SECOND).astype(BF16)
            v_back(d, m).start()

    def v_in(m):
        row = zoff(BACK[m])
        landed(c1r.at[m], (NX - 1) * REST)
        terms = [(cx, cx_part(d, m)) for d in range(1, NX)]
        pkv[row, x, SECOND] = add_up(row, x, SECOND, *terms).astype(BF16)
        if m < NZ - 1:
            v_z(m).start()

    def v_last():
        total = pkv[z, x, SECOND].astype(F32)
        landed(zrsem.at[0], (NZ - 1) * REST)
        for m in range(NZ - 1):
            total = total + zr[m].astype(F32)
        ysum[SECOND] = total.astype(BF16)

    back = (
        {m: [(v_out, m - 2)] + ([(v_in, m - 6)] if m >= 6 else []) for m in range(2, NZ)},
        {m: [(k_hop, m - 2)] for m in range(2, NZ - 1)},
    )

    def drain_scatter():
        @pl.when(c == 1)
        def _():
            landed(sent.at[7], 28 * SPLIT)
            landed(sent.at[10], (NX - 1) * SPLIT)
            landed(sent.at[6], NZ * NX * REST)
            landed(sent.at[11], NT * SPLIT)

        @pl.when(c == 0)
        def _():
            landed(sent.at[8], NZ * (NX - 1) * REST)
            landed(sent.at[9], (NZ - 1) * REST)
            landed(sent.at[6], NZ * NX * SPLIT)
            landed(sent.at[11], NT * REST)

    def scatter_step(m, _):
        gradient_row(m)
        run_plan(m, back)
        return 0

    lax.fori_loop(0, NZ, scatter_step, 0)

    @pl.when(c == 0)
    def _():
        v_out(6)
        v_out(7)
        for m in range(2, 5):
            v_in(m)

    @pl.when(c == 1)
    def _():
        k_hop(5)
        k_hop(6)

    for j, acc in enumerate((dq2[0:HD], dq2[HD:2 * HD] + dql[...])):
        g = (acc * INV_ROOT).T.astype(BF16)
        for i in range(2):
            for h in range(HEADS):
                at_row = i * ROWS + h * HALF
                dqst[i, j * HALF:(j + 1) * HALF, h * HD:(h + 1) * HD] = g[at_row:at_row + HALF]

    def dq_copy(i):
        if i == 0:
            return remote(dqst.at[0], dqr.at[0], sent.at[12], dqsr.at[0], other(t, c))
        part = pl.ds((i - 1) * HALF, HALF)
        return remote(dqst.at[1, part], dqr.at[1, part], sent.at[12], dqsr.at[0],
                      other(mates[i - 1], c))

    for i in range(3):
        dq_copy(i).start()

    @pl.when(c == 1)
    def _():
        k_last()

    @pl.when(c == 0)
    def _():
        for m in range(5, NZ):
            v_in(m)
        v_last()

    def last(tt, part):
        return remote(ysum.at[part], yr.at[t // 2, part], sent.at[11], yrsem.at[0],
                      other(tt, half))

    for core, part in ((0, SECOND), (1, FIRST)):
        @pl.when(c == core)
        def _():
            for tt in range(NT):
                last(tt, part).start()

    drain_gather()
    drain_scatter()

    landed(dqsr.at[0], 8 * 128)
    landed(yrsem.at[0], 2 * BLOCK)
    landed(sent.at[12], 8 * 128)


def last_sums(dqr, yr, dq_out, dk_out, dv_out):
    dq_out[0] = (dqr[0].astype(F32) + dqr[1].astype(F32)).astype(BF16)
    for kind, out in ((0, dk_out), (1, dv_out)):
        part = slice(kind * 128, (kind + 1) * 128)
        out[0] = (yr[0, part].astype(F32) + yr[1, part].astype(F32)).astype(BF16)


def per_device(queries, keys, values, grad_out, span_order):
    vmem = pl.BlockSpec(memory_space=pltpu.VMEM)
    hbm = pl.BlockSpec(memory_space=pl.ANY)
    dma = pltpu.SemaphoreType.DMA

    def plane():
        return pltpu.VMEM((NZ, NX, BLOCK, HD), BF16)

    scratch = [
        pltpu.VMEM(queries.shape, BF16),
        pltpu.VMEM(keys.shape, BF16),
        pltpu.VMEM(values.shape, BF16),
        pltpu.VMEM(grad_out.shape, BF16),
        plane(),
        pltpu.VMEM((NZ, KEYS, SLOTS), F32),
        pltpu.VMEM((NZ, KEYS, SLOTS), F32),
        pltpu.VMEM((NZ, KEYS, SLOTS), F32),
        pltpu.VMEM((NZ, KEYS, SLOTS), F32),
        pltpu.VMEM((NZ, KEYS, 2 * HD), BF16),
        pltpu.VMEM((SLOTS, 2 * HD), BF16),
        pltpu.VMEM((SLOTS, 2 * HD), BF16),
        pltpu.VMEM((2, HALF, HEADS * HD), BF16),
        pltpu.VMEM((2, HALF, HEADS * HD), BF16),
        pltpu.VMEM((HD, SLOTS), F32),
        pltpu.VMEM((2 * HD, SLOTS), F32),
        pltpu.VMEM((2, 128, HEADS * HD), BF16),
        pltpu.VMEM((8, SLOTS), F32),
        pltpu.VMEM((NZ + 1, 8, SLOTS), F32),
        pltpu.VMEM((4, HALF, SLOTS), F32),
        pltpu.VMEM((2, 8, SLOTS), F32),
        pltpu.VMEM((2, 8, SLOTS), F32),
        plane(),
        plane(),
        pltpu.VMEM((2, 4, NX, SPLIT, HD), BF16),
        pltpu.VMEM((NX * NZ * REST, HD), BF16),
        pltpu.VMEM((NZ, REST, HD), BF16),
        pltpu.VMEM((NX, SPLIT, HD), BF16),
        pltpu.VMEM((BLOCK, HD), BF16),
        dma((2,)), dma((13,)),
        dma((NX,)), dma((NZ,)), dma((13,)), dma((NZ,)), dma((NZ,)),
        dma((1,)), dma((1,)),
        dma((NZ,)), dma((12,)), dma((NZ,)), dma((1,)), dma((1,)),
        dma((1,)), dma((1,)),
    ]
    arrived = pl.pallas_call(
        kernel,
        out_shape=(
            jax.ShapeDtypeStruct((2, 128, HEADS * HD), BF16),
            jax.ShapeDtypeStruct((2, BLOCK, HD), BF16),
        ),
        in_specs=[hbm, hbm, hbm, hbm, pl.BlockSpec(memory_space=pltpu.SMEM)],
        out_specs=(hbm, hbm),
        scratch_shapes=scratch,
        compiler_params=pltpu.CompilerParams(
            collective_id=1, has_side_effects=True, vmem_limit_bytes=56 * 2**20
        ),
        name="attention_backward",
    )(queries, keys, values, grad_out, jnp.swapaxes(span_order, 1, 2))
    return pl.pallas_call(
        last_sums,
        out_shape=tuple(jax.ShapeDtypeStruct(a.shape, BF16) for a in (queries, keys, values)),
        in_specs=[vmem, vmem],
        out_specs=(vmem, vmem, vmem),
        name="last_sums",
    )(*arrived)


def solution(mesh):
    return jax.shard_map(
        per_device,
        mesh=mesh,
        in_specs=(
            P("pipe", "ctx", "tp"),
            P("pipe", "ctx", None),
            P("pipe", "ctx", None),
            P("pipe", "ctx", "tp"),
            P("pipe", None, None),
        ),
        out_specs=(P("pipe", "ctx", "tp"), P("pipe", "ctx", None), P("pipe", "ctx", None)),
        check_vma=False,
    )
```
